32 devices in a mesh: dp: 4 (over y, x), expert: 2 (over core), shard: 4 (over z).
Axes of the slice: x: 2, y: 2, z: 4, core: 2. Of those that a mesh axis runs over, the one named last changes fastest.
Arguments:
- output_gradient: bfloat16 [4096, 3072], P(('dp', 'expert', 'shard')), may hold values from -6 to 6
- saved_router_scores: float32 [4096, 8], P(('dp', 'expert', 'shard')), may hold values from -8 to 8
- expert_choice_index: int32 [4096, 2], P(('dp', 'expert', 'shard')), may hold values from 0 to 7, as said below
- router_matrix: bfloat16 [8, 3072], replicated, may hold values from -0.109375 to 0.109375
- weight_normalized_entries: bfloat16 [3072, 8192], P('shard', 'expert'), may hold values from -1 to 1
- scales: bfloat16 [48, 8192], P('shard', 'expert'), may hold values from 0.0099487305 to 0.099609375
- stored_hidden_state: bfloat16 [4, 4, 64, 8192], P('dp', 'shard', None, 'expert'), may hold values from -6 to 6
- context: bfloat16 [4096, 3072], P(('dp', 'expert', 'shard')), may hold values from -6 to 6
- adapter_down_factor: bfloat16 [64, 3072], replicated, may hold values from -0.109375 to 0.109375
- adapter_up_factor: bfloat16 [64, 3072], replicated, may hold values from -0.109375 to 0.109375
Outputs:
- hidden_grad: bfloat16 [4, 4, 64, 8192], P('dp', 'shard', None, 'expert')
- token_grad: bfloat16 [4096, 3072], P(('dp', 'expert', 'shard'))
- grad_down: float32 [64, 3072], P(None, 'shard')
- up_factor_gradient: float32 [64, 3072], P(None, 'shard')
The draws below stay inside these ranges and needn't reach their ends.
Inputs may be any that keep to these rules, and one draw needn't show every extreme that they name: `expert_choice_index`: each token names two different experts and expert 0 at most once. The 128 tokens of one device block name expert 0 at most 32 times, and in every draw all device blocks of some pair of dp and shard indices name it exactly 32 times.
All inputs are finite; a program needn't handle non-finite values.
Results may differ from the reference program's by a relative error of at most 0.015.
Values may be sent and summed in bfloat16 or wider, within the bound.
No kernel may reach another device: no remote copies, remote signals or barrier semaphores. Data moves between devices by JAX's collectives and lax.ppermute only.
A program may use at most 128 MiB of HBM per device.

```python
import math
import jax
import jax.numpy as jnp
from jax import lax

WINDOW_FEATURES = 3072
FF_WIN = 8192
ADAPTER_RANK = 64
BLOCK = 64
EXPERTS = 8
TOK_DEV = 128
CAP = 32
ROWS = 64
TOKENS = 4096
N_DP = 4
N_EXPERT = 2
N_SHARD = 4


def draw_expert_choice_index(key, part):
    blocks = TOKENS // TOK_DEV
    subkeys = jax.random.split(jax.random.fold_in(key, 11), 6)
    counts = jax.random.randint(subkeys[0], (blocks,), CAP // 2, CAP + 1)
    full_group = jax.random.randint(subkeys[1], (), 0, N_DP * N_SHARD)
    block_index = jnp.arange(blocks, dtype=jnp.int32)
    group_index = block_index // (N_EXPERT * N_SHARD) * N_SHARD + block_index % N_SHARD
    counts = jnp.where(group_index == full_group, CAP, counts)
    scores = jax.random.randint(subkeys[2], (blocks, TOK_DEV), 0, 65536) * TOK_DEV + jnp.arange(TOK_DEV, dtype=jnp.int32)[None, :]
    ranking = jnp.argsort(jnp.argsort(scores, axis=1), axis=1)
    in_window = (ranking < counts[:, None]).reshape(TOKENS)
    first_other = jax.random.randint(subkeys[3], (TOKENS,), 1, EXPERTS)
    step_other = jax.random.randint(subkeys[4], (TOKENS,), 1, EXPERTS - 1)
    second_other = 1 + (first_other - 1 + step_other) % (EXPERTS - 1)
    swap_side = jax.random.randint(subkeys[5], (TOKENS,), 0, 2) == 1
    zero_ids = jnp.zeros((TOKENS,), jnp.int32)
    column_first = jnp.where(in_window, jnp.where(swap_side, first_other, zero_ids), first_other)
    column_second = jnp.where(in_window, jnp.where(swap_side, zero_ids, first_other), second_other)
    return jnp.stack([column_first, column_second], axis=1).astype(jnp.int32)


def raised(drawn, stream_key, source, target, shards_of, factor):
    def block_of(position):
        return (jnp.arange(drawn.shape[position]) // (drawn.shape[position] // shards_of)).reshape((-1,) + (1,) * (drawn.ndim - 1 - position))

    near = jax.random.permutation(stream_key, shards_of)[block_of(target)]
    other_side = (block_of(target) + shards_of // 2) % shards_of
    return jnp.where((block_of(source) == near) | (block_of(source) == other_side), factor * drawn, drawn)


def block_levels(own_key, extent, cuts, low, top_value):
    level = 1.0
    for position, parts in cuts:
        steps = jax.random.uniform(jax.random.fold_in(jax.random.fold_in(own_key, 6), position), (parts,), jnp.float32, low / len(cuts), top_value / len(cuts))
        level = level * jnp.repeat(jnp.exp(steps), extent[position] // parts).reshape((-1,) + (1,) * (len(extent) - 1 - position))
    return level


def scatter_about(own_key, dims, width, limit, cuts=(), kind=jnp.bfloat16):
    values = width * jax.random.normal(own_key, dims, jnp.float32)
    if cuts:
        values = values * block_levels(own_key, dims, cuts, -0.22, 0.18)
    return jnp.clip(values, -limit, limit).astype(kind)


def noise_with(own_key, dims, deviation, reach, cuts, heavy, held_as=jnp.bfloat16):
    values = deviation * jax.random.normal(own_key, dims, jnp.float32)
    if cuts:
        values = values * block_levels(own_key, dims, cuts, -0.22, 0.18)
    return jnp.clip(raised(values, jax.random.fold_in(own_key, 3), *heavy), -reach, reach).astype(held_as)


def setup_inputs(seed: int = 0) -> dict:
    seeds = jax.random.split(jax.random.key(seed), 11)
    output_gradient = noise_with(seeds[0], (TOKENS, WINDOW_FEATURES), 1.0, 6.0, ((0, 32),), (0, 1, 32, 2.75))
    saved_router_scores = scatter_about(seeds[1], (TOKENS, EXPERTS), 2.0, 8.0, ((0, 32),), jnp.float32)
    expert_choice_index = draw_expert_choice_index(jax.random.fold_in(seeds[10], 71), 0)
    router_matrix = scatter_about(seeds[3], (EXPERTS, WINDOW_FEATURES), WINDOW_FEATURES ** -0.5, 0.109375)
    weight_normalized_entries = jnp.clip(jax.random.uniform(seeds[4], (WINDOW_FEATURES, FF_WIN), jnp.float32, -1.0, 1.0) * block_levels(seeds[4], (WINDOW_FEATURES, FF_WIN), ((0, 4), (1, 2)), -0.4, 0.0), -1.0, 1.0).astype(jnp.bfloat16)
    scales = jnp.clip(jnp.exp(math.log(0.099609375) - 2.3038113 * jax.random.uniform(seeds[5], (WINDOW_FEATURES // BLOCK, FF_WIN), jnp.float32) ** block_levels(seeds[5], (WINDOW_FEATURES // BLOCK, FF_WIN), ((0, 4), (1, 2)), -0.2, 0.2)), 0.0099487305, 0.099609375).astype(jnp.bfloat16)
    stored_hidden_state = scatter_about(seeds[6], (N_DP, N_SHARD, ROWS, FF_WIN), 1.0, 6.0, ((0, 4), (1, 4), (3, 2)))
    context = scatter_about(seeds[7], (TOKENS, WINDOW_FEATURES), 1.0, 6.0, ((0, 32),))
    adapter_down_factor = scatter_about(seeds[8], (ADAPTER_RANK, WINDOW_FEATURES), WINDOW_FEATURES ** -0.5, 0.109375)
    adapter_up_factor = scatter_about(seeds[9], (ADAPTER_RANK, WINDOW_FEATURES), WINDOW_FEATURES ** -0.5, 0.109375)
    return dict(output_gradient=output_gradient, saved_router_scores=saved_router_scores, expert_choice_index=expert_choice_index, router_matrix=router_matrix, weight_normalized_entries=weight_normalized_entries, scales=scales, stored_hidden_state=stored_hidden_state, context=context, adapter_down_factor=adapter_down_factor, adapter_up_factor=adapter_up_factor)


ADAPTER_SCALE = 0.25


def reference(output_gradient, saved_router_scores, expert_choice_index, router_matrix, weight_normalized_entries, scales, stored_hidden_state, context, adapter_down_factor, adapter_up_factor):
    labels = jnp.arange(EXPERTS, dtype=jnp.int32)
    choose = expert_choice_index[:, :, None] == labels[None, None, :]
    chosen = jnp.sum(jnp.where(choose, saved_router_scores[:, None, :], 0.0), axis=2)
    first_prob = 1.0 / (1.0 + jnp.exp(chosen[:, 1] - chosen[:, 0]))
    second_prob = 1.0 - first_prob
    in_window = expert_choice_index == 0
    window_flag = jnp.any(in_window, axis=1)
    blocks = TOKENS // TOK_DEV
    flag_int = window_flag.astype(jnp.int32).reshape(blocks, TOK_DEV)
    slot_index = (jnp.cumsum(flag_int, axis=1) - flag_int).reshape(TOKENS).astype(jnp.int32)
    block_of = (jnp.arange(TOKENS, dtype=jnp.int32) // TOK_DEV).astype(jnp.int32)
    route_probs = jnp.stack([first_prob, second_prob], axis=1).astype(jnp.bfloat16)
    window_prob = jnp.where(in_window[:, 0], route_probs[:, 0], route_probs[:, 1])
    target = jnp.where(window_flag, slot_index, CAP).astype(jnp.int32)
    buffer_rows = jnp.zeros((blocks, CAP, WINDOW_FEATURES), jnp.bfloat16).at[block_of, target].set(output_gradient, mode="drop")
    buffer_probs = jnp.zeros((blocks, CAP), jnp.bfloat16).at[block_of, target].set(window_prob, mode="drop")
    buffer_rows = buffer_rows.reshape(N_DP, N_EXPERT, N_SHARD, CAP, WINDOW_FEATURES).transpose(0, 2, 1, 3, 4).reshape(N_DP * N_SHARD, ROWS, WINDOW_FEATURES)
    buffer_probs = buffer_probs.reshape(N_DP, N_EXPERT, N_SHARD, CAP).transpose(0, 2, 1, 3).reshape(N_DP * N_SHARD, ROWS)
    weight = (weight_normalized_entries.astype(jnp.float32).reshape(WINDOW_FEATURES // BLOCK, BLOCK, FF_WIN) * scales.astype(jnp.float32)[:, None, :]).astype(jnp.bfloat16).reshape(WINDOW_FEATURES, FF_WIN)
    hidden_rows = stored_hidden_state.reshape(N_DP * N_SHARD, ROWS, FF_WIN)

    def one_group(group_item):
        rows_in, probs_in, hidden_in = group_item
        product = jnp.dot(rows_in, weight, preferred_element_type=jnp.float32)
        scaled_grads = (probs_in.astype(jnp.float32)[:, None] * product).astype(jnp.bfloat16)
        partial_value = jnp.sum(hidden_in.astype(jnp.float32) * product, axis=1)
        return scaled_grads, partial_value

    scaled_grads, prob_grad = lax.map(one_group, (buffer_rows, buffer_probs, hidden_rows))
    hidden_grad = scaled_grads.reshape(N_DP, N_SHARD, ROWS, FF_WIN)
    prob_grad = prob_grad.reshape(N_DP, N_SHARD, N_EXPERT, CAP)
    dp_index = block_of // (N_EXPERT * N_SHARD)
    source_expert = (block_of // N_SHARD) % N_EXPERT
    shard_index = block_of % N_SHARD
    window_grad = prob_grad[dp_index, shard_index, source_expert, jnp.minimum(slot_index, CAP - 1)]
    window_grad = jnp.where(window_flag, window_grad, 0.0)
    pair_grad = jnp.where(in_window, window_grad[:, None], 0.0)
    spread = first_prob * second_prob * (pair_grad[:, 0] - pair_grad[:, 1])
    sign_table = choose[:, 0, :].astype(jnp.float32) - choose[:, 1, :].astype(jnp.float32)
    logit_grad = (spread[:, None] * sign_table).astype(jnp.bfloat16)
    token_grad = jnp.dot(logit_grad, router_matrix, preferred_element_type=jnp.float32).astype(jnp.bfloat16)
    token_kept = lax.optimization_barrier(token_grad)
    residual_gradient = (output_gradient.astype(jnp.float32) + token_kept.astype(jnp.float32)).astype(jnp.bfloat16)
    narrow_input = lax.dot_general(context, adapter_down_factor, (((1,), (1,)), ((), ())), preferred_element_type=jnp.float32).astype(jnp.bfloat16)
    narrow_gradient = (ADAPTER_SCALE * lax.dot_general(residual_gradient, adapter_up_factor, (((1,), (1,)), ((), ())), preferred_element_type=jnp.float32)).astype(jnp.bfloat16)
    up_factor_gradient = ADAPTER_SCALE * lax.dot_general(narrow_input, residual_gradient, (((0,), (0,)), ((), ())), preferred_element_type=jnp.float32)
    grad_down = lax.dot_general(narrow_gradient, context, (((0,), (0,)), ((), ())), preferred_element_type=jnp.float32)
    return (hidden_grad, token_grad, grad_down, up_factor_gradient)
```

```python
import jax
import jax.numpy as jnp
from jax import lax
from jax.sharding import PartitionSpec as P

ADAPTER_SCALE = 0.25


def xor_pairs(count, bits):
    return [(i, i ^ bits) for i in range(count)]


def route(saved_router_scores, expert_choice_index, capacity):
    experts = saved_router_scores.shape[1]
    labels = jnp.arange(experts, dtype=jnp.int32)
    choose = expert_choice_index[:, :, None] == labels[None, None, :]
    chosen = jnp.sum(jnp.where(choose, saved_router_scores[:, None, :], 0.0), axis=2)
    first_prob = 1.0 / (1.0 + jnp.exp(chosen[:, 1] - chosen[:, 0]))
    second_prob = 1.0 - first_prob
    in_window = expert_choice_index == 0
    window_flag = jnp.any(in_window, axis=1)
    flag_int = window_flag.astype(jnp.int32)
    slot_index = jnp.cumsum(flag_int) - flag_int
    route_probs = jnp.stack([first_prob, second_prob], axis=1).astype(jnp.bfloat16)
    window_prob = jnp.where(in_window[:, 0], route_probs[:, 0], route_probs[:, 1])
    slot_labels = jnp.arange(capacity, dtype=jnp.int32)
    placement = window_flag[None, :] & (slot_index[None, :] == slot_labels[:, None])
    window_sign = in_window[:, 0].astype(jnp.float32) - in_window[:, 1].astype(jnp.float32)
    sign_table = choose[:, 0, :].astype(jnp.float32) - choose[:, 1, :].astype(jnp.float32)
    factors = (first_prob * second_prob * window_sign)[:, None] * sign_table
    return placement, window_prob, factors


def exchange_rows(send_rows, shard, shard_count):
    capacity, width = send_rows.shape
    blocks = send_rows.reshape(capacity, shard_count, width // shard_count).transpose(1, 0, 2)
    got = []
    for k in range(shard_count):
        block = lax.dynamic_index_in_dim(blocks, shard ^ k, 0, keepdims=False)
        if k:
            block = lax.ppermute(block, "shard", xor_pairs(shard_count, k))
        got.append(block)
    return jnp.stack(got)


def combine_products(parts, is_end):
    swap = xor_pairs(4, 1)
    first = jnp.where(is_end, parts[3], parts[1])
    last = jnp.where(is_end, parts[1], parts[3])
    near = lax.ppermute(first, "shard", swap)
    middle = lax.ppermute(last, "shard", [(1, 2), (2, 1)])
    near_wide = near.astype(jnp.float32)
    forward = parts[2].astype(jnp.float32) + jnp.where(is_end, 0.0, near_wide)
    far = lax.ppermute(forward.astype(jnp.bfloat16), "shard", xor_pairs(4, 2))
    outer = lax.ppermute(last, "shard", [(0, 1), (3, 2)])
    return (
        jnp.where(is_end, near_wide, 0.0)
        + middle.astype(jnp.float32)
        + far.astype(jnp.float32)
        + outer.astype(jnp.float32)
    )


def halve(value, axis, index, bit, count):
    half = value.shape[0] // 2
    side = (index >> bit) & 1
    keep = lax.dynamic_slice_in_dim(value, side * half, half, 0)
    send = lax.dynamic_slice_in_dim(value, (1 - side) * half, half, 0)
    got = lax.ppermute(send.astype(jnp.bfloat16), axis, xor_pairs(count, 1 << bit))
    return keep + got.astype(jnp.float32)


def widen(value, axis, index, bit, count):
    side = (index >> bit) & 1
    got = lax.ppermute(value, axis, xor_pairs(count, 1 << bit))
    return jnp.where(
        side == 0, jnp.concatenate([value, got], 0), jnp.concatenate([got, value], 0)
    )


def per_device(
    output_gradient,
    saved_router_scores,
    expert_choice_index,
    router_matrix,
    weight_normalized_entries,
    scales,
    stored_hidden_state,
    context,
    adapter_down_factor,
    adapter_up_factor,
):
    dp_count = lax.axis_size("dp")
    expert_count = lax.axis_size("expert")
    shard_count = lax.axis_size("shard")
    dp = lax.axis_index("dp")
    expert = lax.axis_index("expert")
    shard = lax.axis_index("shard")
    direct = (dp_count, expert_count, shard_count) == (4, 2, 4)
    tokens, feature_width = output_gradient.shape
    row_count = stored_hidden_state.shape[2]
    capacity = row_count // expert_count
    ff_share = stored_hidden_state.shape[3]
    share_width = feature_width // shard_count
    block_size = weight_normalized_entries.shape[0] // scales.shape[0]
    rank = adapter_up_factor.shape[0]

    placement, window_prob, factors = route(saved_router_scores, expert_choice_index, capacity)
    placed = placement.astype(jnp.bfloat16)
    send_rows = jnp.dot(placed, output_gradient, preferred_element_type=jnp.float32).astype(
        jnp.bfloat16
    )
    send_probs = jnp.dot(placed, window_prob, preferred_element_type=jnp.float32).astype(
        jnp.bfloat16
    )
    if direct:
        blocks = exchange_rows(send_rows, shard, shard_count)
    else:
        blocks = lax.all_to_all(
            send_rows.reshape(capacity, shard_count, share_width).transpose(1, 0, 2), "shard", 0, 0
        )
    gathered = lax.all_gather(blocks, "expert", axis=1)
    all_probs = lax.all_gather(send_probs, "expert", axis=0, tiled=True)

    code_blocks = weight_normalized_entries.reshape(scales.shape[0], block_size, ff_share)
    own_weight = (code_blocks * scales[:, None, :]).reshape(
        weight_normalized_entries.shape[0], ff_share
    )
    product = jnp.dot(
        gathered.reshape(shard_count * row_count, share_width),
        own_weight,
        preferred_element_type=jnp.float32,
    ).reshape(shard_count, row_count, ff_share)

    narrow_input = lax.dot_general(
        context, adapter_down_factor, (((1,), (1,)), ((), ())), preferred_element_type=jnp.float32
    ).astype(jnp.bfloat16)
    narrow_gradient = (
        ADAPTER_SCALE
        * lax.dot_general(
            output_gradient,
            adapter_up_factor,
            (((1,), (1,)), ((), ())),
            preferred_element_type=jnp.float32,
        )
    ).astype(jnp.bfloat16)
    early_up = ADAPTER_SCALE * lax.dot_general(
        narrow_input, output_gradient, (((0,), (0,)), ((), ())), preferred_element_type=jnp.float32
    )
    early_down = lax.dot_general(
        narrow_gradient, context, (((0,), (0,)), ((), ())), preferred_element_type=jnp.float32
    )
    early = jnp.concatenate([early_up, early_down], 0)

    if direct:
        is_end = (shard == 0) | (shard == 3)
        parts = [product[k].astype(jnp.bfloat16) for k in range(1, 4)]
        total = product[0] + combine_products([None] + parts, is_end)
        early = halve(early, "expert", expert, 0, 2)
        early = halve(early, "dp", dp, 0, 4)
        early = halve(early, "dp", dp, 1, 4)
        early_blocks = early.astype(jnp.bfloat16)
        early = jnp.sum(exchange_rows(early_blocks, shard, shard_count).astype(jnp.float32), 0)
        early = widen(early, "dp", dp, 1, 4)
        early = widen(early, "dp", dp, 0, 4)
        early = widen(early, "expert", expert, 0, 2)
    else:
        total = lax.psum_scatter(product.astype(jnp.bfloat16), "shard", scatter_dimension=0)
        total = total.astype(jnp.float32)
        early = lax.psum(early, ("dp", "expert"))
        early = lax.psum_scatter(early, "shard", scatter_dimension=1, tiled=True)

    hidden_grad = (all_probs.astype(jnp.float32)[:, None] * total).astype(jnp.bfloat16)
    partial_value = jnp.sum(stored_hidden_state[0, 0].astype(jnp.float32) * total, axis=1)
    slot_grad = lax.psum(partial_value, "expert")
    own_grad = lax.dynamic_slice_in_dim(slot_grad, expert * capacity, capacity, 0)
    window_grad = jnp.sum(jnp.where(placement, own_grad[:, None], 0.0), axis=0)
    logit_grad = (factors * window_grad[:, None]).astype(jnp.bfloat16)
    token_grad = jnp.dot(logit_grad, router_matrix, preferred_element_type=jnp.float32).astype(
        jnp.bfloat16
    )
    late_input = lax.dot_general(
        logit_grad, narrow_input, (((0,), (0,)), ((), ())), preferred_element_type=jnp.float32
    )
    late_context = lax.dot_general(
        logit_grad, context, (((0,), (0,)), ((), ())), preferred_element_type=jnp.float32
    )
    if direct:
        for bit in (1, 0):
            half = late_context.shape[1] // 2
            side = (shard >> bit) & 1
            keep = lax.dynamic_slice_in_dim(late_context, side * half, half, 1)
            send = lax.dynamic_slice_in_dim(late_context, (1 - side) * half, half, 1)
            got = lax.ppermute(
                jnp.concatenate([send, late_input], 1), "shard", xor_pairs(4, 1 << bit)
            )
            late_context = keep + got[:, :half]
            late_input = late_input + got[:, half:]
        late = jnp.concatenate([late_context, late_input], 1)
        for bit in (0, 1):
            late = late + lax.ppermute(late, "dp", xor_pairs(4, 1 << bit))
        late = late + lax.ppermute(late, "expert", [(0, 1), (1, 0)])
        late_context, late_input = late[:, :share_width], late[:, share_width:]
    else:
        late_input = lax.psum(late_input, ("dp", "expert", "shard"))
        late_context = lax.psum(late_context, ("dp", "expert"))
        late_context = lax.psum_scatter(late_context, "shard", scatter_dimension=1, tiled=True)
    own_router = lax.dynamic_slice_in_dim(router_matrix, shard * share_width, share_width, 1)
    factor_router = ADAPTER_SCALE * lax.dot_general(
        adapter_up_factor, router_matrix, (((1,), (1,)), ((), ())), preferred_element_type=jnp.float32
    )
    up_factor_gradient = early[:rank] + ADAPTER_SCALE * lax.dot_general(
        late_input,
        own_router.astype(jnp.float32),
        (((0,), (0,)), ((), ())),
        precision=lax.Precision.HIGHEST,
        preferred_element_type=jnp.float32,
    )
    grad_down = early[rank:] + jnp.dot(
        factor_router,
        late_context,
        precision=lax.Precision.HIGHEST,
        preferred_element_type=jnp.float32,
    )
    return (
        hidden_grad.reshape(stored_hidden_state.shape),
        token_grad,
        grad_down,
        up_factor_gradient,
    )


def solution(mesh):
    tokens_spec = P(("dp", "expert", "shard"), None)
    in_specs = (
        tokens_spec,
        tokens_spec,
        tokens_spec,
        P(),
        P("shard", "expert"),
        P("shard", "expert"),
        P("dp", "shard", None, "expert"),
        tokens_spec,
        P(),
        P(),
    )
    out_specs = (
        P("dp", "shard", None, "expert"),
        tokens_spec,
        P(None, "shard"),
        P(None, "shard"),
    )
    return jax.shard_map(
        per_device, mesh=mesh, in_specs=in_specs, out_specs=out_specs, check_vma=False
    )
```

```python
import functools

import jax
import jax.numpy as jnp
from jax import lax
from jax.experimental import pallas as pl
from jax.experimental.pallas import tpu as pltpu
from jax.sharding import PartitionSpec as P

ADAPTER_SCALE = 0.25
LANES = 128
F32 = jnp.float32
BF16 = jnp.bfloat16
SMEM = pl.BlockSpec(memory_space=pltpu.SMEM)
VMEM = pl.BlockSpec(memory_space=pltpu.VMEM)
HBM = pl.BlockSpec(memory_space=pltpu.HBM)
EXACT = lax.Precision.HIGHEST


def params(mebibytes=16):
    return pltpu.CompilerParams(vmem_limit_bytes=mebibytes * 1024 * 1024)


def cost(flops, bytes_accessed):
    return pl.CostEstimate(flops=flops, bytes_accessed=bytes_accessed, transcendentals=0)


def in_hbm(value):
    return pltpu.with_memory_space_constraint(value, pltpu.HBM)


def whole(shape):
    return pl.BlockSpec(shape, lambda *_: (0,) * len(shape))


def contract(a, b, dim_a, dim_b, precision=None):
    return lax.dot_general(
        a, b, (((dim_a,), (dim_b,)), ((), ())), precision=precision, preferred_element_type=F32
    )


def xor_pairs(count, bits):
    return [(i, i ^ bits) for i in range(count)]


def feature_block(ref, place, k, width):
    start = pl.multiple_of((place[0] ^ k) * width, LANES)
    return ref[:, pl.ds(start, width)]


def route_kernel(
    place, scores_hbm, choice_hbm, grad_hbm, rows_ref, slots_ref, info_ref,
    scores_ref, choice_ref, grad_ref, sems,
):
    load_scores = pltpu.make_async_copy(scores_hbm, scores_ref, sems.at[0])
    load_choice = pltpu.make_async_copy(choice_hbm, choice_ref, sems.at[1])
    load = pltpu.make_async_copy(grad_hbm, grad_ref, sems.at[2])
    load_scores.start()
    load_choice.start()
    load.start()
    load_scores.wait()
    load_choice.wait()
    scores = scores_ref[...]
    experts, tokens = scores.shape
    shards, capacity, width = rows_ref.shape
    first_choice = choice_ref[0:1, :]
    second_choice = choice_ref[1:2, :]
    labels = lax.broadcasted_iota(jnp.int32, (experts, tokens), 0)
    chosen_first = jnp.sum(jnp.where(labels == first_choice, scores, 0.0), axis=0, keepdims=True)
    chosen_second = jnp.sum(jnp.where(labels == second_choice, scores, 0.0), axis=0, keepdims=True)
    first_prob = 1.0 / (1.0 + jnp.exp(chosen_second - chosen_first))
    second_prob = 1.0 - first_prob
    in_first = (first_choice == 0).astype(F32)
    in_second = (second_choice == 0).astype(F32)
    flags = jnp.broadcast_to(in_first + in_second, (capacity, tokens))
    row = lax.broadcasted_iota(jnp.int32, (tokens, tokens), 0)
    column = lax.broadcasted_iota(jnp.int32, (tokens, tokens), 1)
    before = (row < column).astype(F32).astype(BF16)
    slot = jnp.dot(flags.astype(BF16), before, preferred_element_type=F32)
    number = lax.broadcasted_iota(jnp.int32, (capacity, tokens), 0).astype(F32)
    slots = jnp.where((flags > 0.5) & (slot == number), 1.0, 0.0)
    slots_ref[...] = slots
    sign = (labels == first_choice).astype(F32) - (labels == second_choice).astype(F32)
    info_ref[:experts] = first_prob * second_prob * (in_first - in_second) * sign
    window_prob = jnp.where(in_first > 0.5, first_prob, second_prob)
    info_ref[experts:] = jnp.broadcast_to(window_prob, (info_ref.shape[0] - experts, tokens))
    picks = slots.astype(BF16)
    load.wait()
    for k in range(shards):
        block = feature_block(grad_ref, place, k, width)
        rows_ref[k] = jnp.dot(picks, block, preferred_element_type=F32).astype(BF16)


def route(place, scores, choice, grad, capacity, shards):
    tokens, features = grad.shape
    return pl.pallas_call(
        route_kernel,
        out_shape=(
            jax.ShapeDtypeStruct((shards, capacity, features // shards), BF16),
            jax.ShapeDtypeStruct((capacity, tokens), F32),
            jax.ShapeDtypeStruct((2 * scores.shape[1], tokens), F32),
        ),
        in_specs=[SMEM, HBM, HBM, HBM],
        out_specs=(VMEM,) * 3,
        scratch_shapes=[
            pltpu.VMEM(scores.T.shape, F32),
            pltpu.VMEM(choice.T.shape, jnp.int32),
            pltpu.VMEM(grad.shape, BF16),
            pltpu.SemaphoreType.DMA((3,)),
        ],
        compiler_params=params(),
        cost_estimate=cost(2 * tokens * capacity * features, 2 * tokens * features),
        name="route",
    )(place, in_hbm(scores.T), in_hbm(choice.T), in_hbm(grad))


def product_kernel(half, place, rows_ref, weight_ref, *refs):
    outs, lhs = refs[-5:-1], refs[-1]
    shards, capacity, _ = rows_ref.shape
    is_end = place[3]
    order = (1 + 2 * is_end, 2, 3 - 2 * is_end, 0)
    for slot, k in enumerate(order):
        lhs[slot * capacity : (slot + 1) * capacity] = rows_ref[k]
    rows = slice(half * capacity, (half + 1) * capacity)
    tile = 512
    for t in range(weight_ref.shape[1] // tile):
        part = slice(t * tile, (t + 1) * tile)
        result = jnp.dot(lhs[...], weight_ref[:, part], preferred_element_type=F32)
        for slot, ref in enumerate(outs):
            ref[rows, part] = result[slot * capacity : (slot + 1) * capacity].astype(ref.dtype)


def products(place, rows, weight, before=()):
    shards, capacity, width = rows.shape
    hidden = weight.shape[1]
    sent = pltpu.VMEM((2 * capacity, hidden), BF16)
    return pl.pallas_call(
        functools.partial(product_kernel, len(before) // 4),
        out_shape=(sent, sent, sent, pltpu.VMEM((2 * capacity, hidden), F32)),
        in_specs=[SMEM, VMEM, VMEM] + [VMEM] * len(before),
        out_specs=(VMEM,) * 4,
        input_output_aliases={3 + i: i for i in range(len(before))},
        scratch_shapes=[pltpu.VMEM((shards * capacity, width), BF16)],
        compiler_params=params(),
        cost_estimate=cost(2 * shards * capacity * width * hidden, 2 * width * hidden),
        name="products",
    )(place, rows, pltpu.with_memory_space_constraint(weight, pltpu.VMEM), *before)


def forward_kernel(place, far_ref, near_ref, out_ref):
    keep = 1.0 - place[3].astype(F32)
    out_ref[...] = (far_ref[...].astype(F32) + keep * near_ref[...].astype(F32)).astype(BF16)


def add_near(place, far, near):
    return pl.pallas_call(
        forward_kernel,
        out_shape=pltpu.VMEM(far.shape, BF16),
        in_specs=[SMEM, VMEM, VMEM],
        out_specs=VMEM,
        compiler_params=params(),
        cost_estimate=cost(2 * far.size, 6 * far.size),
        name="add_near",
    )(place, far, near)


def weight_kernel(codes_hbm, scales_hbm, weight_ref, codes_ref, scales_ref, scale_sem, sems):
    load_scales = pltpu.make_async_copy(scales_hbm, scales_ref, scale_sem)
    load_scales.start()
    tiles = sems.shape[0]
    tile = codes_ref.shape[1] // tiles
    loads = []
    for t in range(tiles):
        part = pl.ds(t * tile, tile)
        loads.append(
            pltpu.make_async_copy(codes_hbm.at[:, part], codes_ref.at[:, part], sems.at[t])
        )
        loads[t].start()
    blocks = scales_ref.shape[0]
    size = codes_ref.shape[0] // blocks
    load_scales.wait()
    for t in range(tiles):
        loads[t].wait()
        part = slice(t * tile, (t + 1) * tile)
        for b in range(blocks):
            rows = slice(b * size, (b + 1) * size)
            weight_ref[rows, part] = codes_ref[rows, part] * scales_ref[b : b + 1, part]


def dequantize(codes, scales, tiles):
    return pl.pallas_call(
        weight_kernel,
        out_shape=pltpu.VMEM(codes.shape, BF16),
        in_specs=[HBM, HBM],
        out_specs=VMEM,
        scratch_shapes=[
            pltpu.VMEM(codes.shape, BF16),
            pltpu.VMEM(scales.shape, BF16),
            pltpu.SemaphoreType.DMA,
            pltpu.SemaphoreType.DMA((tiles,)),
        ],
        compiler_params=params(),
        cost_estimate=cost(codes.size, 4 * codes.size),
        name="dequantize",
    )(in_hbm(codes), in_hbm(scales))


def adapter_kernel(
    place, grad_hbm, context_hbm, down_hbm, up_hbm, router_hbm, slots_ref, info_ref,
    early_ref, picked_ref, mixed_ref,
    grad_ref, context_ref, down_ref, up_ref, router_ref, sems,
):
    pairs = (
        (context_hbm, context_ref),
        (down_hbm, down_ref),
        (grad_hbm, grad_ref),
        (up_hbm, up_ref),
        (router_hbm, router_ref),
    )
    loads = [
        pltpu.make_async_copy(source, target, sems.at[i])
        for i, (source, target) in enumerate(pairs)
    ]
    for load in loads:
        load.start()
    groups, shards, rows, width = early_ref.shape
    capacity = picked_ref.shape[0]
    features = shards * width
    half = groups // 2
    loads[0].wait()
    loads[1].wait()
    low_in = contract(context_ref[...], down_ref[...], 1, 1).astype(BF16)
    for load in loads[2:]:
        load.wait()
    low_grad = (ADAPTER_SCALE * contract(grad_ref[...], up_ref[...], 1, 1)).astype(BF16)
    mixed_ref[...] = ADAPTER_SCALE * contract(up_ref[...], router_ref[...], 1, 1)
    slots = slots_ref[...].astype(BF16)
    for k in range(shards):
        grad = feature_block(grad_ref, place, k, width)
        context = feature_block(context_ref, place, k, width)
        up = ADAPTER_SCALE * contract(low_in, grad, 0, 0)
        down = contract(low_grad, context, 0, 0)
        for g in range(half):
            early_ref[g ^ place[1], k] = up[g * rows : (g + 1) * rows]
            early_ref[(g + half) ^ place[1], k] = down[g * rows : (g + 1) * rows]
        picked_ref[:, k * width : (k + 1) * width] = jnp.dot(
            slots, context, preferred_element_type=F32
        ).astype(BF16)
    low = jnp.dot(slots, low_in, preferred_element_type=F32).astype(BF16)
    picked_ref[:, features:] = jnp.zeros((capacity, 2 * LANES), BF16)
    picked_ref[:, features : features + low.shape[1]] = low
    info = contract(slots_ref[...], info_ref[...], 1, 1, EXACT)
    picked_ref[:, features + LANES : features + LANES + info.shape[1]] = info.astype(BF16)


def adapter_early(place, grad, context, down, up, router, slots, info, groups, shards):
    tokens, features = grad.shape
    rank = up.shape[0]
    rows = 2 * rank // groups
    arrays = (grad, context, down, up, router)
    return pl.pallas_call(
        adapter_kernel,
        out_shape=(
            jax.ShapeDtypeStruct((groups, shards, rows, features // shards), F32),
            jax.ShapeDtypeStruct((slots.shape[0], features + 2 * LANES), BF16),
            jax.ShapeDtypeStruct((rank, router.shape[0]), F32),
        ),
        in_specs=[SMEM] + [HBM] * 5 + [VMEM] * 2,
        out_specs=(VMEM,) * 3,
        scratch_shapes=[pltpu.VMEM(value.shape, BF16) for value in arrays]
        + [pltpu.SemaphoreType.DMA((5,))],
        compiler_params=params(),
        cost_estimate=cost(0, 0),
        name="adapter_early",
    )(place, *[in_hbm(value) for value in arrays], slots, info)


def finish_kernel(
    experts, place, own_ref, near_ref, middle_ref, far_ref, outer_ref, hidden_ref, picked_ref, other_ref,
    grad_hbm, prob_ref, prob_other_ref, late_ref, grad_ref, sems,
):
    shards, _, late_width = late_ref.shape
    width = late_width - LANES
    features = shards * width
    is_end = place[3].astype(F32)
    tiles = sems.shape[0]
    hidden = far_ref.shape[1]
    tile = hidden // tiles

    def store(t):
        part = pl.ds(t * tile, tile)
        return pltpu.make_async_copy(grad_ref.at[:, part], grad_hbm.at[:, part], sems.at[t])

    capacity = picked_ref.shape[0]
    pickeds = (picked_ref, other_ref)
    infos = [ref[:, features + LANES :].astype(F32) for ref in pickeds]
    totals = [jnp.zeros((capacity, LANES), F32) for _ in pickeds]
    for t in range(tiles):
        part = slice(t * tile, (t + 1) * tile)
        for half, info in enumerate(infos):
            rows = slice(half * capacity, (half + 1) * capacity)
            whole_rows = pl.ds(pl.multiple_of((place[2] ^ half) * capacity, capacity), capacity)
            product = (
                own_ref[rows, part]
                + is_end * near_ref[rows, part].astype(F32)
                + far_ref[rows, part].astype(F32)
                + (1.0 - is_end)
                * (middle_ref[rows, part].astype(F32) + outer_ref[rows, part].astype(F32))
            )
            grad_ref[whole_rows, part] = (info[:, experts : experts + 1] * product).astype(BF16)
            weighted = hidden_ref[whole_rows, part].astype(F32) * product
            for j in range(tile // LANES):
                totals[half] = totals[half] + weighted[:, j * LANES : (j + 1) * LANES]
        store(t).start()
    diagonal = lax.broadcasted_iota(jnp.int32, (capacity, capacity), 0) == lax.broadcasted_iota(
        jnp.int32, (capacity, capacity), 1
    )
    lane = lax.broadcasted_iota(jnp.int32, (capacity, LANES), 1)
    logits = []
    for info, total, out in zip(infos, totals, (prob_ref, prob_other_ref), strict=True):
        prob = jnp.sum(total, axis=1, keepdims=True)
        flat = jnp.sum(jnp.where(diagonal, prob, 0.0), axis=0, keepdims=True)
        out[...] = jnp.broadcast_to(flat, out.shape)
        logits.append(jnp.where(lane < experts, info * prob, 0.0).astype(BF16))

    def late(columns):
        return sum(
            contract(logit, ref[:, columns], 0, 0)[:experts]
            for logit, ref in zip(logits, pickeds, strict=True)
        )

    low = late(slice(features, features + LANES))
    for k in range(shards):
        late_ref[k, :, :width] = late(slice(k * width, (k + 1) * width))
        late_ref[k, :, width:] = low
    for t in range(tiles):
        store(t).wait()


def finish(place, own, near, middle, far, outer, hidden_state, picked, other, experts, shards, tiles):
    rows, hidden = far.shape
    capacity = picked.shape[0]
    width = (picked.shape[1] - 2 * LANES) // shards
    return pl.pallas_call(
        functools.partial(finish_kernel, experts),
        out_shape=(
            jax.ShapeDtypeStruct((rows, hidden), BF16),
            jax.ShapeDtypeStruct((8, capacity), F32),
            jax.ShapeDtypeStruct((8, capacity), F32),
            jax.ShapeDtypeStruct((shards, experts, width + LANES), F32),
        ),
        in_specs=[SMEM] + [VMEM] * 8,
        out_specs=(HBM, VMEM, VMEM, VMEM),
        scratch_shapes=[pltpu.VMEM((rows, hidden), BF16), pltpu.SemaphoreType.DMA((tiles,))],
        compiler_params=params(),
        cost_estimate=cost(8 * rows * hidden, 10 * rows * hidden),
        name="finish",
    )(place, own, near, middle, far, outer, hidden_state, picked, other)


def token_kernel(prob_ref, prob_got_ref, slots_ref, info_ref, router_ref, token_hbm, token_ref, sems):
    experts = router_ref.shape[0]
    own = prob_ref[...] + prob_got_ref[...]
    window = jnp.dot(own, slots_ref[...], precision=EXACT, preferred_element_type=F32)[0:1]
    logits = (info_ref[:experts] * window).astype(BF16)
    tiles = sems.shape[0]
    tile = token_ref.shape[1] // tiles
    stores = []
    for t in range(tiles):
        part = pl.ds(t * tile, tile)
        token_ref[:, part] = contract(logits, router_ref[:, part], 0, 0).astype(BF16)
        store = pltpu.make_async_copy(token_ref.at[:, part], token_hbm.at[:, part], sems.at[t])
        store.start()
        stores.append(store)
    for store in stores:
        store.wait()


def token_gradient(prob, prob_got, slots, info, router, tiles):
    tokens = slots.shape[1]
    features = router.shape[1]
    return pl.pallas_call(
        token_kernel,
        out_shape=jax.ShapeDtypeStruct((tokens, features), BF16),
        in_specs=[VMEM] * 5,
        out_specs=HBM,
        scratch_shapes=[pltpu.VMEM((tokens, features), BF16), pltpu.SemaphoreType.DMA((tiles,))],
        compiler_params=params(),
        cost_estimate=cost(2 * tokens * features * router.shape[0], 2 * tokens * features),
        name="token_gradient",
    )(prob, prob_got, slots, info, router)


def adapter_late_kernel(place, early_ref, late_ref, mixed_ref, router_ref, down_ref, up_ref):
    groups, rows, _ = early_ref.shape
    half = groups // 2
    rank, width = up_ref.shape
    router = feature_block(router_ref, place, 0, width).astype(F32)
    up = ADAPTER_SCALE * contract(late_ref[:, width : width + rank], router, 0, 0, EXACT)
    down = jnp.dot(
        mixed_ref[...], late_ref[:, :width], precision=EXACT, preferred_element_type=F32
    )
    for g in range(half):
        part = slice(g * rows, (g + 1) * rows)
        up_ref[part] = early_ref[g ^ place[1], :, :width].astype(F32) + up[part]
        down_ref[part] = early_ref[(g + half) ^ place[1], :, :width].astype(F32) + down[part]


def adapter_late(place, early, late, mixed, router):
    groups, rows, width = early.shape
    out = jax.ShapeDtypeStruct((groups * rows // 2, width - LANES), F32)
    return pl.pallas_call(
        adapter_late_kernel,
        out_shape=(out, out),
        in_specs=[SMEM] + [VMEM] * 4,
        out_specs=(whole(out.shape),) * 2,
        compiler_params=params(),
        cost_estimate=cost(64 * groups * rows * width, 8 * groups * rows * width),
        name="adapter_late",
    )(place, early, late, mixed, router)


def swap(value, axis, count, bits):
    return lax.ppermute(value, axis, xor_pairs(count, bits))


def after(value, *others):
    return lax.optimization_barrier((value,) + others)[0]


def direct_device(
    output_gradient,
    saved_router_scores,
    expert_choice_index,
    router_matrix,
    weight_normalized_entries,
    scales,
    stored_hidden_state,
    context,
    adapter_down_factor,
    adapter_up_factor,
):
    dp = lax.axis_index("dp")
    expert = lax.axis_index("expert")
    shard = lax.axis_index("shard")
    is_end = ((shard == 0) | (shard == 3)).astype(jnp.int32)
    group = expert * 4 + dp
    place = jnp.stack([shard, group, expert, is_end]).astype(jnp.int32)
    row_count, ff_share = stored_hidden_state.shape[2:]
    capacity = row_count // 2
    experts = saved_router_scores.shape[1]

    send_rows, slots, info = route(
        place, saved_router_scores, expert_choice_index, output_gradient, capacity, 4
    )
    rows = jnp.stack(
        [send_rows[0]] + [swap(send_rows[k], "shard", 4, k) for k in range(1, 4)]
    )
    weight = dequantize(weight_normalized_entries, scales, 4)
    rows, weight = lax.optimization_barrier((rows, weight))
    other_rows = swap(rows, "expert", 2, 1)

    partial = products(place, rows, weight)
    first, far, last, own = products(place, other_rows, weight, partial)
    near = swap(first, "shard", 4, 1)
    middle = lax.ppermute(last, "shard", [(1, 2), (2, 1)])
    early, picked, mixed = adapter_early(
        after(place, last), output_gradient, context, adapter_down_factor, adapter_up_factor,
        router_matrix, slots, info, 8, 4,
    )
    far, near, early, picked = lax.optimization_barrier((far, near, early, picked))
    forward = add_near(place, far, near)
    across = swap(forward, "shard", 4, 2)
    forward, last, middle = lax.optimization_barrier((forward, last, middle))
    outer = swap(last, "shard", 4, 1)
    forward, early, picked = lax.optimization_barrier((forward, early, picked))
    other_picked = swap(picked, "expert", 2, 1)
    early = early[:4] + swap(early[4:].astype(BF16), "expert", 2, 1).astype(F32)
    parts = early.astype(BF16)
    early = early[0] + sum(swap(parts[k], "dp", 4, k).astype(F32) for k in range(1, 4))
    across, early, other_picked = lax.optimization_barrier((across, early, other_picked))
    across, outer = lax.optimization_barrier((across, outer))

    hidden_grad, prob, prob_other, late = finish(
        place, own, near, middle, across, outer, stored_hidden_state[0, 0], picked, other_picked,
        experts, 4, 4,
    )
    early = jnp.pad(early, ((0, 0), (0, 0), (0, LANES)))
    late = jnp.concatenate([late, early], 1)
    late = late[:2] + swap(late[2:].astype(BF16), "shard", 4, 2).astype(F32)
    prob_got = swap(prob_other, "expert", 2, 1)
    late = late[0] + swap(late[1].astype(BF16), "shard", 4, 1).astype(F32)
    late, early = late[:experts], late[experts:].astype(BF16)
    mine = jnp.concatenate([late.astype(BF16), early], 0)
    got = [swap(mine, "dp", 4, k) for k in range(1, 4)]
    token_grad = token_gradient(prob, prob_got, slots, info, router_matrix, 4)
    late = late + sum(other[:experts].astype(F32) for other in got)
    early = jnp.concatenate([early] + [other[experts:] for other in got], 0)
    got = swap(jnp.concatenate([late.astype(BF16), early], 0), "expert", 2, 1)
    late = late + got[:experts].astype(F32)
    early = jnp.concatenate([early, got[experts:]], 0)
    early = early.reshape(8, -1, early.shape[1])
    grad_down, up_factor_gradient = adapter_late(place, early, late, mixed, router_matrix)
    return (
        hidden_grad.reshape(stored_hidden_state.shape),
        token_grad,
        grad_down,
        up_factor_gradient,
    )


def route_general(saved_router_scores, expert_choice_index, capacity):
    experts = saved_router_scores.shape[1]
    labels = jnp.arange(experts, dtype=jnp.int32)
    choose = expert_choice_index[:, :, None] == labels[None, None, :]
    chosen = jnp.sum(jnp.where(choose, saved_router_scores[:, None, :], 0.0), axis=2)
    first_prob = 1.0 / (1.0 + jnp.exp(chosen[:, 1] - chosen[:, 0]))
    second_prob = 1.0 - first_prob
    in_window = expert_choice_index == 0
    window_flag = jnp.any(in_window, axis=1)
    flag_int = window_flag.astype(jnp.int32)
    slot_index = jnp.cumsum(flag_int) - flag_int
    route_probs = jnp.stack([first_prob, second_prob], axis=1).astype(jnp.bfloat16)
    window_prob = jnp.where(in_window[:, 0], route_probs[:, 0], route_probs[:, 1])
    slot_labels = jnp.arange(capacity, dtype=jnp.int32)
    placement = window_flag[None, :] & (slot_index[None, :] == slot_labels[:, None])
    window_sign = in_window[:, 0].astype(jnp.float32) - in_window[:, 1].astype(jnp.float32)
    sign_table = choose[:, 0, :].astype(jnp.float32) - choose[:, 1, :].astype(jnp.float32)
    factors = (first_prob * second_prob * window_sign)[:, None] * sign_table
    return placement, window_prob, factors


def general_device(
    output_gradient,
    saved_router_scores,
    expert_choice_index,
    router_matrix,
    weight_normalized_entries,
    scales,
    stored_hidden_state,
    context,
    adapter_down_factor,
    adapter_up_factor,
):
    expert_count = lax.axis_size("expert")
    shard_count = lax.axis_size("shard")
    expert = lax.axis_index("expert")
    shard = lax.axis_index("shard")
    tokens, feature_width = output_gradient.shape
    row_count = stored_hidden_state.shape[2]
    capacity = row_count // expert_count
    ff_share = stored_hidden_state.shape[3]
    share_width = feature_width // shard_count
    block_size = weight_normalized_entries.shape[0] // scales.shape[0]
    rank = adapter_up_factor.shape[0]

    placement, window_prob, factors = route_general(saved_router_scores, expert_choice_index, capacity)
    placed = placement.astype(jnp.bfloat16)
    send_rows = jnp.dot(placed, output_gradient, preferred_element_type=jnp.float32).astype(
        jnp.bfloat16
    )
    send_probs = jnp.dot(placed, window_prob, preferred_element_type=jnp.float32).astype(
        jnp.bfloat16
    )
    blocks = lax.all_to_all(
        send_rows.reshape(capacity, shard_count, share_width).transpose(1, 0, 2), "shard", 0, 0
    )
    gathered = lax.all_gather(blocks, "expert", axis=1)
    all_probs = lax.all_gather(send_probs, "expert", axis=0, tiled=True)

    code_blocks = weight_normalized_entries.reshape(scales.shape[0], block_size, ff_share)
    own_weight = (code_blocks * scales[:, None, :]).reshape(
        weight_normalized_entries.shape[0], ff_share
    )
    product = jnp.dot(
        gathered.reshape(shard_count * row_count, share_width),
        own_weight,
        preferred_element_type=jnp.float32,
    ).reshape(shard_count, row_count, ff_share)

    narrow_input = lax.dot_general(
        context, adapter_down_factor, (((1,), (1,)), ((), ())), preferred_element_type=jnp.float32
    ).astype(jnp.bfloat16)
    narrow_gradient = (
        ADAPTER_SCALE
        * lax.dot_general(
            output_gradient,
            adapter_up_factor,
            (((1,), (1,)), ((), ())),
            preferred_element_type=jnp.float32,
        )
    ).astype(jnp.bfloat16)
    early_up = ADAPTER_SCALE * lax.dot_general(
        narrow_input, output_gradient, (((0,), (0,)), ((), ())), preferred_element_type=jnp.float32
    )
    early_down = lax.dot_general(
        narrow_gradient, context, (((0,), (0,)), ((), ())), preferred_element_type=jnp.float32
    )
    early = jnp.concatenate([early_up, early_down], 0)

    total = lax.psum_scatter(product.astype(jnp.bfloat16), "shard", scatter_dimension=0)
    total = total.astype(jnp.float32)
    early = lax.psum(early, ("dp", "expert"))
    early = lax.psum_scatter(early, "shard", scatter_dimension=1, tiled=True)

    hidden_grad = (all_probs.astype(jnp.float32)[:, None] * total).astype(jnp.bfloat16)
    partial_value = jnp.sum(stored_hidden_state[0, 0].astype(jnp.float32) * total, axis=1)
    slot_grad = lax.psum(partial_value, "expert")
    own_grad = lax.dynamic_slice_in_dim(slot_grad, expert * capacity, capacity, 0)
    window_grad = jnp.sum(jnp.where(placement, own_grad[:, None], 0.0), axis=0)
    logit_grad = (factors * window_grad[:, None]).astype(jnp.bfloat16)
    token_grad = jnp.dot(logit_grad, router_matrix, preferred_element_type=jnp.float32).astype(
        jnp.bfloat16
    )
    late_input = lax.dot_general(
        logit_grad, narrow_input, (((0,), (0,)), ((), ())), preferred_element_type=jnp.float32
    )
    late_context = lax.dot_general(
        logit_grad, context, (((0,), (0,)), ((), ())), preferred_element_type=jnp.float32
    )
    late_input = lax.psum(late_input, ("dp", "expert", "shard"))
    late_context = lax.psum(late_context, ("dp", "expert"))
    late_context = lax.psum_scatter(late_context, "shard", scatter_dimension=1, tiled=True)
    own_router = lax.dynamic_slice_in_dim(router_matrix, shard * share_width, share_width, 1)
    factor_router = ADAPTER_SCALE * lax.dot_general(
        adapter_up_factor, router_matrix, (((1,), (1,)), ((), ())), preferred_element_type=jnp.float32
    )
    up_factor_gradient = early[:rank] + ADAPTER_SCALE * lax.dot_general(
        late_input,
        own_router.astype(jnp.float32),
        (((0,), (0,)), ((), ())),
        precision=lax.Precision.HIGHEST,
        preferred_element_type=jnp.float32,
    )
    grad_down = early[rank:] + jnp.dot(
        factor_router,
        late_context,
        precision=lax.Precision.HIGHEST,
        preferred_element_type=jnp.float32,
    )
    return (
        hidden_grad.reshape(stored_hidden_state.shape),
        token_grad,
        grad_down,
        up_factor_gradient,
    )


def solution(mesh):
    axes = dict(mesh.shape)
    direct = (axes["dp"], axes["expert"], axes["shard"]) == (4, 2, 4)
    tokens_spec = P(("dp", "expert", "shard"), None)
    in_specs = (
        tokens_spec,
        tokens_spec,
        tokens_spec,
        P(),
        P("shard", "expert"),
        P("shard", "expert"),
        P("dp", "shard", None, "expert"),
        tokens_spec,
        P(),
        P(),
    )
    out_specs = (
        P("dp", "shard", None, "expert"),
        tokens_spec,
        P(None, "shard"),
        P(None, "shard"),
    )
    return jax.shard_map(
        direct_device if direct else general_device, mesh=mesh, in_specs=in_specs, out_specs=out_specs, check_vma=False
    )
```

```python
import functools

import jax
import jax.numpy as jnp
from jax import lax
from jax.experimental import pallas as pl
from jax.experimental.pallas import tpu as pltpu
from jax.sharding import PartitionSpec as P

ADAPTER_SCALE = 0.25
LANES = 128
F32 = jnp.float32
BF16 = jnp.bfloat16
SMEM = pl.BlockSpec(memory_space=pltpu.SMEM)
VMEM = pl.BlockSpec(memory_space=pltpu.VMEM)
HBM = pl.BlockSpec(memory_space=pltpu.HBM)
EXACT = lax.Precision.HIGHEST


def params(mebibytes=16):
    return pltpu.CompilerParams(vmem_limit_bytes=mebibytes * 1024 * 1024)


def cost(flops, bytes_accessed):
    return pl.CostEstimate(flops=flops, bytes_accessed=bytes_accessed, transcendentals=0)


def in_hbm(value):
    return pltpu.with_memory_space_constraint(value, pltpu.HBM)


def whole(shape):
    return pl.BlockSpec(shape, lambda *_: (0,) * len(shape))


def contract(a, b, dim_a, dim_b, precision=None):
    return lax.dot_general(
        a, b, (((dim_a,), (dim_b,)), ((), ())), precision=precision, preferred_element_type=F32
    )


def xor_pairs(count, bits):
    return [(i, i ^ bits) for i in range(count)]


def feature_block(ref, place, k, width):
    start = pl.multiple_of((place[0] ^ k) * width, LANES)
    return ref[:, pl.ds(start, width)]


def route_kernel(
    place, scores_hbm, choice_hbm, grad_hbm, rows_ref, slots_ref, info_ref,
    scores_ref, choice_ref, grad_ref, sems,
):
    load_scores = pltpu.make_async_copy(scores_hbm, scores_ref, sems.at[0])
    load_choice = pltpu.make_async_copy(choice_hbm, choice_ref, sems.at[1])
    load = pltpu.make_async_copy(grad_hbm, grad_ref, sems.at[2])
    load_scores.start()
    load_choice.start()
    load.start()
    load_scores.wait()
    load_choice.wait()
    scores = scores_ref[...]
    experts, tokens = scores.shape
    shards, capacity, width = rows_ref.shape
    first_choice = choice_ref[0:1, :]
    second_choice = choice_ref[1:2, :]
    labels = lax.broadcasted_iota(jnp.int32, (experts, tokens), 0)
    chosen_first = jnp.sum(jnp.where(labels == first_choice, scores, 0.0), axis=0, keepdims=True)
    chosen_second = jnp.sum(jnp.where(labels == second_choice, scores, 0.0), axis=0, keepdims=True)
    first_prob = 1.0 / (1.0 + jnp.exp(chosen_second - chosen_first))
    second_prob = 1.0 - first_prob
    in_first = (first_choice == 0).astype(F32)
    in_second = (second_choice == 0).astype(F32)
    flags = jnp.broadcast_to(in_first + in_second, (capacity, tokens))
    row = lax.broadcasted_iota(jnp.int32, (tokens, tokens), 0)
    column = lax.broadcasted_iota(jnp.int32, (tokens, tokens), 1)
    before = (row < column).astype(F32).astype(BF16)
    slot = jnp.dot(flags.astype(BF16), before, preferred_element_type=F32)
    number = lax.broadcasted_iota(jnp.int32, (capacity, tokens), 0).astype(F32)
    slots = jnp.where((flags > 0.5) & (slot == number), 1.0, 0.0)
    slots_ref[...] = slots
    sign = (labels == first_choice).astype(F32) - (labels == second_choice).astype(F32)
    info_ref[:experts] = first_prob * second_prob * (in_first - in_second) * sign
    window_prob = jnp.where(in_first > 0.5, first_prob, second_prob)
    info_ref[experts:] = jnp.broadcast_to(window_prob, (info_ref.shape[0] - experts, tokens))
    picks = slots.astype(BF16)
    load.wait()
    for k in range(shards):
        block = feature_block(grad_ref, place, k, width)
        rows_ref[k] = jnp.dot(picks, block, preferred_element_type=F32).astype(BF16)


def route(place, scores, choice, grad, capacity, shards):
    tokens, features = grad.shape
    return pl.pallas_call(
        route_kernel,
        out_shape=(
            jax.ShapeDtypeStruct((shards, capacity, features // shards), BF16),
            jax.ShapeDtypeStruct((capacity, tokens), F32),
            jax.ShapeDtypeStruct((2 * scores.shape[1], tokens), F32),
        ),
        in_specs=[SMEM, HBM, HBM, HBM],
        out_specs=(VMEM,) * 3,
        scratch_shapes=[
            pltpu.VMEM(scores.T.shape, F32),
            pltpu.VMEM(choice.T.shape, jnp.int32),
            pltpu.VMEM(grad.shape, BF16),
            pltpu.SemaphoreType.DMA((3,)),
        ],
        compiler_params=params(),
        cost_estimate=cost(2 * tokens * capacity * features, 2 * tokens * features),
        name="route",
    )(place, in_hbm(scores.T), in_hbm(choice.T), in_hbm(grad))


def product_kernel(half, place, rows_ref, weight_ref, *refs):
    outs, lhs = refs[-5:-1], refs[-1]
    shards, capacity, _ = rows_ref.shape
    is_end = place[3]
    order = (1 + 2 * is_end, 2, 3 - 2 * is_end, 0)
    for slot, k in enumerate(order):
        lhs[slot * capacity : (slot + 1) * capacity] = rows_ref[k]
    rows = slice(half * capacity, (half + 1) * capacity)
    tile = 512
    for t in range(weight_ref.shape[1] // tile):
        part = slice(t * tile, (t + 1) * tile)
        result = jnp.dot(lhs[...], weight_ref[:, part], preferred_element_type=F32)
        for slot, ref in enumerate(outs):
            ref[rows, part] = result[slot * capacity : (slot + 1) * capacity].astype(ref.dtype)


def products(place, rows, weight, before=()):
    shards, capacity, width = rows.shape
    hidden = weight.shape[1]
    sent = pltpu.VMEM((2 * capacity, hidden), BF16)
    return pl.pallas_call(
        functools.partial(product_kernel, len(before) // 4),
        out_shape=(sent, sent, sent, pltpu.VMEM((2 * capacity, hidden), F32)),
        in_specs=[SMEM, VMEM, VMEM] + [VMEM] * len(before),
        out_specs=(VMEM,) * 4,
        input_output_aliases={3 + i: i for i in range(len(before))},
        scratch_shapes=[pltpu.VMEM((shards * capacity, width), BF16)],
        compiler_params=params(),
        cost_estimate=cost(2 * shards * capacity * width * hidden, 2 * width * hidden),
        name="products",
    )(place, rows, pltpu.with_memory_space_constraint(weight, pltpu.VMEM), *before)


def forward_kernel(place, far_ref, near_ref, out_ref):
    keep = 1.0 - place[3].astype(F32)
    out_ref[...] = (far_ref[...].astype(F32) + keep * near_ref[...].astype(F32)).astype(BF16)


def add_near(place, far, near):
    return pl.pallas_call(
        forward_kernel,
        out_shape=pltpu.VMEM(far.shape, BF16),
        in_specs=[SMEM, VMEM, VMEM],
        out_specs=VMEM,
        compiler_params=params(),
        cost_estimate=cost(2 * far.size, 6 * far.size),
        name="add_near",
    )(place, far, near)


def partial_kernel(place, own_ref, near_ref, middle_ref, out_ref):
    is_end = place[3].astype(F32)
    out_ref[...] = (
        own_ref[...]
        + is_end * near_ref[...].astype(F32)
        + (1.0 - is_end) * middle_ref[...].astype(F32)
    )


def add_first(place, own, near, middle):
    return pl.pallas_call(
        partial_kernel,
        out_shape=pltpu.VMEM(own.shape, F32),
        in_specs=[SMEM] + [VMEM] * 3,
        out_specs=VMEM,
        compiler_params=params(),
        cost_estimate=cost(0, 0),
        name="add_first",
    )(place, own, near, middle)


def weight_kernel(codes_hbm, scales_hbm, weight_ref, codes_ref, scales_ref, scale_sem, sems):
    load_scales = pltpu.make_async_copy(scales_hbm, scales_ref, scale_sem)
    load_scales.start()
    tiles = sems.shape[0]
    tile = codes_ref.shape[1] // tiles
    loads = []
    for t in range(tiles):
        part = pl.ds(t * tile, tile)
        loads.append(
            pltpu.make_async_copy(codes_hbm.at[:, part], codes_ref.at[:, part], sems.at[t])
        )
        loads[t].start()
    blocks = scales_ref.shape[0]
    size = codes_ref.shape[0] // blocks
    load_scales.wait()
    for t in range(tiles):
        loads[t].wait()
        part = slice(t * tile, (t + 1) * tile)
        for b in range(blocks):
            rows = slice(b * size, (b + 1) * size)
            weight_ref[rows, part] = codes_ref[rows, part] * scales_ref[b : b + 1, part]


def dequantize(codes, scales, tiles):
    return pl.pallas_call(
        weight_kernel,
        out_shape=pltpu.VMEM(codes.shape, BF16),
        in_specs=[HBM, HBM],
        out_specs=VMEM,
        scratch_shapes=[
            pltpu.VMEM(codes.shape, BF16),
            pltpu.VMEM(scales.shape, BF16),
            pltpu.SemaphoreType.DMA,
            pltpu.SemaphoreType.DMA((tiles,)),
        ],
        compiler_params=params(),
        cost_estimate=cost(codes.size, 4 * codes.size),
        name="dequantize",
    )(in_hbm(codes), in_hbm(scales))


def adapter_kernel(
    place, grad_hbm, context_hbm, down_hbm, up_hbm, router_hbm, slots_ref, info_ref,
    early_ref, picked_ref, mixed_ref,
    grad_ref, context_ref, down_ref, up_ref, router_ref, sems,
):
    pairs = (
        (context_hbm, context_ref),
        (down_hbm, down_ref),
        (grad_hbm, grad_ref),
        (up_hbm, up_ref),
        (router_hbm, router_ref),
    )
    loads = [
        pltpu.make_async_copy(source, target, sems.at[i])
        for i, (source, target) in enumerate(pairs)
    ]
    for load in loads:
        load.start()
    groups, shards, rows, width = early_ref.shape
    capacity = picked_ref.shape[0]
    features = shards * width
    half = groups // 2
    loads[0].wait()
    loads[1].wait()
    low_in = contract(context_ref[...], down_ref[...], 1, 1).astype(BF16)
    for load in loads[2:]:
        load.wait()
    low_grad = (ADAPTER_SCALE * contract(grad_ref[...], up_ref[...], 1, 1)).astype(BF16)
    mixed_ref[...] = ADAPTER_SCALE * contract(up_ref[...], router_ref[...], 1, 1)
    slots = slots_ref[...].astype(BF16)
    for k in range(shards):
        grad = feature_block(grad_ref, place, k, width)
        context = feature_block(context_ref, place, k, width)
        up = ADAPTER_SCALE * contract(low_in, grad, 0, 0)
        down = contract(low_grad, context, 0, 0)
        for g in range(half):
            early_ref[g ^ place[1], k] = up[g * rows : (g + 1) * rows]
            early_ref[(g + half) ^ place[1], k] = down[g * rows : (g + 1) * rows]
        picked_ref[:, k * width : (k + 1) * width] = jnp.dot(
            slots, context, preferred_element_type=F32
        ).astype(BF16)
    low = jnp.dot(slots, low_in, preferred_element_type=F32).astype(BF16)
    picked_ref[:, features:] = jnp.zeros((capacity, 2 * LANES), BF16)
    picked_ref[:, features : features + low.shape[1]] = low
    info = contract(slots_ref[...], info_ref[...], 1, 1, EXACT)
    picked_ref[:, features + LANES : features + LANES + info.shape[1]] = info.astype(BF16)


def adapter_early(place, grad, context, down, up, router, slots, info, groups, shards):
    tokens, features = grad.shape
    rank = up.shape[0]
    rows = 2 * rank // groups
    arrays = (grad, context, down, up, router)
    return pl.pallas_call(
        adapter_kernel,
        out_shape=(
            jax.ShapeDtypeStruct((groups, shards, rows, features // shards), F32),
            jax.ShapeDtypeStruct((slots.shape[0], features + 2 * LANES), BF16),
            jax.ShapeDtypeStruct((rank, router.shape[0]), F32),
        ),
        in_specs=[SMEM] + [HBM] * 5 + [VMEM] * 2,
        out_specs=(VMEM,) * 3,
        scratch_shapes=[pltpu.VMEM(value.shape, BF16) for value in arrays]
        + [pltpu.SemaphoreType.DMA((5,))],
        compiler_params=params(),
        cost_estimate=cost(0, 0),
        name="adapter_early",
    )(place, *[in_hbm(value) for value in arrays], slots, info)


def finish_kernel(
    experts, place, partial_ref, far_ref, outer_ref, hidden_ref, picked_ref, other_ref,
    product_ref, prob_ref, prob_other_ref, late_ref,
):
    shards, _, late_width = late_ref.shape
    width = late_width - LANES
    features = shards * width
    is_end = place[3].astype(F32)
    hidden = far_ref.shape[1]
    tile = 512
    capacity = picked_ref.shape[0]
    pickeds = (picked_ref, other_ref)
    infos = [ref[:, features + LANES :].astype(F32) for ref in pickeds]
    totals = [jnp.zeros((capacity, LANES), F32) for _ in pickeds]
    for t in range(hidden // tile):
        part = slice(t * tile, (t + 1) * tile)
        for half in range(2):
            rows = slice(half * capacity, (half + 1) * capacity)
            whole_rows = pl.ds(pl.multiple_of((place[2] ^ half) * capacity, capacity), capacity)
            product = (
                partial_ref[rows, part]
                + far_ref[rows, part].astype(F32)
                + (1.0 - is_end) * outer_ref[rows, part].astype(F32)
            )
            product_ref[rows, part] = product
            weighted = hidden_ref[whole_rows, part].astype(F32) * product
            for j in range(tile // LANES):
                totals[half] = totals[half] + weighted[:, j * LANES : (j + 1) * LANES]
    diagonal = lax.broadcasted_iota(jnp.int32, (capacity, capacity), 0) == lax.broadcasted_iota(
        jnp.int32, (capacity, capacity), 1
    )
    lane = lax.broadcasted_iota(jnp.int32, (capacity, LANES), 1)
    logits = []
    for info, total, out in zip(infos, totals, (prob_ref, prob_other_ref), strict=True):
        prob = jnp.sum(total, axis=1, keepdims=True)
        flat = jnp.sum(jnp.where(diagonal, prob, 0.0), axis=0, keepdims=True)
        out[...] = jnp.broadcast_to(flat, out.shape)
        logits.append(jnp.where(lane < experts, info * prob, 0.0).astype(BF16))

    def late(columns):
        return sum(
            contract(logit, ref[:, columns], 0, 0)[:experts]
            for logit, ref in zip(logits, pickeds, strict=True)
        )

    low = late(slice(features, features + LANES))
    for k in range(shards):
        late_ref[k, :, :width] = late(slice(k * width, (k + 1) * width))
        late_ref[k, :, width:] = low


def hidden_kernel(experts, place, product_ref, picked_ref, other_ref, grad_hbm, grad_ref, sems):
    capacity = picked_ref.shape[0]
    column = picked_ref.shape[1] - LANES + experts
    tiles = sems.shape[0]
    tile = product_ref.shape[1] // tiles
    stores = []
    for t in range(tiles):
        part = pl.ds(t * tile, tile)
        for half, ref in enumerate((picked_ref, other_ref)):
            rows = slice(half * capacity, (half + 1) * capacity)
            whole_rows = pl.ds(pl.multiple_of((place[2] ^ half) * capacity, capacity), capacity)
            window_prob = ref[:, column - experts :].astype(F32)[:, experts : experts + 1]
            grad_ref[whole_rows, part] = (window_prob * product_ref[rows, part]).astype(BF16)
        store = pltpu.make_async_copy(grad_ref.at[:, part], grad_hbm.at[:, part], sems.at[t])
        store.start()
        stores.append(store)
    for store in stores:
        store.wait()


def hidden_gradient(place, product, picked, other, experts, tiles):
    return pl.pallas_call(
        functools.partial(hidden_kernel, experts),
        out_shape=jax.ShapeDtypeStruct(product.shape, BF16),
        in_specs=[SMEM] + [VMEM] * 3,
        out_specs=HBM,
        scratch_shapes=[pltpu.VMEM(product.shape, BF16), pltpu.SemaphoreType.DMA((tiles,))],
        compiler_params=params(),
        cost_estimate=cost(0, 0),
        name="hidden_gradient",
    )(place, product, picked, other)


def finish(place, partial, far, outer, hidden_state, picked, other, experts, shards):
    rows, hidden = far.shape
    capacity = picked.shape[0]
    width = (picked.shape[1] - 2 * LANES) // shards
    return pl.pallas_call(
        functools.partial(finish_kernel, experts),
        out_shape=(
            pltpu.VMEM((rows, hidden), F32),
            jax.ShapeDtypeStruct((8, capacity), F32),
            jax.ShapeDtypeStruct((8, capacity), F32),
            jax.ShapeDtypeStruct((shards, experts, width + LANES), F32),
        ),
        in_specs=[SMEM] + [VMEM] * 6,
        out_specs=(VMEM,) * 4,
        compiler_params=params(),
        cost_estimate=cost(8 * rows * hidden, 10 * rows * hidden),
        name="finish",
    )(place, partial, far, outer, hidden_state, picked, other)


def token_kernel(prob_ref, prob_got_ref, slots_ref, info_ref, router_ref, token_hbm, token_ref, sems):
    experts = router_ref.shape[0]
    own = prob_ref[...] + prob_got_ref[...]
    window = jnp.dot(own, slots_ref[...], precision=EXACT, preferred_element_type=F32)[0:1]
    logits = (info_ref[:experts] * window).astype(BF16)
    tiles = sems.shape[0]
    tile = token_ref.shape[1] // tiles
    stores = []
    for t in range(tiles):
        part = pl.ds(t * tile, tile)
        token_ref[:, part] = contract(logits, router_ref[:, part], 0, 0).astype(BF16)
        store = pltpu.make_async_copy(token_ref.at[:, part], token_hbm.at[:, part], sems.at[t])
        store.start()
        stores.append(store)
    for store in stores:
        store.wait()


def token_gradient(prob, prob_got, slots, info, router, tiles):
    tokens = slots.shape[1]
    features = router.shape[1]
    return pl.pallas_call(
        token_kernel,
        out_shape=jax.ShapeDtypeStruct((tokens, features), BF16),
        in_specs=[VMEM] * 5,
        out_specs=HBM,
        scratch_shapes=[pltpu.VMEM((tokens, features), BF16), pltpu.SemaphoreType.DMA((tiles,))],
        compiler_params=params(),
        cost_estimate=cost(2 * tokens * features * router.shape[0], 2 * tokens * features),
        name="token_gradient",
    )(prob, prob_got, slots, info, router)


def adapter_late_kernel(
    place, early_ref, late_ref, mixed_ref, router_ref, down_hbm, up_hbm, down_ref, up_ref, sems
):
    groups, rows, _ = early_ref.shape
    half = groups // 2
    rank, width = up_ref.shape
    parts = [slice(g * rows, (g + 1) * rows) for g in range(half)]
    down = jnp.dot(
        mixed_ref[...], late_ref[:, :width], precision=EXACT, preferred_element_type=F32
    )
    for g, part in enumerate(parts):
        down_ref[part] = early_ref[(g + half) ^ place[1], :, :width].astype(F32) + down[part]
    store_down = pltpu.make_async_copy(down_ref, down_hbm, sems.at[0])
    store_down.start()
    router = feature_block(router_ref, place, 0, width).astype(F32)
    up = ADAPTER_SCALE * contract(late_ref[:, width : width + rank], router, 0, 0, EXACT)
    for g, part in enumerate(parts):
        up_ref[part] = early_ref[g ^ place[1], :, :width].astype(F32) + up[part]
    store_up = pltpu.make_async_copy(up_ref, up_hbm, sems.at[1])
    store_up.start()
    store_down.wait()
    store_up.wait()


def adapter_late(place, early, late, mixed, router):
    groups, rows, width = early.shape
    out = jax.ShapeDtypeStruct((groups * rows // 2, width - LANES), F32)
    return pl.pallas_call(
        adapter_late_kernel,
        out_shape=(out, out),
        in_specs=[SMEM] + [VMEM] * 4,
        out_specs=(HBM, HBM),
        scratch_shapes=[pltpu.VMEM(out.shape, F32)] * 2 + [pltpu.SemaphoreType.DMA((2,))],
        compiler_params=params(),
        cost_estimate=cost(64 * groups * rows * width, 8 * groups * rows * width),
        name="adapter_late",
    )(place, early, late, mixed, router)


def swap(value, axis, count, bits):
    return lax.ppermute(value, axis, xor_pairs(count, bits))


def after(value, *others):
    return lax.optimization_barrier((value,) + others)[0]


def direct_device(
    output_gradient,
    saved_router_scores,
    expert_choice_index,
    router_matrix,
    weight_normalized_entries,
    scales,
    stored_hidden_state,
    context,
    adapter_down_factor,
    adapter_up_factor,
):
    dp = lax.axis_index("dp")
    expert = lax.axis_index("expert")
    shard = lax.axis_index("shard")
    is_end = ((shard == 0) | (shard == 3)).astype(jnp.int32)
    group = expert * 4 + dp
    place = jnp.stack([shard, group, expert, is_end]).astype(jnp.int32)
    row_count, ff_share = stored_hidden_state.shape[2:]
    capacity = row_count // 2
    experts = saved_router_scores.shape[1]

    send_rows, slots, info = route(
        place, saved_router_scores, expert_choice_index, output_gradient, capacity, 4
    )
    rows = jnp.stack(
        [send_rows[0]] + [swap(send_rows[k], "shard", 4, k) for k in range(1, 4)]
    )
    weight = dequantize(weight_normalized_entries, scales, 4)
    rows, weight = lax.optimization_barrier((rows, weight))
    other_rows = swap(rows, "expert", 2, 1)

    partial = products(place, rows, weight)
    first, far, last, own = products(place, other_rows, weight, partial)
    near = swap(first, "shard", 4, 1)
    middle = lax.ppermute(last, "shard", [(1, 2), (2, 1)])
    early, picked, mixed = adapter_early(
        after(place, last), output_gradient, context, adapter_down_factor, adapter_up_factor,
        router_matrix, slots, info, 8, 4,
    )
    far, near, early, picked = lax.optimization_barrier((far, near, early, picked))
    forward = add_near(place, far, near)
    across = swap(forward, "shard", 4, 2)
    forward, last, middle = lax.optimization_barrier((forward, last, middle))
    outer = lax.ppermute(last, "shard", [(0, 1), (3, 2)])
    forward, early, picked = lax.optimization_barrier((forward, early, picked))
    other_picked = swap(picked, "expert", 2, 1)
    early = early[:4] + swap(early[4:].astype(BF16), "expert", 2, 1).astype(F32)
    partial = add_first(place, own, near, middle)
    early, partial = lax.optimization_barrier((early, partial))
    parts = early.astype(BF16)
    early = early[0] + sum(swap(parts[k], "dp", 4, k).astype(F32) for k in range(1, 4))
    across, early, other_picked = lax.optimization_barrier((across, early, other_picked))
    across, outer = lax.optimization_barrier((across, outer))

    product, prob, prob_other, late = finish(
        place, partial, across, outer, stored_hidden_state[0, 0], picked, other_picked, experts, 4
    )
    early = jnp.pad(early, ((0, 0), (0, 0), (0, LANES)))
    late = jnp.concatenate([late, early], 1)
    late = late[:2] + swap(late[2:].astype(BF16), "shard", 4, 2).astype(F32)
    hidden_grad = hidden_gradient(place, product, picked, other_picked, experts, 4)
    late, hidden_grad = lax.optimization_barrier((late, hidden_grad))
    prob_got = swap(prob_other, "expert", 2, 1)
    late = late[0] + swap(late[1].astype(BF16), "shard", 4, 1).astype(F32)
    late, early = late[:experts], late[experts:].astype(BF16)
    mine = jnp.concatenate([late.astype(BF16), early], 0)
    got = [swap(mine, "dp", 4, k) for k in range(1, 4)]
    token_grad = token_gradient(prob, prob_got, slots, info, router_matrix, 4)
    late = late + sum(other[:experts].astype(F32) for other in got)
    early = jnp.concatenate([early] + [other[experts:] for other in got], 0)
    got = swap(jnp.concatenate([late.astype(BF16), early], 0), "expert", 2, 1)
    late = late + got[:experts].astype(F32)
    early = jnp.concatenate([early, got[experts:]], 0)
    early = early.reshape(8, -1, early.shape[1])
    grad_down, up_factor_gradient = adapter_late(place, early, late, mixed, router_matrix)
    return (
        hidden_grad.reshape(stored_hidden_state.shape),
        token_grad,
        grad_down,
        up_factor_gradient,
    )


def route_general(saved_router_scores, expert_choice_index, capacity):
    experts = saved_router_scores.shape[1]
    labels = jnp.arange(experts, dtype=jnp.int32)
    choose = expert_choice_index[:, :, None] == labels[None, None, :]
    chosen = jnp.sum(jnp.where(choose, saved_router_scores[:, None, :], 0.0), axis=2)
    first_prob = 1.0 / (1.0 + jnp.exp(chosen[:, 1] - chosen[:, 0]))
    second_prob = 1.0 - first_prob
    in_window = expert_choice_index == 0
    window_flag = jnp.any(in_window, axis=1)
    flag_int = window_flag.astype(jnp.int32)
    slot_index = jnp.cumsum(flag_int) - flag_int
    route_probs = jnp.stack([first_prob, second_prob], axis=1).astype(jnp.bfloat16)
    window_prob = jnp.where(in_window[:, 0], route_probs[:, 0], route_probs[:, 1])
    slot_labels = jnp.arange(capacity, dtype=jnp.int32)
    placement = window_flag[None, :] & (slot_index[None, :] == slot_labels[:, None])
    window_sign = in_window[:, 0].astype(jnp.float32) - in_window[:, 1].astype(jnp.float32)
    sign_table = choose[:, 0, :].astype(jnp.float32) - choose[:, 1, :].astype(jnp.float32)
    factors = (first_prob * second_prob * window_sign)[:, None] * sign_table
    return placement, window_prob, factors


def general_device(
    output_gradient,
    saved_router_scores,
    expert_choice_index,
    router_matrix,
    weight_normalized_entries,
    scales,
    stored_hidden_state,
    context,
    adapter_down_factor,
    adapter_up_factor,
):
    expert_count = lax.axis_size("expert")
    shard_count = lax.axis_size("shard")
    expert = lax.axis_index("expert")
    shard = lax.axis_index("shard")
    tokens, feature_width = output_gradient.shape
    row_count = stored_hidden_state.shape[2]
    capacity = row_count // expert_count
    ff_share = stored_hidden_state.shape[3]
    share_width = feature_width // shard_count
    block_size = weight_normalized_entries.shape[0] // scales.shape[0]
    rank = adapter_up_factor.shape[0]

    placement, window_prob, factors = route_general(saved_router_scores, expert_choice_index, capacity)
    placed = placement.astype(jnp.bfloat16)
    send_rows = jnp.dot(placed, output_gradient, preferred_element_type=jnp.float32).astype(
        jnp.bfloat16
    )
    send_probs = jnp.dot(placed, window_prob, preferred_element_type=jnp.float32).astype(
        jnp.bfloat16
    )
    blocks = lax.all_to_all(
        send_rows.reshape(capacity, shard_count, share_width).transpose(1, 0, 2), "shard", 0, 0
    )
    gathered = lax.all_gather(blocks, "expert", axis=1)
    all_probs = lax.all_gather(send_probs, "expert", axis=0, tiled=True)

    code_blocks = weight_normalized_entries.reshape(scales.shape[0], block_size, ff_share)
    own_weight = (code_blocks * scales[:, None, :]).reshape(
        weight_normalized_entries.shape[0], ff_share
    )
    product = jnp.dot(
        gathered.reshape(shard_count * row_count, share_width),
        own_weight,
        preferred_element_type=jnp.float32,
    ).reshape(shard_count, row_count, ff_share)

    narrow_input = lax.dot_general(
        context, adapter_down_factor, (((1,), (1,)), ((), ())), preferred_element_type=jnp.float32
    ).astype(jnp.bfloat16)
    narrow_gradient = (
        ADAPTER_SCALE
        * lax.dot_general(
            output_gradient,
            adapter_up_factor,
            (((1,), (1,)), ((), ())),
            preferred_element_type=jnp.float32,
        )
    ).astype(jnp.bfloat16)
    early_up = ADAPTER_SCALE * lax.dot_general(
        narrow_input, output_gradient, (((0,), (0,)), ((), ())), preferred_element_type=jnp.float32
    )
    early_down = lax.dot_general(
        narrow_gradient, context, (((0,), (0,)), ((), ())), preferred_element_type=jnp.float32
    )
    early = jnp.concatenate([early_up, early_down], 0)

    total = lax.psum_scatter(product.astype(jnp.bfloat16), "shard", scatter_dimension=0)
    total = total.astype(jnp.float32)
    early = lax.psum(early, ("dp", "expert"))
    early = lax.psum_scatter(early, "shard", scatter_dimension=1, tiled=True)

    hidden_grad = (all_probs.astype(jnp.float32)[:, None] * total).astype(jnp.bfloat16)
    partial_value = jnp.sum(stored_hidden_state[0, 0].astype(jnp.float32) * total, axis=1)
    slot_grad = lax.psum(partial_value, "expert")
    own_grad = lax.dynamic_slice_in_dim(slot_grad, expert * capacity, capacity, 0)
    window_grad = jnp.sum(jnp.where(placement, own_grad[:, None], 0.0), axis=0)
    logit_grad = (factors * window_grad[:, None]).astype(jnp.bfloat16)
    token_grad = jnp.dot(logit_grad, router_matrix, preferred_element_type=jnp.float32).astype(
        jnp.bfloat16
    )
    late_input = lax.dot_general(
        logit_grad, narrow_input, (((0,), (0,)), ((), ())), preferred_element_type=jnp.float32
    )
    late_context = lax.dot_general(
        logit_grad, context, (((0,), (0,)), ((), ())), preferred_element_type=jnp.float32
    )
    late_input = lax.psum(late_input, ("dp", "expert", "shard"))
    late_context = lax.psum(late_context, ("dp", "expert"))
    late_context = lax.psum_scatter(late_context, "shard", scatter_dimension=1, tiled=True)
    own_router = lax.dynamic_slice_in_dim(router_matrix, shard * share_width, share_width, 1)
    factor_router = ADAPTER_SCALE * lax.dot_general(
        adapter_up_factor, router_matrix, (((1,), (1,)), ((), ())), preferred_element_type=jnp.float32
    )
    up_factor_gradient = early[:rank] + ADAPTER_SCALE * lax.dot_general(
        late_input,
        own_router.astype(jnp.float32),
        (((0,), (0,)), ((), ())),
        precision=lax.Precision.HIGHEST,
        preferred_element_type=jnp.float32,
    )
    grad_down = early[rank:] + jnp.dot(
        factor_router,
        late_context,
        precision=lax.Precision.HIGHEST,
        preferred_element_type=jnp.float32,
    )
    return (
        hidden_grad.reshape(stored_hidden_state.shape),
        token_grad,
        grad_down,
        up_factor_gradient,
    )


def solution(mesh):
    axes = dict(mesh.shape)
    direct = (axes["dp"], axes["expert"], axes["shard"]) == (4, 2, 4)
    tokens_spec = P(("dp", "expert", "shard"), None)
    in_specs = (
        tokens_spec,
        tokens_spec,
        tokens_spec,
        P(),
        P("shard", "expert"),
        P("shard", "expert"),
        P("dp", "shard", None, "expert"),
        tokens_spec,
        P(),
        P(),
    )
    out_specs = (
        P("dp", "shard", None, "expert"),
        tokens_spec,
        P(None, "shard"),
        P(None, "shard"),
    )
    return jax.shard_map(
        direct_device if direct else general_device, mesh=mesh, in_specs=in_specs, out_specs=out_specs, check_vma=False
    )
```

```python
import functools

import jax
import jax.numpy as jnp
from jax import lax
from jax.experimental import pallas as pl
from jax.experimental.pallas import tpu as pltpu
from jax.sharding import PartitionSpec as P

ADAPTER_SCALE = 0.25
LANES = 128
F32 = jnp.float32
BF16 = jnp.bfloat16
SMEM = pl.BlockSpec(memory_space=pltpu.SMEM)
VMEM = pl.BlockSpec(memory_space=pltpu.VMEM)
HBM = pl.BlockSpec(memory_space=pltpu.HBM)
EXACT = lax.Precision.HIGHEST


def params(mebibytes=16):
    return pltpu.CompilerParams(vmem_limit_bytes=mebibytes * 1024 * 1024)


def cost(flops, bytes_accessed):
    return pl.CostEstimate(flops=flops, bytes_accessed=bytes_accessed, transcendentals=0)


def in_hbm(value):
    return pltpu.with_memory_space_constraint(value, pltpu.HBM)


def whole(shape):
    return pl.BlockSpec(shape, lambda *_: (0,) * len(shape))


def contract(a, b, dim_a, dim_b, precision=None):
    return lax.dot_general(
        a, b, (((dim_a,), (dim_b,)), ((), ())), precision=precision, preferred_element_type=F32
    )


def xor_pairs(count, bits):
    return [(i, i ^ bits) for i in range(count)]


def feature_block(ref, place, k, width):
    start = pl.multiple_of((place[0] ^ k) * width, LANES)
    return ref[:, pl.ds(start, width)]


def route_kernel(
    place, scores_hbm, choice_hbm, grad_hbm, rows_ref, slots_ref, info_ref,
    scores_ref, choice_ref, grad_ref, sems,
):
    load_scores = pltpu.make_async_copy(scores_hbm, scores_ref, sems.at[0])
    load_choice = pltpu.make_async_copy(choice_hbm, choice_ref, sems.at[1])
    load = pltpu.make_async_copy(grad_hbm, grad_ref, sems.at[2])
    load_scores.start()
    load_choice.start()
    load.start()
    load_scores.wait()
    load_choice.wait()
    scores = scores_ref[...]
    experts, tokens = scores.shape
    shards, capacity, width = rows_ref.shape
    first_choice = choice_ref[0:1, :]
    second_choice = choice_ref[1:2, :]
    labels = lax.broadcasted_iota(jnp.int32, (experts, tokens), 0)
    chosen_first = jnp.sum(jnp.where(labels == first_choice, scores, 0.0), axis=0, keepdims=True)
    chosen_second = jnp.sum(jnp.where(labels == second_choice, scores, 0.0), axis=0, keepdims=True)
    first_prob = 1.0 / (1.0 + jnp.exp(chosen_second - chosen_first))
    second_prob = 1.0 - first_prob
    in_first = (first_choice == 0).astype(F32)
    in_second = (second_choice == 0).astype(F32)
    flags = jnp.broadcast_to(in_first + in_second, (capacity, tokens))
    row = lax.broadcasted_iota(jnp.int32, (tokens, tokens), 0)
    column = lax.broadcasted_iota(jnp.int32, (tokens, tokens), 1)
    before = (row < column).astype(F32).astype(BF16)
    slot = jnp.dot(flags.astype(BF16), before, preferred_element_type=F32)
    number = lax.broadcasted_iota(jnp.int32, (capacity, tokens), 0).astype(F32)
    slots = jnp.where((flags > 0.5) & (slot == number), 1.0, 0.0)
    slots_ref[...] = slots
    sign = (labels == first_choice).astype(F32) - (labels == second_choice).astype(F32)
    info_ref[:experts] = first_prob * second_prob * (in_first - in_second) * sign
    window_prob = jnp.where(in_first > 0.5, first_prob, second_prob)
    info_ref[experts:] = jnp.broadcast_to(window_prob, (info_ref.shape[0] - experts, tokens))
    picks = slots.astype(BF16)
    load.wait()
    for k in range(shards):
        block = feature_block(grad_ref, place, k, width)
        rows_ref[k] = jnp.dot(picks, block, preferred_element_type=F32).astype(BF16)


def route(place, scores, choice, grad, capacity, shards):
    tokens, features = grad.shape
    return pl.pallas_call(
        route_kernel,
        out_shape=(
            jax.ShapeDtypeStruct((shards, capacity, features // shards), BF16),
            jax.ShapeDtypeStruct((capacity, tokens), F32),
            jax.ShapeDtypeStruct((2 * scores.shape[1], tokens), F32),
        ),
        in_specs=[SMEM, HBM, HBM, HBM],
        out_specs=(VMEM,) * 3,
        scratch_shapes=[
            pltpu.VMEM(scores.T.shape, F32),
            pltpu.VMEM(choice.T.shape, jnp.int32),
            pltpu.VMEM(grad.shape, BF16),
            pltpu.SemaphoreType.DMA((3,)),
        ],
        compiler_params=params(),
        cost_estimate=cost(2 * tokens * capacity * features, 2 * tokens * features),
        name="route",
    )(place, in_hbm(scores.T), in_hbm(choice.T), in_hbm(grad))


def product_kernel(half, place, rows_ref, weight_ref, *refs):
    outs, lhs = refs[-5:-1], refs[-1]
    shards, capacity, _ = rows_ref.shape
    is_end = place[3]
    order = (1 + 2 * is_end, 2, 3 - 2 * is_end, 0)
    for slot, k in enumerate(order):
        lhs[slot * capacity : (slot + 1) * capacity] = rows_ref[k]
    rows = slice(half * capacity, (half + 1) * capacity)
    tile = 512
    for t in range(weight_ref.shape[1] // tile):
        part = slice(t * tile, (t + 1) * tile)
        result = jnp.dot(lhs[...], weight_ref[:, part], preferred_element_type=F32)
        for slot, ref in enumerate(outs):
            ref[rows, part] = result[slot * capacity : (slot + 1) * capacity].astype(ref.dtype)


def products(place, rows, weight, before=()):
    shards, capacity, width = rows.shape
    hidden = weight.shape[1]
    sent = pltpu.VMEM((2 * capacity, hidden), BF16)
    return pl.pallas_call(
        functools.partial(product_kernel, len(before) // 4),
        out_shape=(sent, sent, sent, pltpu.VMEM((2 * capacity, hidden), F32)),
        in_specs=[SMEM, VMEM, VMEM] + [VMEM] * len(before),
        out_specs=(VMEM,) * 4,
        input_output_aliases={3 + i: i for i in range(len(before))},
        scratch_shapes=[pltpu.VMEM((shards * capacity, width), BF16)],
        compiler_params=params(),
        cost_estimate=cost(2 * shards * capacity * width * hidden, 2 * width * hidden),
        name="products",
    )(place, rows, pltpu.with_memory_space_constraint(weight, pltpu.VMEM), *before)


def forward_kernel(place, far_ref, near_ref, out_ref):
    keep = 1.0 - place[3].astype(F32)
    out_ref[...] = (far_ref[...].astype(F32) + keep * near_ref[...].astype(F32)).astype(BF16)


def add_near(place, far, near):
    return pl.pallas_call(
        forward_kernel,
        out_shape=pltpu.VMEM(far.shape, BF16),
        in_specs=[SMEM, VMEM, VMEM],
        out_specs=VMEM,
        compiler_params=params(),
        cost_estimate=cost(2 * far.size, 6 * far.size),
        name="add_near",
    )(place, far, near)


def partial_kernel(place, own_ref, near_ref, middle_ref, far_ref, out_ref):
    is_end = place[3].astype(F32)
    out_ref[...] = (
        own_ref[...]
        + is_end * near_ref[...].astype(F32)
        + (1.0 - is_end) * middle_ref[...].astype(F32)
        + far_ref[...].astype(F32)
    )


def add_far(place, own, near, middle, far):
    return pl.pallas_call(
        partial_kernel,
        out_shape=pltpu.VMEM(own.shape, F32),
        in_specs=[SMEM] + [VMEM] * 4,
        out_specs=VMEM,
        compiler_params=params(),
        cost_estimate=cost(round(3.0 * 1e9), 14 * own.size),
        name="add_far",
    )(place, own, near, middle, far)


def weight_kernel(codes_hbm, scales_hbm, weight_ref, codes_ref, scales_ref, scale_sem, sems):
    load_scales = pltpu.make_async_copy(scales_hbm, scales_ref, scale_sem)
    load_scales.start()
    tiles = sems.shape[0]
    tile = codes_ref.shape[1] // tiles
    loads = []
    for t in range(tiles):
        part = pl.ds(t * tile, tile)
        loads.append(
            pltpu.make_async_copy(codes_hbm.at[:, part], codes_ref.at[:, part], sems.at[t])
        )
        loads[t].start()
    blocks = scales_ref.shape[0]
    size = codes_ref.shape[0] // blocks
    load_scales.wait()
    for t in range(tiles):
        loads[t].wait()
        part = slice(t * tile, (t + 1) * tile)
        for b in range(blocks):
            rows = slice(b * size, (b + 1) * size)
            weight_ref[rows, part] = codes_ref[rows, part] * scales_ref[b : b + 1, part]


def dequantize(codes, scales, tiles):
    return pl.pallas_call(
        weight_kernel,
        out_shape=pltpu.VMEM(codes.shape, BF16),
        in_specs=[HBM, HBM],
        out_specs=VMEM,
        scratch_shapes=[
            pltpu.VMEM(codes.shape, BF16),
            pltpu.VMEM(scales.shape, BF16),
            pltpu.SemaphoreType.DMA,
            pltpu.SemaphoreType.DMA((tiles,)),
        ],
        compiler_params=params(),
        cost_estimate=cost(codes.size, 4 * codes.size),
        name="dequantize",
    )(in_hbm(codes), in_hbm(scales))


def adapter_kernel(
    place, grad_hbm, context_hbm, down_hbm, up_hbm, router_hbm, slots_ref, info_ref,
    early_ref, picked_ref, mixed_ref,
    grad_ref, context_ref, down_ref, up_ref, router_ref, sems,
):
    pairs = (
        (context_hbm, context_ref),
        (down_hbm, down_ref),
        (grad_hbm, grad_ref),
        (up_hbm, up_ref),
        (router_hbm, router_ref),
    )
    loads = [
        pltpu.make_async_copy(source, target, sems.at[i])
        for i, (source, target) in enumerate(pairs)
    ]
    for load in loads:
        load.start()
    groups, shards, rows, width = early_ref.shape
    capacity = picked_ref.shape[0]
    features = shards * width
    half = groups // 2
    loads[0].wait()
    loads[1].wait()
    low_in = contract(context_ref[...], down_ref[...], 1, 1).astype(BF16)
    for load in loads[2:]:
        load.wait()
    low_grad = (ADAPTER_SCALE * contract(grad_ref[...], up_ref[...], 1, 1)).astype(BF16)
    mixed_ref[...] = ADAPTER_SCALE * contract(up_ref[...], router_ref[...], 1, 1)
    slots = slots_ref[...].astype(BF16)
    for k in range(shards):
        grad = feature_block(grad_ref, place, k, width)
        context = feature_block(context_ref, place, k, width)
        up = ADAPTER_SCALE * contract(low_in, grad, 0, 0)
        down = contract(low_grad, context, 0, 0)
        for g in range(half):
            early_ref[g ^ place[1], k] = up[g * rows : (g + 1) * rows]
            early_ref[(g + half) ^ place[1], k] = down[g * rows : (g + 1) * rows]
        picked_ref[:, k * width : (k + 1) * width] = jnp.dot(
            slots, context, preferred_element_type=F32
        ).astype(BF16)
    low = jnp.dot(slots, low_in, preferred_element_type=F32).astype(BF16)
    picked_ref[:, features:] = jnp.zeros((capacity, 2 * LANES), BF16)
    picked_ref[:, features : features + low.shape[1]] = low
    info = contract(slots_ref[...], info_ref[...], 1, 1, EXACT)
    picked_ref[:, features + LANES : features + LANES + info.shape[1]] = info.astype(BF16)


def adapter_early(place, grad, context, down, up, router, slots, info, groups, shards):
    tokens, features = grad.shape
    rank = up.shape[0]
    rows = 2 * rank // groups
    arrays = (grad, context, down, up, router)
    return pl.pallas_call(
        adapter_kernel,
        out_shape=(
            jax.ShapeDtypeStruct((groups, shards, rows, features // shards), F32),
            jax.ShapeDtypeStruct((slots.shape[0], features + 2 * LANES), BF16),
            jax.ShapeDtypeStruct((rank, router.shape[0]), F32),
        ),
        in_specs=[SMEM] + [HBM] * 5 + [VMEM] * 2,
        out_specs=(VMEM,) * 3,
        scratch_shapes=[pltpu.VMEM(value.shape, BF16) for value in arrays]
        + [pltpu.SemaphoreType.DMA((5,))],
        compiler_params=params(),
        cost_estimate=cost(0, 0),
        name="adapter_early",
    )(place, *[in_hbm(value) for value in arrays], slots, info)


def finish_kernel(
    experts, place, partial_ref, outer_ref, hidden_ref, picked_ref, other_ref,
    product_ref, prob_ref, prob_other_ref, late_ref,
):
    shards, _, late_width = late_ref.shape
    width = late_width - LANES
    features = shards * width
    is_end = place[3].astype(F32)
    hidden = outer_ref.shape[1]
    tile = 512
    capacity = picked_ref.shape[0]
    pickeds = (picked_ref, other_ref)
    infos = [ref[:, features + LANES :].astype(F32) for ref in pickeds]
    totals = [jnp.zeros((capacity, LANES), F32) for _ in pickeds]
    for t in range(hidden // tile):
        part = slice(t * tile, (t + 1) * tile)
        for half in range(2):
            rows = slice(half * capacity, (half + 1) * capacity)
            whole_rows = pl.ds(pl.multiple_of((place[2] ^ half) * capacity, capacity), capacity)
            product = partial_ref[rows, part] + (1.0 - is_end) * outer_ref[rows, part].astype(F32)
            product_ref[rows, part] = product
            weighted = hidden_ref[whole_rows, part].astype(F32) * product
            for j in range(tile // LANES):
                totals[half] = totals[half] + weighted[:, j * LANES : (j + 1) * LANES]
    lane = lax.broadcasted_iota(jnp.int32, (capacity, LANES), 1)
    logits = []
    for info, total, out in zip(infos, totals, (prob_ref, prob_other_ref), strict=True):
        prob = jnp.sum(total, axis=1, keepdims=True)
        out[...] = jnp.broadcast_to(prob, out.shape)
        logits.append(jnp.where(lane < experts, info * prob, 0.0).astype(BF16))

    def late(columns):
        return sum(
            contract(logit, ref[:, columns], 0, 0)[:experts]
            for logit, ref in zip(logits, pickeds, strict=True)
        )

    low = late(slice(features, features + LANES))
    for k in range(shards):
        late_ref[k, :, :width] = late(slice(k * width, (k + 1) * width))
        late_ref[k, :, width:] = low


def hidden_kernel(experts, place, product_ref, picked_ref, other_ref, grad_hbm, grad_ref, sems):
    capacity = picked_ref.shape[0]
    column = picked_ref.shape[1] - LANES + experts
    tiles = sems.shape[0]
    tile = product_ref.shape[1] // tiles
    stores = []
    for t in range(tiles):
        part = pl.ds(t * tile, tile)
        for half, ref in enumerate((picked_ref, other_ref)):
            rows = slice(half * capacity, (half + 1) * capacity)
            whole_rows = pl.ds(pl.multiple_of((place[2] ^ half) * capacity, capacity), capacity)
            window_prob = ref[:, column - experts :].astype(F32)[:, experts : experts + 1]
            grad_ref[whole_rows, part] = (window_prob * product_ref[rows, part]).astype(BF16)
        store = pltpu.make_async_copy(grad_ref.at[:, part], grad_hbm.at[:, part], sems.at[t])
        store.start()
        stores.append(store)
    for store in stores:
        store.wait()


def hidden_gradient(place, product, picked, other, experts, tiles):
    return pl.pallas_call(
        functools.partial(hidden_kernel, experts),
        out_shape=jax.ShapeDtypeStruct(product.shape, BF16),
        in_specs=[SMEM] + [VMEM] * 3,
        out_specs=HBM,
        scratch_shapes=[pltpu.VMEM(product.shape, BF16), pltpu.SemaphoreType.DMA((tiles,))],
        compiler_params=params(),
        cost_estimate=cost(0, 0),
        name="hidden_gradient",
    )(place, product, picked, other)


def finish(place, partial, outer, hidden_state, picked, other, experts, shards):
    rows, hidden = outer.shape
    capacity = picked.shape[0]
    width = (picked.shape[1] - 2 * LANES) // shards
    return pl.pallas_call(
        functools.partial(finish_kernel, experts),
        out_shape=(
            pltpu.VMEM((rows, hidden), F32),
            jax.ShapeDtypeStruct((capacity, LANES), F32),
            jax.ShapeDtypeStruct((capacity, LANES), F32),
            jax.ShapeDtypeStruct((shards, experts, width + LANES), F32),
        ),
        in_specs=[SMEM] + [VMEM] * 5,
        out_specs=(VMEM,) * 4,
        compiler_params=params(),
        cost_estimate=cost(8 * rows * hidden, 10 * rows * hidden),
        name="finish",
    )(place, partial, outer, hidden_state, picked, other)


def token_kernel(prob_ref, prob_got_ref, slots_ref, info_ref, router_ref, token_hbm, token_ref, sems):
    experts = router_ref.shape[0]
    own = prob_ref[:, 0:1] + prob_got_ref[:, 0:1]
    window = jnp.sum(slots_ref[...] * own, axis=0, keepdims=True)
    logits = (info_ref[:experts] * window).astype(BF16)
    tiles = sems.shape[0]
    tile = token_ref.shape[1] // tiles
    stores = []
    for t in range(tiles):
        part = pl.ds(t * tile, tile)
        token_ref[:, part] = contract(logits, router_ref[:, part], 0, 0).astype(BF16)
        store = pltpu.make_async_copy(token_ref.at[:, part], token_hbm.at[:, part], sems.at[t])
        store.start()
        stores.append(store)
    for store in stores:
        store.wait()


def token_gradient(prob, prob_got, slots, info, router, tiles):
    tokens = slots.shape[1]
    features = router.shape[1]
    return pl.pallas_call(
        token_kernel,
        out_shape=jax.ShapeDtypeStruct((tokens, features), BF16),
        in_specs=[VMEM] * 5,
        out_specs=HBM,
        scratch_shapes=[pltpu.VMEM((tokens, features), BF16), pltpu.SemaphoreType.DMA((tiles,))],
        compiler_params=params(),
        cost_estimate=cost(2 * tokens * features * router.shape[0], 2 * tokens * features),
        name="token_gradient",
    )(prob, prob_got, slots, info, router)


def adapter_late_kernel(
    place, early_ref, late_ref, mixed_ref, router_ref, down_hbm, up_hbm, down_ref, up_ref, sems
):
    groups, rows, _ = early_ref.shape
    half = groups // 2
    rank, width = up_ref.shape
    parts = [slice(g * rows, (g + 1) * rows) for g in range(half)]
    down = jnp.dot(
        mixed_ref[...].astype(BF16),
        late_ref[:, :width].astype(BF16),
        preferred_element_type=F32,
    )
    for g, part in enumerate(parts):
        down_ref[part] = early_ref[(g + half) ^ place[1], :, :width].astype(F32) + down[part]
    store_down = pltpu.make_async_copy(down_ref, down_hbm, sems.at[0])
    store_down.start()
    router = feature_block(router_ref, place, 0, width)
    up = ADAPTER_SCALE * contract(late_ref[:, width : width + rank].astype(BF16), router, 0, 0)
    for g, part in enumerate(parts):
        up_ref[part] = early_ref[g ^ place[1], :, :width].astype(F32) + up[part]
    store_up = pltpu.make_async_copy(up_ref, up_hbm, sems.at[1])
    store_up.start()
    store_down.wait()
    store_up.wait()


def adapter_late(place, early, late, mixed, router):
    groups, rows, width = early.shape
    out = jax.ShapeDtypeStruct((groups * rows // 2, width - LANES), F32)
    return pl.pallas_call(
        adapter_late_kernel,
        out_shape=(out, out),
        in_specs=[SMEM] + [VMEM] * 4,
        out_specs=(HBM, HBM),
        scratch_shapes=[pltpu.VMEM(out.shape, F32)] * 2 + [pltpu.SemaphoreType.DMA((2,))],
        compiler_params=params(),
        cost_estimate=cost(64 * groups * rows * width, 8 * groups * rows * width),
        name="adapter_late",
    )(place, early, late, mixed, router)


def swap(value, axis, count, bits):
    return lax.ppermute(value, axis, xor_pairs(count, bits))


def swap_group(value, bits):
    pairs = [(d * 2 + e, (d ^ (bits & 3)) * 2 + (e ^ (bits >> 2))) for d in range(4) for e in range(2)]
    return lax.ppermute(value, ("dp", "expert"), pairs)


def after(value, *others):
    return lax.optimization_barrier((value,) + others)[0]


def direct_device(
    output_gradient,
    saved_router_scores,
    expert_choice_index,
    router_matrix,
    weight_normalized_entries,
    scales,
    stored_hidden_state,
    context,
    adapter_down_factor,
    adapter_up_factor,
):
    dp = lax.axis_index("dp")
    expert = lax.axis_index("expert")
    shard = lax.axis_index("shard")
    is_end = ((shard == 0) | (shard == 3)).astype(jnp.int32)
    group = expert * 4 + dp
    place = jnp.stack([shard, group, expert, is_end]).astype(jnp.int32)
    row_count, ff_share = stored_hidden_state.shape[2:]
    capacity = row_count // 2
    experts = saved_router_scores.shape[1]

    send_rows, slots, info = route(
        place, saved_router_scores, expert_choice_index, output_gradient, capacity, 4
    )
    rows = jnp.stack(
        [send_rows[0]] + [swap(send_rows[k], "shard", 4, k) for k in range(1, 4)]
    )
    weight = dequantize(weight_normalized_entries, scales, 4)
    rows, weight = lax.optimization_barrier((rows, weight))
    other_rows = swap(rows, "expert", 2, 1)

    partial = products(place, rows, weight)
    first, far, last, own = products(place, other_rows, weight, partial)
    near = swap(first, "shard", 4, 1)
    middle = lax.ppermute(last, "shard", [(1, 2), (2, 1)])
    early, picked, mixed = adapter_early(
        after(place, last), output_gradient, context, adapter_down_factor, adapter_up_factor,
        router_matrix, slots, info, 8, 4,
    )
    far, near, early, picked = lax.optimization_barrier((far, near, early, picked))
    forward = add_near(place, far, near)
    across = swap(forward, "shard", 4, 2)
    forward, last, middle = lax.optimization_barrier((forward, last, middle))
    outer = lax.ppermute(last, "shard", [(0, 1), (3, 2)])
    forward, early, picked = lax.optimization_barrier((forward, early, picked))
    other_picked = swap(picked, "expert", 2, 1)
    parts = early.astype(BF16)
    early = early[0] + sum(swap_group(parts[g], g).astype(F32) for g in range(1, 8))
    partial = add_far(place, own, near, middle, across)
    partial, outer, early, other_picked = lax.optimization_barrier(
        (partial, outer, early, other_picked)
    )

    product, prob, prob_other, late = finish(
        place, partial, outer, stored_hidden_state[0, 0], picked, other_picked, experts, 4
    )
    early = jnp.pad(early, ((0, 0), (0, 0), (0, LANES)))
    late = jnp.concatenate([late, early], 1)
    late = late[:2] + swap(late[2:].astype(BF16), "shard", 4, 2).astype(F32)
    hidden_grad = hidden_gradient(place, product, picked, other_picked, experts, 4)
    late, hidden_grad = lax.optimization_barrier((late, hidden_grad))
    prob_got = swap(prob_other, "expert", 2, 1)
    late = late[0] + swap(late[1].astype(BF16), "shard", 4, 1).astype(F32)
    late, early = late[:experts], late[experts:].astype(BF16)
    mine = jnp.concatenate([late.astype(BF16), early], 0)
    got = [swap(mine, "dp", 4, k) for k in range(1, 4)]
    token_grad = token_gradient(prob, prob_got, slots, info, router_matrix, 4)
    late = late + sum(other[:experts].astype(F32) for other in got)
    early = jnp.concatenate([early] + [other[experts:] for other in got], 0)
    got = swap(jnp.concatenate([late.astype(BF16), early], 0), "expert", 2, 1)
    late = late + got[:experts].astype(F32)
    early = jnp.concatenate([early, got[experts:]], 0)
    early = early.reshape(8, -1, early.shape[1])
    grad_down, up_factor_gradient = adapter_late(place, early, late, mixed, router_matrix)
    return (
        hidden_grad.reshape(stored_hidden_state.shape),
        token_grad,
        grad_down,
        up_factor_gradient,
    )


def route_general(saved_router_scores, expert_choice_index, capacity):
    experts = saved_router_scores.shape[1]
    labels = jnp.arange(experts, dtype=jnp.int32)
    choose = expert_choice_index[:, :, None] == labels[None, None, :]
    chosen = jnp.sum(jnp.where(choose, saved_router_scores[:, None, :], 0.0), axis=2)
    first_prob = 1.0 / (1.0 + jnp.exp(chosen[:, 1] - chosen[:, 0]))
    second_prob = 1.0 - first_prob
    in_window = expert_choice_index == 0
    window_flag = jnp.any(in_window, axis=1)
    flag_int = window_flag.astype(jnp.int32)
    slot_index = jnp.cumsum(flag_int) - flag_int
    route_probs = jnp.stack([first_prob, second_prob], axis=1).astype(jnp.bfloat16)
    window_prob = jnp.where(in_window[:, 0], route_probs[:, 0], route_probs[:, 1])
    slot_labels = jnp.arange(capacity, dtype=jnp.int32)
    placement = window_flag[None, :] & (slot_index[None, :] == slot_labels[:, None])
    window_sign = in_window[:, 0].astype(jnp.float32) - in_window[:, 1].astype(jnp.float32)
    sign_table = choose[:, 0, :].astype(jnp.float32) - choose[:, 1, :].astype(jnp.float32)
    factors = (first_prob * second_prob * window_sign)[:, None] * sign_table
    return placement, window_prob, factors


def general_device(
    output_gradient,
    saved_router_scores,
    expert_choice_index,
    router_matrix,
    weight_normalized_entries,
    scales,
    stored_hidden_state,
    context,
    adapter_down_factor,
    adapter_up_factor,
):
    expert_count = lax.axis_size("expert")
    shard_count = lax.axis_size("shard")
    expert = lax.axis_index("expert")
    shard = lax.axis_index("shard")
    tokens, feature_width = output_gradient.shape
    row_count = stored_hidden_state.shape[2]
    capacity = row_count // expert_count
    ff_share = stored_hidden_state.shape[3]
    share_width = feature_width // shard_count
    block_size = weight_normalized_entries.shape[0] // scales.shape[0]
    rank = adapter_up_factor.shape[0]

    placement, window_prob, factors = route_general(saved_router_scores, expert_choice_index, capacity)
    placed = placement.astype(jnp.bfloat16)
    send_rows = jnp.dot(placed, output_gradient, preferred_element_type=jnp.float32).astype(
        jnp.bfloat16
    )
    send_probs = jnp.dot(placed, window_prob, preferred_element_type=jnp.float32).astype(
        jnp.bfloat16
    )
    blocks = lax.all_to_all(
        send_rows.reshape(capacity, shard_count, share_width).transpose(1, 0, 2), "shard", 0, 0
    )
    gathered = lax.all_gather(blocks, "expert", axis=1)
    all_probs = lax.all_gather(send_probs, "expert", axis=0, tiled=True)

    code_blocks = weight_normalized_entries.reshape(scales.shape[0], block_size, ff_share)
    own_weight = (code_blocks * scales[:, None, :]).reshape(
        weight_normalized_entries.shape[0], ff_share
    )
    product = jnp.dot(
        gathered.reshape(shard_count * row_count, share_width),
        own_weight,
        preferred_element_type=jnp.float32,
    ).reshape(shard_count, row_count, ff_share)

    narrow_input = lax.dot_general(
        context, adapter_down_factor, (((1,), (1,)), ((), ())), preferred_element_type=jnp.float32
    ).astype(jnp.bfloat16)
    narrow_gradient = (
        ADAPTER_SCALE
        * lax.dot_general(
            output_gradient,
            adapter_up_factor,
            (((1,), (1,)), ((), ())),
            preferred_element_type=jnp.float32,
        )
    ).astype(jnp.bfloat16)
    early_up = ADAPTER_SCALE * lax.dot_general(
        narrow_input, output_gradient, (((0,), (0,)), ((), ())), preferred_element_type=jnp.float32
    )
    early_down = lax.dot_general(
        narrow_gradient, context, (((0,), (0,)), ((), ())), preferred_element_type=jnp.float32
    )
    early = jnp.concatenate([early_up, early_down], 0)

    total = lax.psum_scatter(product.astype(jnp.bfloat16), "shard", scatter_dimension=0)
    total = total.astype(jnp.float32)
    early = lax.psum(early, ("dp", "expert"))
    early = lax.psum_scatter(early, "shard", scatter_dimension=1, tiled=True)

    hidden_grad = (all_probs.astype(jnp.float32)[:, None] * total).astype(jnp.bfloat16)
    partial_value = jnp.sum(stored_hidden_state[0, 0].astype(jnp.float32) * total, axis=1)
    slot_grad = lax.psum(partial_value, "expert")
    own_grad = lax.dynamic_slice_in_dim(slot_grad, expert * capacity, capacity, 0)
    window_grad = jnp.sum(jnp.where(placement, own_grad[:, None], 0.0), axis=0)
    logit_grad = (factors * window_grad[:, None]).astype(jnp.bfloat16)
    token_grad = jnp.dot(logit_grad, router_matrix, preferred_element_type=jnp.float32).astype(
        jnp.bfloat16
    )
    late_input = lax.dot_general(
        logit_grad, narrow_input, (((0,), (0,)), ((), ())), preferred_element_type=jnp.float32
    )
    late_context = lax.dot_general(
        logit_grad, context, (((0,), (0,)), ((), ())), preferred_element_type=jnp.float32
    )
    late_input = lax.psum(late_input, ("dp", "expert", "shard"))
    late_context = lax.psum(late_context, ("dp", "expert"))
    late_context = lax.psum_scatter(late_context, "shard", scatter_dimension=1, tiled=True)
    own_router = lax.dynamic_slice_in_dim(router_matrix, shard * share_width, share_width, 1)
    factor_router = ADAPTER_SCALE * lax.dot_general(
        adapter_up_factor, router_matrix, (((1,), (1,)), ((), ())), preferred_element_type=jnp.float32
    )
    up_factor_gradient = early[:rank] + ADAPTER_SCALE * lax.dot_general(
        late_input,
        own_router.astype(jnp.float32),
        (((0,), (0,)), ((), ())),
        precision=lax.Precision.HIGHEST,
        preferred_element_type=jnp.float32,
    )
    grad_down = early[rank:] + jnp.dot(
        factor_router,
        late_context,
        precision=lax.Precision.HIGHEST,
        preferred_element_type=jnp.float32,
    )
    return (
        hidden_grad.reshape(stored_hidden_state.shape),
        token_grad,
        grad_down,
        up_factor_gradient,
    )


def solution(mesh):
    axes = dict(mesh.shape)
    direct = (axes["dp"], axes["expert"], axes["shard"]) == (4, 2, 4)
    tokens_spec = P(("dp", "expert", "shard"), None)
    in_specs = (
        tokens_spec,
        tokens_spec,
        tokens_spec,
        P(),
        P("shard", "expert"),
        P("shard", "expert"),
        P("dp", "shard", None, "expert"),
        tokens_spec,
        P(),
        P(),
    )
    out_specs = (
        P("dp", "shard", None, "expert"),
        tokens_spec,
        P(None, "shard"),
        P(None, "shard"),
    )
    return jax.shard_map(
        direct_device if direct else general_device, mesh=mesh, in_specs=in_specs, out_specs=out_specs, check_vma=False
    )
```

```python
import functools

import jax
import jax.numpy as jnp
from jax import lax
from jax.experimental import pallas as pl
from jax.experimental.pallas import tpu as pltpu
from jax.sharding import PartitionSpec as P

ADAPTER_SCALE = 0.25
LANES = 128
F32 = jnp.float32
BF16 = jnp.bfloat16
SMEM = pl.BlockSpec(memory_space=pltpu.SMEM)
VMEM = pl.BlockSpec(memory_space=pltpu.VMEM)
HBM = pl.BlockSpec(memory_space=pltpu.HBM)
EXACT = lax.Precision.HIGHEST


def params(mebibytes=16):
    return pltpu.CompilerParams(vmem_limit_bytes=mebibytes * 1024 * 1024)


def cost(flops, bytes_accessed):
    return pl.CostEstimate(flops=flops, bytes_accessed=bytes_accessed, transcendentals=0)


def in_hbm(value):
    return pltpu.with_memory_space_constraint(value, pltpu.HBM)


def whole(shape):
    return pl.BlockSpec(shape, lambda *_: (0,) * len(shape))


def contract(a, b, dim_a, dim_b, precision=None):
    return lax.dot_general(
        a, b, (((dim_a,), (dim_b,)), ((), ())), precision=precision, preferred_element_type=F32
    )


def xor_pairs(count, bits):
    return [(i, i ^ bits) for i in range(count)]


def feature_block(ref, place, k, width):
    start = pl.multiple_of((place[0] ^ k) * width, LANES)
    return ref[:, pl.ds(start, width)]


def route_kernel(
    place, scores_hbm, choice_hbm, grad_hbm, rows_ref, slots_ref, info_ref,
    scores_ref, choice_ref, grad_ref, sems,
):
    load_scores = pltpu.make_async_copy(scores_hbm, scores_ref, sems.at[0])
    load_choice = pltpu.make_async_copy(choice_hbm, choice_ref, sems.at[1])
    load = pltpu.make_async_copy(grad_hbm, grad_ref, sems.at[2])
    load_scores.start()
    load_choice.start()
    load.start()
    load_scores.wait()
    load_choice.wait()
    scores = scores_ref[...]
    experts, tokens = scores.shape
    shards, capacity, width = rows_ref.shape
    first_choice = choice_ref[0:1, :]
    second_choice = choice_ref[1:2, :]
    labels = lax.broadcasted_iota(jnp.int32, (experts, tokens), 0)
    chosen_first = jnp.sum(jnp.where(labels == first_choice, scores, 0.0), axis=0, keepdims=True)
    chosen_second = jnp.sum(jnp.where(labels == second_choice, scores, 0.0), axis=0, keepdims=True)
    first_prob = 1.0 / (1.0 + jnp.exp(chosen_second - chosen_first))
    second_prob = 1.0 - first_prob
    in_first = (first_choice == 0).astype(F32)
    in_second = (second_choice == 0).astype(F32)
    flags = jnp.broadcast_to(in_first + in_second, (capacity, tokens))
    row = lax.broadcasted_iota(jnp.int32, (tokens, tokens), 0)
    column = lax.broadcasted_iota(jnp.int32, (tokens, tokens), 1)
    before = (row < column).astype(F32).astype(BF16)
    slot = jnp.dot(flags.astype(BF16), before, preferred_element_type=F32)
    number = lax.broadcasted_iota(jnp.int32, (capacity, tokens), 0).astype(F32)
    slots = jnp.where((flags > 0.5) & (slot == number), 1.0, 0.0)
    slots_ref[...] = slots
    sign = (labels == first_choice).astype(F32) - (labels == second_choice).astype(F32)
    info_ref[:experts] = first_prob * second_prob * (in_first - in_second) * sign
    window_prob = jnp.where(in_first > 0.5, first_prob, second_prob)
    info_ref[experts:] = jnp.broadcast_to(window_prob, (info_ref.shape[0] - experts, tokens))
    picks = slots.astype(BF16)
    load.wait()
    for k in range(shards):
        block = feature_block(grad_ref, place, k, width)
        rows_ref[k] = jnp.dot(picks, block, preferred_element_type=F32).astype(BF16)


def route(place, scores, choice, grad, capacity, shards):
    tokens, features = grad.shape
    return pl.pallas_call(
        route_kernel,
        out_shape=(
            jax.ShapeDtypeStruct((shards, capacity, features // shards), BF16),
            jax.ShapeDtypeStruct((capacity, tokens), F32),
            jax.ShapeDtypeStruct((2 * scores.shape[1], tokens), F32),
        ),
        in_specs=[SMEM, HBM, HBM, HBM],
        out_specs=(VMEM,) * 3,
        scratch_shapes=[
            pltpu.VMEM(scores.T.shape, F32),
            pltpu.VMEM(choice.T.shape, jnp.int32),
            pltpu.VMEM(grad.shape, BF16),
            pltpu.SemaphoreType.DMA((3,)),
        ],
        compiler_params=params(),
        cost_estimate=cost(2 * tokens * capacity * features, 2 * tokens * features),
        name="route",
    )(place, in_hbm(scores.T), in_hbm(choice.T), in_hbm(grad))


def product_kernel(half, place, rows_ref, weight_ref, *refs):
    outs, lhs = refs[-5:-1], refs[-1]
    shards, capacity, _ = rows_ref.shape
    is_end = place[3]
    order = (1 + 2 * is_end, 2, 3 - 2 * is_end, 0)
    for slot, k in enumerate(order):
        lhs[slot * capacity : (slot + 1) * capacity] = rows_ref[k]
    rows = slice(half * capacity, (half + 1) * capacity)
    tile = 512
    for t in range(weight_ref.shape[1] // tile):
        part = slice(t * tile, (t + 1) * tile)
        result = jnp.dot(lhs[...], weight_ref[:, part], preferred_element_type=F32)
        for slot, ref in enumerate(outs):
            ref[rows, part] = result[slot * capacity : (slot + 1) * capacity].astype(ref.dtype)


def products(place, rows, weight, before=()):
    shards, capacity, width = rows.shape
    hidden = weight.shape[1]
    sent = pltpu.VMEM((2 * capacity, hidden), BF16)
    return pl.pallas_call(
        functools.partial(product_kernel, len(before) // 4),
        out_shape=(sent, sent, sent, pltpu.VMEM((2 * capacity, hidden), F32)),
        in_specs=[SMEM, VMEM, VMEM] + [VMEM] * len(before),
        out_specs=(VMEM,) * 4,
        input_output_aliases={3 + i: i for i in range(len(before))},
        scratch_shapes=[pltpu.VMEM((shards * capacity, width), BF16)],
        compiler_params=params(),
        cost_estimate=cost(2 * shards * capacity * width * hidden, 2 * width * hidden),
        name="products",
    )(place, rows, pltpu.with_memory_space_constraint(weight, pltpu.VMEM), *before)


def forward_kernel(place, far_ref, near_ref, out_ref):
    keep = 1.0 - place[3].astype(F32)
    out_ref[...] = (far_ref[...].astype(F32) + keep * near_ref[...].astype(F32)).astype(BF16)


def add_near(place, far, near):
    return pl.pallas_call(
        forward_kernel,
        out_shape=pltpu.VMEM(far.shape, BF16),
        in_specs=[SMEM, VMEM, VMEM],
        out_specs=VMEM,
        compiler_params=params(),
        cost_estimate=cost(2 * far.size, 6 * far.size),
        name="add_near",
    )(place, far, near)


def partial_kernel(place, own_ref, near_ref, middle_ref, far_ref, out_ref):
    is_end = place[3].astype(F32)
    out_ref[...] = (
        own_ref[...]
        + is_end * near_ref[...].astype(F32)
        + (1.0 - is_end) * middle_ref[...].astype(F32)
        + far_ref[...].astype(F32)
    )


def add_far(place, own, near, middle, far):
    return pl.pallas_call(
        partial_kernel,
        out_shape=pltpu.VMEM(own.shape, F32),
        in_specs=[SMEM] + [VMEM] * 4,
        out_specs=VMEM,
        compiler_params=params(),
        cost_estimate=cost(round(3.0 * 1e9), 14 * own.size),
        name="add_far",
    )(place, own, near, middle, far)


def weight_kernel(codes_hbm, scales_hbm, weight_ref, codes_ref, scales_ref, scale_sem, sems):
    load_scales = pltpu.make_async_copy(scales_hbm, scales_ref, scale_sem)
    load_scales.start()
    tiles = sems.shape[0]
    tile = codes_ref.shape[1] // tiles
    loads = []
    for t in range(tiles):
        part = pl.ds(t * tile, tile)
        loads.append(
            pltpu.make_async_copy(codes_hbm.at[:, part], codes_ref.at[:, part], sems.at[t])
        )
        loads[t].start()
    blocks = scales_ref.shape[0]
    size = codes_ref.shape[0] // blocks
    load_scales.wait()
    for t in range(tiles):
        loads[t].wait()
        part = slice(t * tile, (t + 1) * tile)
        for b in range(blocks):
            rows = slice(b * size, (b + 1) * size)
            weight_ref[rows, part] = codes_ref[rows, part] * scales_ref[b : b + 1, part]


def dequantize(codes, scales, tiles):
    return pl.pallas_call(
        weight_kernel,
        out_shape=pltpu.VMEM(codes.shape, BF16),
        in_specs=[HBM, HBM],
        out_specs=VMEM,
        scratch_shapes=[
            pltpu.VMEM(codes.shape, BF16),
            pltpu.VMEM(scales.shape, BF16),
            pltpu.SemaphoreType.DMA,
            pltpu.SemaphoreType.DMA((tiles,)),
        ],
        compiler_params=params(),
        cost_estimate=cost(codes.size, 4 * codes.size),
        name="dequantize",
    )(in_hbm(codes), in_hbm(scales))


def adapter_kernel(
    place, grad_hbm, context_hbm, down_hbm, up_hbm, router_hbm, slots_ref, info_ref,
    early_ref, picked_ref, mixed_ref,
    grad_ref, context_ref, down_ref, up_ref, router_ref, sems,
):
    pairs = (
        (context_hbm, context_ref),
        (down_hbm, down_ref),
        (grad_hbm, grad_ref),
        (up_hbm, up_ref),
        (router_hbm, router_ref),
    )
    loads = [
        pltpu.make_async_copy(source, target, sems.at[i])
        for i, (source, target) in enumerate(pairs)
    ]
    for load in loads:
        load.start()
    groups, shards, rows, width = early_ref.shape
    capacity = picked_ref.shape[0]
    features = shards * width
    half = groups // 2
    loads[0].wait()
    loads[1].wait()
    low_in = contract(context_ref[...], down_ref[...], 1, 1).astype(BF16)
    for load in loads[2:]:
        load.wait()
    low_grad = (ADAPTER_SCALE * contract(grad_ref[...], up_ref[...], 1, 1)).astype(BF16)
    mixed_ref[...] = ADAPTER_SCALE * contract(up_ref[...], router_ref[...], 1, 1)
    slots = slots_ref[...].astype(BF16)
    for k in range(shards):
        grad = feature_block(grad_ref, place, k, width)
        context = feature_block(context_ref, place, k, width)
        up = ADAPTER_SCALE * contract(low_in, grad, 0, 0)
        down = contract(low_grad, context, 0, 0)
        for g in range(half):
            early_ref[g ^ place[1], k] = up[g * rows : (g + 1) * rows]
            early_ref[(g + half) ^ place[1], k] = down[g * rows : (g + 1) * rows]
        picked_ref[:, k * width : (k + 1) * width] = jnp.dot(
            slots, context, preferred_element_type=F32
        ).astype(BF16)
    low = jnp.dot(slots, low_in, preferred_element_type=F32).astype(BF16)
    picked_ref[:, features:] = jnp.zeros((capacity, 2 * LANES), BF16)
    picked_ref[:, features : features + low.shape[1]] = low
    info = contract(slots_ref[...], info_ref[...], 1, 1, EXACT)
    picked_ref[:, features + LANES : features + LANES + info.shape[1]] = info.astype(BF16)


def adapter_early(place, grad, context, down, up, router, slots, info, groups, shards):
    tokens, features = grad.shape
    rank = up.shape[0]
    rows = 2 * rank // groups
    arrays = (grad, context, down, up, router)
    return pl.pallas_call(
        adapter_kernel,
        out_shape=(
            jax.ShapeDtypeStruct((groups, shards, rows, features // shards), F32),
            jax.ShapeDtypeStruct((slots.shape[0], features + 2 * LANES), BF16),
            jax.ShapeDtypeStruct((rank, router.shape[0]), F32),
        ),
        in_specs=[SMEM] + [HBM] * 5 + [VMEM] * 2,
        out_specs=(VMEM,) * 3,
        scratch_shapes=[pltpu.VMEM(value.shape, BF16) for value in arrays]
        + [pltpu.SemaphoreType.DMA((5,))],
        compiler_params=params(),
        cost_estimate=cost(0, 0),
        name="adapter_early",
    )(place, *[in_hbm(value) for value in arrays], slots, info)


def finish_kernel(
    experts, place, partial_ref, outer_ref, hidden_ref, picked_ref, other_ref,
    product_ref, prob_ref, prob_other_ref, late_ref,
):
    shards, _, late_width = late_ref.shape
    width = late_width - LANES
    features = shards * width
    is_end = place[3].astype(F32)
    hidden = outer_ref.shape[1]
    tile = 512
    capacity = picked_ref.shape[0]
    pickeds = (picked_ref, other_ref)
    infos = [ref[:, features + LANES :].astype(F32) for ref in pickeds]
    totals = [jnp.zeros((capacity, LANES), F32) for _ in pickeds]
    for t in range(hidden // tile):
        part = slice(t * tile, (t + 1) * tile)
        for half in range(2):
            rows = slice(half * capacity, (half + 1) * capacity)
            whole_rows = pl.ds(pl.multiple_of((place[2] ^ half) * capacity, capacity), capacity)
            product = partial_ref[rows, part] + (1.0 - is_end) * outer_ref[rows, part].astype(F32)
            product_ref[rows, part] = product
            weighted = hidden_ref[whole_rows, part].astype(F32) * product
            for j in range(tile // LANES):
                totals[half] = totals[half] + weighted[:, j * LANES : (j + 1) * LANES]
    lane = lax.broadcasted_iota(jnp.int32, (capacity, LANES), 1)
    logits = []
    for info, total, out in zip(infos, totals, (prob_ref, prob_other_ref), strict=True):
        prob = jnp.sum(total, axis=1, keepdims=True)
        out[...] = jnp.broadcast_to(prob, out.shape)
        logits.append(jnp.where(lane < experts, info * prob, 0.0).astype(BF16))

    def late(columns):
        return sum(
            contract(logit, ref[:, columns], 0, 0)[:experts]
            for logit, ref in zip(logits, pickeds, strict=True)
        )

    low = late(slice(features, features + LANES))
    for k in range(shards):
        late_ref[k, :, :width] = late(slice(k * width, (k + 1) * width))
        late_ref[k, :, width:] = low


def hidden_kernel(experts, place, product_ref, picked_ref, other_ref, grad_hbm, grad_ref, sems):
    capacity = picked_ref.shape[0]
    column = picked_ref.shape[1] - LANES + experts
    tiles = sems.shape[0]
    tile = product_ref.shape[1] // tiles
    stores = []
    for t in range(tiles):
        part = pl.ds(t * tile, tile)
        for half, ref in enumerate((picked_ref, other_ref)):
            rows = slice(half * capacity, (half + 1) * capacity)
            whole_rows = pl.ds(pl.multiple_of((place[2] ^ half) * capacity, capacity), capacity)
            window_prob = ref[:, column - experts :].astype(F32)[:, experts : experts + 1]
            grad_ref[whole_rows, part] = (window_prob * product_ref[rows, part]).astype(BF16)
        store = pltpu.make_async_copy(grad_ref.at[:, part], grad_hbm.at[:, part], sems.at[t])
        store.start()
        stores.append(store)
    for store in stores:
        store.wait()


def hidden_gradient(place, product, picked, other, experts, tiles):
    return pl.pallas_call(
        functools.partial(hidden_kernel, experts),
        out_shape=jax.ShapeDtypeStruct(product.shape, BF16),
        in_specs=[SMEM] + [VMEM] * 3,
        out_specs=HBM,
        scratch_shapes=[pltpu.VMEM(product.shape, BF16), pltpu.SemaphoreType.DMA((tiles,))],
        compiler_params=params(),
        cost_estimate=cost(0, 0),
        name="hidden_gradient",
    )(place, product, picked, other)


def finish(place, partial, outer, hidden_state, picked, other, experts, shards):
    rows, hidden = outer.shape
    capacity = picked.shape[0]
    width = (picked.shape[1] - 2 * LANES) // shards
    return pl.pallas_call(
        functools.partial(finish_kernel, experts),
        out_shape=(
            pltpu.VMEM((rows, hidden), F32),
            jax.ShapeDtypeStruct((capacity, LANES), F32),
            jax.ShapeDtypeStruct((capacity, LANES), F32),
            jax.ShapeDtypeStruct((shards, experts, width + LANES), F32),
        ),
        in_specs=[SMEM] + [VMEM] * 5,
        out_specs=(VMEM,) * 4,
        compiler_params=params(),
        cost_estimate=cost(8 * rows * hidden, 10 * rows * hidden),
        name="finish",
    )(place, partial, outer, hidden_state, picked, other)


def token_kernel(prob_ref, prob_got_ref, slots_ref, info_ref, router_ref, token_hbm, token_ref, sems):
    experts = router_ref.shape[0]
    own = prob_ref[:, 0:1] + prob_got_ref[:, 0:1]
    window = jnp.sum(slots_ref[...] * own, axis=0, keepdims=True)
    logits = (info_ref[:experts] * window).astype(BF16)
    tiles = sems.shape[0]
    tile = token_ref.shape[1] // tiles
    stores = []
    for t in range(tiles):
        part = pl.ds(t * tile, tile)
        token_ref[:, part] = contract(logits, router_ref[:, part], 0, 0).astype(BF16)
        store = pltpu.make_async_copy(token_ref.at[:, part], token_hbm.at[:, part], sems.at[t])
        store.start()
        stores.append(store)
    for store in stores:
        store.wait()


def token_gradient(prob, prob_got, slots, info, router, tiles):
    tokens = slots.shape[1]
    features = router.shape[1]
    return pl.pallas_call(
        token_kernel,
        out_shape=jax.ShapeDtypeStruct((tokens, features), BF16),
        in_specs=[VMEM] * 5,
        out_specs=HBM,
        scratch_shapes=[pltpu.VMEM((tokens, features), BF16), pltpu.SemaphoreType.DMA((tiles,))],
        compiler_params=params(),
        cost_estimate=cost(2 * tokens * features * router.shape[0], 2 * tokens * features),
        name="token_gradient",
    )(prob, prob_got, slots, info, router)


def adapter_late_kernel(
    place, early_ref, late_ref, mixed_ref, router_ref, down_hbm, up_hbm, down_ref, up_ref, sems
):
    groups, rows, _ = early_ref.shape
    half = groups // 2
    rank, width = up_ref.shape
    parts = [slice(g * rows, (g + 1) * rows) for g in range(half)]
    down = jnp.dot(
        mixed_ref[...].astype(BF16),
        late_ref[:, :width].astype(BF16),
        preferred_element_type=F32,
    )
    for g, part in enumerate(parts):
        down_ref[part] = early_ref[(g + half) ^ place[1], :, :width].astype(F32) + down[part]
    store_down = pltpu.make_async_copy(down_ref, down_hbm, sems.at[0])
    store_down.start()
    router = feature_block(router_ref, place, 0, width)
    up = ADAPTER_SCALE * contract(late_ref[:, width : width + rank].astype(BF16), router, 0, 0)
    for g, part in enumerate(parts):
        up_ref[part] = early_ref[g ^ place[1], :, :width].astype(F32) + up[part]
    store_up = pltpu.make_async_copy(up_ref, up_hbm, sems.at[1])
    store_up.start()
    store_down.wait()
    store_up.wait()


def adapter_late(place, early, late, mixed, router):
    groups, rows, width = early.shape
    out = jax.ShapeDtypeStruct((groups * rows // 2, width - LANES), F32)
    return pl.pallas_call(
        adapter_late_kernel,
        out_shape=(out, out),
        in_specs=[SMEM] + [VMEM] * 4,
        out_specs=(HBM, HBM),
        scratch_shapes=[pltpu.VMEM(out.shape, F32)] * 2 + [pltpu.SemaphoreType.DMA((2,))],
        compiler_params=params(),
        cost_estimate=cost(64 * groups * rows * width, 8 * groups * rows * width),
        name="adapter_late",
    )(place, early, late, mixed, router)


def swap(value, axis, count, bits):
    return lax.ppermute(value, axis, xor_pairs(count, bits))


def swap_group(value, bits):
    pairs = [(d * 2 + e, (d ^ (bits & 3)) * 2 + (e ^ (bits >> 2))) for d in range(4) for e in range(2)]
    return lax.ppermute(value, ("dp", "expert"), pairs)


def after(value, *others):
    return lax.optimization_barrier((value,) + others)[0]


def direct_device(
    output_gradient,
    saved_router_scores,
    expert_choice_index,
    router_matrix,
    weight_normalized_entries,
    scales,
    stored_hidden_state,
    context,
    adapter_down_factor,
    adapter_up_factor,
):
    dp = lax.axis_index("dp")
    expert = lax.axis_index("expert")
    shard = lax.axis_index("shard")
    is_end = ((shard == 0) | (shard == 3)).astype(jnp.int32)
    group = expert * 4 + dp
    place = jnp.stack([shard, group, expert, is_end]).astype(jnp.int32)
    row_count, ff_share = stored_hidden_state.shape[2:]
    capacity = row_count // 2
    experts = saved_router_scores.shape[1]

    send_rows, slots, info = route(
        place, saved_router_scores, expert_choice_index, output_gradient, capacity, 4
    )
    rows = jnp.stack(
        [send_rows[0]] + [swap(send_rows[k], "shard", 4, k) for k in range(1, 4)]
    )
    weight = dequantize(weight_normalized_entries, scales, 4)
    rows, weight = lax.optimization_barrier((rows, weight))
    other_rows = swap(rows, "expert", 2, 1)

    partial = products(place, rows, weight)
    first, far, last, own = products(place, other_rows, weight, partial)
    near = swap(first, "shard", 4, 1)
    middle = lax.ppermute(last, "shard", [(1, 2), (2, 1)])
    early, picked, mixed = adapter_early(
        after(place, last), output_gradient, context, adapter_down_factor, adapter_up_factor,
        router_matrix, slots, info, 8, 4,
    )
    far, near, early, picked = lax.optimization_barrier((far, near, early, picked))
    forward = add_near(place, far, near)
    across = swap(forward, "shard", 4, 2)
    forward, last, middle = lax.optimization_barrier((forward, last, middle))
    outer = lax.ppermute(last, "shard", [(0, 1), (3, 2)])
    forward, early, picked = lax.optimization_barrier((forward, early, picked))
    other_picked = swap(picked, "expert", 2, 1)
    parts = early.astype(BF16)
    early = early[0] + sum(swap_group(parts[g], g).astype(F32) for g in range(1, 8))
    partial = add_far(place, own, near, middle, across)
    partial, outer, early, other_picked = lax.optimization_barrier(
        (partial, outer, early, other_picked)
    )

    product, prob, prob_other, late = finish(
        place, partial, outer, stored_hidden_state[0, 0], picked, other_picked, experts, 4
    )
    early = jnp.pad(early, ((0, 0), (0, 0), (0, LANES)))
    late = jnp.concatenate([late, early], 1)
    late = late[:2] + swap(late[2:].astype(BF16), "shard", 4, 2).astype(F32)
    hidden_grad = hidden_gradient(place, product, picked, other_picked, experts, 4)
    late, hidden_grad = lax.optimization_barrier((late, hidden_grad))
    prob_got = swap(prob_other, "expert", 2, 1)
    late = late[0] + swap(late[1].astype(BF16), "shard", 4, 1).astype(F32)
    late, early = late[:experts], late[experts:].astype(BF16)
    mine = jnp.concatenate([late.astype(BF16), early], 0)
    got = [swap(mine, "dp", 4, k) for k in range(1, 4)]
    token_grad = token_gradient(prob, prob_got, slots, info, router_matrix, 4)
    got, token_grad = lax.optimization_barrier((got, token_grad))
    late = late + sum(other[:experts].astype(F32) for other in got)
    early = jnp.concatenate([early] + [other[experts:] for other in got], 0)
    got = swap(jnp.concatenate([late.astype(BF16), early], 0), "expert", 2, 1)
    late = late + got[:experts].astype(F32)
    early = jnp.concatenate([early, got[experts:]], 0)
    early = early.reshape(8, -1, early.shape[1])
    grad_down, up_factor_gradient = adapter_late(place, early, late, mixed, router_matrix)
    return (
        hidden_grad.reshape(stored_hidden_state.shape),
        token_grad,
        grad_down,
        up_factor_gradient,
    )


def route_general(saved_router_scores, expert_choice_index, capacity):
    experts = saved_router_scores.shape[1]
    labels = jnp.arange(experts, dtype=jnp.int32)
    choose = expert_choice_index[:, :, None] == labels[None, None, :]
    chosen = jnp.sum(jnp.where(choose, saved_router_scores[:, None, :], 0.0), axis=2)
    first_prob = 1.0 / (1.0 + jnp.exp(chosen[:, 1] - chosen[:, 0]))
    second_prob = 1.0 - first_prob
    in_window = expert_choice_index == 0
    window_flag = jnp.any(in_window, axis=1)
    flag_int = window_flag.astype(jnp.int32)
    slot_index = jnp.cumsum(flag_int) - flag_int
    route_probs = jnp.stack([first_prob, second_prob], axis=1).astype(jnp.bfloat16)
    window_prob = jnp.where(in_window[:, 0], route_probs[:, 0], route_probs[:, 1])
    slot_labels = jnp.arange(capacity, dtype=jnp.int32)
    placement = window_flag[None, :] & (slot_index[None, :] == slot_labels[:, None])
    window_sign = in_window[:, 0].astype(jnp.float32) - in_window[:, 1].astype(jnp.float32)
    sign_table = choose[:, 0, :].astype(jnp.float32) - choose[:, 1, :].astype(jnp.float32)
    factors = (first_prob * second_prob * window_sign)[:, None] * sign_table
    return placement, window_prob, factors


def general_device(
    output_gradient,
    saved_router_scores,
    expert_choice_index,
    router_matrix,
    weight_normalized_entries,
    scales,
    stored_hidden_state,
    context,
    adapter_down_factor,
    adapter_up_factor,
):
    expert_count = lax.axis_size("expert")
    shard_count = lax.axis_size("shard")
    expert = lax.axis_index("expert")
    shard = lax.axis_index("shard")
    tokens, feature_width = output_gradient.shape
    row_count = stored_hidden_state.shape[2]
    capacity = row_count // expert_count
    ff_share = stored_hidden_state.shape[3]
    share_width = feature_width // shard_count
    block_size = weight_normalized_entries.shape[0] // scales.shape[0]
    rank = adapter_up_factor.shape[0]

    placement, window_prob, factors = route_general(saved_router_scores, expert_choice_index, capacity)
    placed = placement.astype(jnp.bfloat16)
    send_rows = jnp.dot(placed, output_gradient, preferred_element_type=jnp.float32).astype(
        jnp.bfloat16
    )
    send_probs = jnp.dot(placed, window_prob, preferred_element_type=jnp.float32).astype(
        jnp.bfloat16
    )
    blocks = lax.all_to_all(
        send_rows.reshape(capacity, shard_count, share_width).transpose(1, 0, 2), "shard", 0, 0
    )
    gathered = lax.all_gather(blocks, "expert", axis=1)
    all_probs = lax.all_gather(send_probs, "expert", axis=0, tiled=True)

    code_blocks = weight_normalized_entries.reshape(scales.shape[0], block_size, ff_share)
    own_weight = (code_blocks * scales[:, None, :]).reshape(
        weight_normalized_entries.shape[0], ff_share
    )
    product = jnp.dot(
        gathered.reshape(shard_count * row_count, share_width),
        own_weight,
        preferred_element_type=jnp.float32,
    ).reshape(shard_count, row_count, ff_share)

    narrow_input = lax.dot_general(
        context, adapter_down_factor, (((1,), (1,)), ((), ())), preferred_element_type=jnp.float32
    ).astype(jnp.bfloat16)
    narrow_gradient = (
        ADAPTER_SCALE
        * lax.dot_general(
            output_gradient,
            adapter_up_factor,
            (((1,), (1,)), ((), ())),
            preferred_element_type=jnp.float32,
        )
    ).astype(jnp.bfloat16)
    early_up = ADAPTER_SCALE * lax.dot_general(
        narrow_input, output_gradient, (((0,), (0,)), ((), ())), preferred_element_type=jnp.float32
    )
    early_down = lax.dot_general(
        narrow_gradient, context, (((0,), (0,)), ((), ())), preferred_element_type=jnp.float32
    )
    early = jnp.concatenate([early_up, early_down], 0)

    total = lax.psum_scatter(product.astype(jnp.bfloat16), "shard", scatter_dimension=0)
    total = total.astype(jnp.float32)
    early = lax.psum(early, ("dp", "expert"))
    early = lax.psum_scatter(early, "shard", scatter_dimension=1, tiled=True)

    hidden_grad = (all_probs.astype(jnp.float32)[:, None] * total).astype(jnp.bfloat16)
    partial_value = jnp.sum(stored_hidden_state[0, 0].astype(jnp.float32) * total, axis=1)
    slot_grad = lax.psum(partial_value, "expert")
    own_grad = lax.dynamic_slice_in_dim(slot_grad, expert * capacity, capacity, 0)
    window_grad = jnp.sum(jnp.where(placement, own_grad[:, None], 0.0), axis=0)
    logit_grad = (factors * window_grad[:, None]).astype(jnp.bfloat16)
    token_grad = jnp.dot(logit_grad, router_matrix, preferred_element_type=jnp.float32).astype(
        jnp.bfloat16
    )
    late_input = lax.dot_general(
        logit_grad, narrow_input, (((0,), (0,)), ((), ())), preferred_element_type=jnp.float32
    )
    late_context = lax.dot_general(
        logit_grad, context, (((0,), (0,)), ((), ())), preferred_element_type=jnp.float32
    )
    late_input = lax.psum(late_input, ("dp", "expert", "shard"))
    late_context = lax.psum(late_context, ("dp", "expert"))
    late_context = lax.psum_scatter(late_context, "shard", scatter_dimension=1, tiled=True)
    own_router = lax.dynamic_slice_in_dim(router_matrix, shard * share_width, share_width, 1)
    factor_router = ADAPTER_SCALE * lax.dot_general(
        adapter_up_factor, router_matrix, (((1,), (1,)), ((), ())), preferred_element_type=jnp.float32
    )
    up_factor_gradient = early[:rank] + ADAPTER_SCALE * lax.dot_general(
        late_input,
        own_router.astype(jnp.float32),
        (((0,), (0,)), ((), ())),
        precision=lax.Precision.HIGHEST,
        preferred_element_type=jnp.float32,
    )
    grad_down = early[rank:] + jnp.dot(
        factor_router,
        late_context,
        precision=lax.Precision.HIGHEST,
        preferred_element_type=jnp.float32,
    )
    return (
        hidden_grad.reshape(stored_hidden_state.shape),
        token_grad,
        grad_down,
        up_factor_gradient,
    )


def solution(mesh):
    axes = dict(mesh.shape)
    direct = (axes["dp"], axes["expert"], axes["shard"]) == (4, 2, 4)
    tokens_spec = P(("dp", "expert", "shard"), None)
    in_specs = (
        tokens_spec,
        tokens_spec,
        tokens_spec,
        P(),
        P("shard", "expert"),
        P("shard", "expert"),
        P("dp", "shard", None, "expert"),
        tokens_spec,
        P(),
        P(),
    )
    out_specs = (
        P("dp", "shard", None, "expert"),
        tokens_spec,
        P(None, "shard"),
        P(None, "shard"),
    )
    return jax.shard_map(
        direct_device if direct else general_device, mesh=mesh, in_specs=in_specs, out_specs=out_specs, check_vma=False
    )
```

```python
import functools

import jax
import jax.numpy as jnp
from jax import lax
from jax.experimental import pallas as pl
from jax.experimental.pallas import tpu as pltpu
from jax.sharding import PartitionSpec as P

ADAPTER_SCALE = 0.25
LANES = 128
F32 = jnp.float32
BF16 = jnp.bfloat16
BLOCKS = (0, 2, 1, 3)
SMEM = pl.BlockSpec(memory_space=pltpu.SMEM)
VMEM = pl.BlockSpec(memory_space=pltpu.VMEM)
HBM = pl.BlockSpec(memory_space=pltpu.HBM)
EXACT = lax.Precision.HIGHEST


def params(mebibytes=16):
    return pltpu.CompilerParams(vmem_limit_bytes=mebibytes * 1024 * 1024)


def cost(flops, bytes_accessed):
    return pl.CostEstimate(flops=flops, bytes_accessed=bytes_accessed, transcendentals=0)


def in_hbm(value):
    return pltpu.with_memory_space_constraint(value, pltpu.HBM)


def whole(shape):
    return pl.BlockSpec(shape, lambda *_: (0,) * len(shape))


def contract(a, b, dim_a, dim_b, precision=None):
    return lax.dot_general(
        a, b, (((dim_a,), (dim_b,)), ((), ())), precision=precision, preferred_element_type=F32
    )


def xor_pairs(count, bits):
    return [(i, i ^ bits) for i in range(count)]


def feature_block(ref, place, k, width):
    start = pl.multiple_of((place[0] ^ k) * width, LANES)
    return ref[:, pl.ds(start, width)]


def route_kernel(
    place, scores_hbm, choice_hbm, grad_hbm, rows_ref, slots_ref, info_ref,
    scores_ref, choice_ref, grad_ref, sems,
):
    load_scores = pltpu.make_async_copy(scores_hbm, scores_ref, sems.at[0])
    load_choice = pltpu.make_async_copy(choice_hbm, choice_ref, sems.at[1])
    load = pltpu.make_async_copy(grad_hbm, grad_ref, sems.at[2])
    load_scores.start()
    load_choice.start()
    load.start()
    load_scores.wait()
    load_choice.wait()
    scores = scores_ref[...]
    experts, tokens = scores.shape
    shards, capacity, width = rows_ref.shape
    first_choice = choice_ref[0:1, :]
    second_choice = choice_ref[1:2, :]
    labels = lax.broadcasted_iota(jnp.int32, (experts, tokens), 0)
    chosen_first = jnp.sum(jnp.where(labels == first_choice, scores, 0.0), axis=0, keepdims=True)
    chosen_second = jnp.sum(jnp.where(labels == second_choice, scores, 0.0), axis=0, keepdims=True)
    first_prob = 1.0 / (1.0 + jnp.exp(chosen_second - chosen_first))
    second_prob = 1.0 - first_prob
    in_first = (first_choice == 0).astype(F32)
    in_second = (second_choice == 0).astype(F32)
    flags = jnp.broadcast_to(in_first + in_second, (capacity, tokens))
    row = lax.broadcasted_iota(jnp.int32, (tokens, tokens), 0)
    column = lax.broadcasted_iota(jnp.int32, (tokens, tokens), 1)
    before = (row < column).astype(F32).astype(BF16)
    slot = jnp.dot(flags.astype(BF16), before, preferred_element_type=F32)
    number = lax.broadcasted_iota(jnp.int32, (capacity, tokens), 0).astype(F32)
    slots = jnp.where((flags > 0.5) & (slot == number), 1.0, 0.0)
    slots_ref[...] = slots
    sign = (labels == first_choice).astype(F32) - (labels == second_choice).astype(F32)
    info_ref[:experts] = first_prob * second_prob * (in_first - in_second) * sign
    window_prob = jnp.where(in_first > 0.5, first_prob, second_prob)
    info_ref[experts:] = jnp.broadcast_to(window_prob, (info_ref.shape[0] - experts, tokens))
    picks = slots.astype(BF16)
    load.wait()
    for k in range(shards):
        block = feature_block(grad_ref, place, k, width)
        rows_ref[k] = jnp.dot(picks, block, preferred_element_type=F32).astype(BF16)


def route(place, scores, choice, grad, capacity, shards):
    tokens, features = grad.shape
    return pl.pallas_call(
        route_kernel,
        out_shape=(
            jax.ShapeDtypeStruct((shards, capacity, features // shards), BF16),
            jax.ShapeDtypeStruct((capacity, tokens), F32),
            jax.ShapeDtypeStruct((2 * scores.shape[1], tokens), F32),
        ),
        in_specs=[SMEM, HBM, HBM, HBM],
        out_specs=(VMEM,) * 3,
        scratch_shapes=[
            pltpu.VMEM(scores.T.shape, F32),
            pltpu.VMEM(choice.T.shape, jnp.int32),
            pltpu.VMEM(grad.shape, BF16),
            pltpu.SemaphoreType.DMA((3,)),
        ],
        compiler_params=params(),
        cost_estimate=cost(2 * tokens * capacity * features, 2 * tokens * features),
        name="route",
    )(place, in_hbm(scores.T), in_hbm(choice.T), in_hbm(grad))


def product_kernel(half, place, rows_ref, weight_ref, *refs):
    outs, lhs = refs[-5:-1], refs[-1]
    shards, capacity, _ = rows_ref.shape
    is_end = place[3]
    order = (1 + 2 * is_end, 2, 3 - 2 * is_end, 0)
    for slot, k in enumerate(order):
        lhs[slot * capacity : (slot + 1) * capacity] = rows_ref[k]
    rows = slice(half * capacity, (half + 1) * capacity)
    tile = 512
    for t in range(weight_ref.shape[1] // tile):
        part = slice(t * tile, (t + 1) * tile)
        result = jnp.dot(lhs[...], weight_ref[:, part], preferred_element_type=F32)
        for slot, ref in enumerate(outs):
            ref[rows, part] = result[slot * capacity : (slot + 1) * capacity].astype(ref.dtype)


def products(place, rows, weight, before=()):
    shards, capacity, width = rows.shape
    hidden = weight.shape[1]
    sent = pltpu.VMEM((2 * capacity, hidden), BF16)
    return pl.pallas_call(
        functools.partial(product_kernel, len(before) // 4),
        out_shape=(sent, sent, sent, pltpu.VMEM((2 * capacity, hidden), F32)),
        in_specs=[SMEM, VMEM, VMEM] + [VMEM] * len(before),
        out_specs=(VMEM,) * 4,
        input_output_aliases={3 + i: i for i in range(len(before))},
        scratch_shapes=[pltpu.VMEM((shards * capacity, width), BF16)],
        compiler_params=params(),
        cost_estimate=cost(2 * shards * capacity * width * hidden, 2 * width * hidden),
        name="products",
    )(place, rows, pltpu.with_memory_space_constraint(weight, pltpu.VMEM), *before)


def forward_kernel(place, far_ref, near_ref, out_ref):
    keep = 1.0 - place[3].astype(F32)
    out_ref[...] = (far_ref[...].astype(F32) + keep * near_ref[...].astype(F32)).astype(BF16)


def add_near(place, far, near):
    return pl.pallas_call(
        forward_kernel,
        out_shape=pltpu.VMEM(far.shape, BF16),
        in_specs=[SMEM, VMEM, VMEM],
        out_specs=VMEM,
        compiler_params=params(),
        cost_estimate=cost(2 * far.size, 6 * far.size),
        name="add_near",
    )(place, far, near)


def partial_kernel(place, own_ref, near_ref, middle_ref, far_ref, out_ref):
    is_end = place[3].astype(F32)
    out_ref[...] = (
        own_ref[...]
        + is_end * near_ref[...].astype(F32)
        + (1.0 - is_end) * middle_ref[...].astype(F32)
        + far_ref[...].astype(F32)
    )


def add_far(place, own, near, middle, far):
    return pl.pallas_call(
        partial_kernel,
        out_shape=pltpu.VMEM(own.shape, F32),
        in_specs=[SMEM] + [VMEM] * 4,
        out_specs=VMEM,
        compiler_params=params(),
        cost_estimate=cost(round(3.0 * 1e9), 14 * own.size),
        name="add_far",
    )(place, own, near, middle, far)


def weight_kernel(codes_hbm, scales_hbm, weight_ref, codes_ref, scales_ref, scale_sem, sems):
    load_scales = pltpu.make_async_copy(scales_hbm, scales_ref, scale_sem)
    load_scales.start()
    tiles = sems.shape[0]
    tile = codes_ref.shape[1] // tiles
    loads = []
    for t in range(tiles):
        part = pl.ds(t * tile, tile)
        loads.append(
            pltpu.make_async_copy(codes_hbm.at[:, part], codes_ref.at[:, part], sems.at[t])
        )
        loads[t].start()
    blocks = scales_ref.shape[0]
    size = codes_ref.shape[0] // blocks
    load_scales.wait()
    for t in range(tiles):
        loads[t].wait()
        part = slice(t * tile, (t + 1) * tile)
        for b in range(blocks):
            rows = slice(b * size, (b + 1) * size)
            weight_ref[rows, part] = codes_ref[rows, part] * scales_ref[b : b + 1, part]


def dequantize(codes, scales, tiles):
    return pl.pallas_call(
        weight_kernel,
        out_shape=pltpu.VMEM(codes.shape, BF16),
        in_specs=[HBM, HBM],
        out_specs=VMEM,
        scratch_shapes=[
            pltpu.VMEM(codes.shape, BF16),
            pltpu.VMEM(scales.shape, BF16),
            pltpu.SemaphoreType.DMA,
            pltpu.SemaphoreType.DMA((tiles,)),
        ],
        compiler_params=params(),
        cost_estimate=cost(codes.size, 4 * codes.size),
        name="dequantize",
    )(in_hbm(codes), in_hbm(scales))


def adapter_kernel(
    place, grad_hbm, context_hbm, down_hbm, up_hbm, router_hbm, slots_ref, info_ref,
    early_ref, picked_ref, mixed_ref,
    grad_ref, context_ref, down_ref, up_ref, router_ref, sems,
):
    pairs = (
        (context_hbm, context_ref),
        (down_hbm, down_ref),
        (grad_hbm, grad_ref),
        (up_hbm, up_ref),
        (router_hbm, router_ref),
    )
    loads = [
        pltpu.make_async_copy(source, target, sems.at[i])
        for i, (source, target) in enumerate(pairs)
    ]
    for load in loads:
        load.start()
    groups, shards, rows, width = early_ref.shape
    capacity = picked_ref.shape[0]
    features = shards * width
    half = groups // 2
    loads[0].wait()
    loads[1].wait()
    low_in = contract(context_ref[...], down_ref[...], 1, 1).astype(BF16)
    for load in loads[2:]:
        load.wait()
    low_grad = (ADAPTER_SCALE * contract(grad_ref[...], up_ref[...], 1, 1)).astype(BF16)
    mixed_ref[...] = ADAPTER_SCALE * contract(up_ref[...], router_ref[...], 1, 1)
    slots = slots_ref[...].astype(BF16)
    for position, k in enumerate(BLOCKS):
        grad = feature_block(grad_ref, place, k, width)
        context = feature_block(context_ref, place, k, width)
        up = ADAPTER_SCALE * contract(low_in, grad, 0, 0)
        down = contract(low_grad, context, 0, 0)
        for g in range(half):
            early_ref[g ^ place[1], position] = up[g * rows : (g + 1) * rows]
            early_ref[(g + half) ^ place[1], position] = down[g * rows : (g + 1) * rows]
        picked_ref[:, k * width : (k + 1) * width] = jnp.dot(
            slots, context, preferred_element_type=F32
        ).astype(BF16)
    low = jnp.dot(slots, low_in, preferred_element_type=F32).astype(BF16)
    picked_ref[:, features:] = jnp.zeros((capacity, 2 * LANES), BF16)
    picked_ref[:, features : features + low.shape[1]] = low
    info = contract(slots_ref[...], info_ref[...], 1, 1, EXACT)
    picked_ref[:, features + LANES : features + LANES + info.shape[1]] = info.astype(BF16)


def adapter_early(place, grad, context, down, up, router, slots, info, groups, shards):
    tokens, features = grad.shape
    rank = up.shape[0]
    rows = 2 * rank // groups
    arrays = (grad, context, down, up, router)
    return pl.pallas_call(
        adapter_kernel,
        out_shape=(
            jax.ShapeDtypeStruct((groups, shards, rows, features // shards), F32),
            jax.ShapeDtypeStruct((slots.shape[0], features + 2 * LANES), BF16),
            jax.ShapeDtypeStruct((rank, router.shape[0]), F32),
        ),
        in_specs=[SMEM] + [HBM] * 5 + [VMEM] * 2,
        out_specs=(VMEM,) * 3,
        scratch_shapes=[pltpu.VMEM(value.shape, BF16) for value in arrays]
        + [pltpu.SemaphoreType.DMA((5,))],
        compiler_params=params(),
        cost_estimate=cost(0, 0),
        name="adapter_early",
    )(place, *[in_hbm(value) for value in arrays], slots, info)


def finish_kernel(
    experts, place, partial_ref, outer_ref, hidden_ref, picked_ref, other_ref,
    product_ref, prob_ref, prob_other_ref, late_ref,
):
    shards, _, late_width = late_ref.shape
    width = late_width - LANES
    features = shards * width
    is_end = place[3].astype(F32)
    hidden = outer_ref.shape[1]
    tile = 512
    capacity = picked_ref.shape[0]
    pickeds = (picked_ref, other_ref)
    infos = [ref[:, features + LANES :].astype(F32) for ref in pickeds]
    totals = [jnp.zeros((capacity, LANES), F32) for _ in pickeds]
    for t in range(hidden // tile):
        part = slice(t * tile, (t + 1) * tile)
        for half in range(2):
            rows = slice(half * capacity, (half + 1) * capacity)
            whole_rows = pl.ds(pl.multiple_of((place[2] ^ half) * capacity, capacity), capacity)
            product = partial_ref[rows, part] + (1.0 - is_end) * outer_ref[rows, part].astype(F32)
            product_ref[rows, part] = product
            weighted = hidden_ref[whole_rows, part].astype(F32) * product
            for j in range(tile // LANES):
                totals[half] = totals[half] + weighted[:, j * LANES : (j + 1) * LANES]
    lane = lax.broadcasted_iota(jnp.int32, (capacity, LANES), 1)
    logits = []
    for info, total, out in zip(infos, totals, (prob_ref, prob_other_ref), strict=True):
        prob = jnp.sum(total, axis=1, keepdims=True)
        out[...] = jnp.broadcast_to(prob, out.shape)
        logits.append(jnp.where(lane < experts, info * prob, 0.0).astype(BF16))

    def late(columns):
        return sum(
            contract(logit, ref[:, columns], 0, 0)[:experts]
            for logit, ref in zip(logits, pickeds, strict=True)
        )

    low = late(slice(features, features + LANES))
    for position, k in enumerate(BLOCKS):
        late_ref[position, :, :width] = late(slice(k * width, (k + 1) * width))
        late_ref[position, :, width:] = low


def hidden_kernel(experts, place, product_ref, picked_ref, other_ref, grad_hbm, grad_ref, sems):
    capacity = picked_ref.shape[0]
    column = picked_ref.shape[1] - LANES + experts
    tiles = sems.shape[0]
    tile = product_ref.shape[1] // tiles
    stores = []
    for t in range(tiles):
        part = pl.ds(t * tile, tile)
        for half, ref in enumerate((picked_ref, other_ref)):
            rows = slice(half * capacity, (half + 1) * capacity)
            whole_rows = pl.ds(pl.multiple_of((place[2] ^ half) * capacity, capacity), capacity)
            window_prob = ref[:, column - experts :].astype(F32)[:, experts : experts + 1]
            grad_ref[whole_rows, part] = (window_prob * product_ref[rows, part]).astype(BF16)
        store = pltpu.make_async_copy(grad_ref.at[:, part], grad_hbm.at[:, part], sems.at[t])
        store.start()
        stores.append(store)
    for store in stores:
        store.wait()


def hidden_gradient(place, product, picked, other, experts, tiles):
    return pl.pallas_call(
        functools.partial(hidden_kernel, experts),
        out_shape=jax.ShapeDtypeStruct(product.shape, BF16),
        in_specs=[SMEM] + [VMEM] * 3,
        out_specs=HBM,
        scratch_shapes=[pltpu.VMEM(product.shape, BF16), pltpu.SemaphoreType.DMA((tiles,))],
        compiler_params=params(),
        cost_estimate=cost(0, 0),
        name="hidden_gradient",
    )(place, product, picked, other)


def finish(place, partial, outer, hidden_state, picked, other, experts, shards):
    rows, hidden = outer.shape
    capacity = picked.shape[0]
    width = (picked.shape[1] - 2 * LANES) // shards
    return pl.pallas_call(
        functools.partial(finish_kernel, experts),
        out_shape=(
            pltpu.VMEM((rows, hidden), F32),
            jax.ShapeDtypeStruct((capacity, LANES), F32),
            jax.ShapeDtypeStruct((capacity, LANES), F32),
            jax.ShapeDtypeStruct((shards, experts, width + LANES), F32),
        ),
        in_specs=[SMEM] + [VMEM] * 5,
        out_specs=(VMEM,) * 4,
        compiler_params=params(),
        cost_estimate=cost(8 * rows * hidden, 10 * rows * hidden),
        name="finish",
    )(place, partial, outer, hidden_state, picked, other)


def token_kernel(prob_ref, prob_got_ref, slots_ref, info_ref, router_ref, token_hbm, token_ref, sems):
    experts = router_ref.shape[0]
    own = prob_ref[:, 0:1] + prob_got_ref[:, 0:1]
    window = jnp.sum(slots_ref[...] * own, axis=0, keepdims=True)
    logits = (info_ref[:experts] * window).astype(BF16)
    tiles = sems.shape[0]
    tile = token_ref.shape[1] // tiles
    stores = []
    for t in range(tiles):
        part = pl.ds(t * tile, tile)
        token_ref[:, part] = contract(logits, router_ref[:, part], 0, 0).astype(BF16)
        store = pltpu.make_async_copy(token_ref.at[:, part], token_hbm.at[:, part], sems.at[t])
        store.start()
        stores.append(store)
    for store in stores:
        store.wait()


def token_gradient(prob, prob_got, slots, info, router, tiles):
    tokens = slots.shape[1]
    features = router.shape[1]
    return pl.pallas_call(
        token_kernel,
        out_shape=jax.ShapeDtypeStruct((tokens, features), BF16),
        in_specs=[VMEM] * 5,
        out_specs=HBM,
        scratch_shapes=[pltpu.VMEM((tokens, features), BF16), pltpu.SemaphoreType.DMA((tiles,))],
        compiler_params=params(),
        cost_estimate=cost(2 * tokens * features * router.shape[0], 2 * tokens * features),
        name="token_gradient",
    )(prob, prob_got, slots, info, router)


def adapter_late_kernel(
    place, early_ref, late_ref, mixed_ref, router_ref, down_hbm, up_hbm, down_ref, up_ref, sems
):
    groups, rows, _ = early_ref.shape
    half = groups // 2
    rank, width = up_ref.shape
    parts = [slice(g * rows, (g + 1) * rows) for g in range(half)]
    down = jnp.dot(
        mixed_ref[...].astype(BF16),
        late_ref[:, :width].astype(BF16),
        preferred_element_type=F32,
    )
    for g, part in enumerate(parts):
        down_ref[part] = early_ref[(g + half) ^ place[1], :, :width].astype(F32) + down[part]
    store_down = pltpu.make_async_copy(down_ref, down_hbm, sems.at[0])
    store_down.start()
    router = feature_block(router_ref, place, 0, width)
    up = ADAPTER_SCALE * contract(late_ref[:, width : width + rank].astype(BF16), router, 0, 0)
    for g, part in enumerate(parts):
        up_ref[part] = early_ref[g ^ place[1], :, :width].astype(F32) + up[part]
    store_up = pltpu.make_async_copy(up_ref, up_hbm, sems.at[1])
    store_up.start()
    store_down.wait()
    store_up.wait()


def adapter_late(place, early, late, mixed, router):
    groups, rows, width = early.shape
    out = jax.ShapeDtypeStruct((groups * rows // 2, width - LANES), F32)
    return pl.pallas_call(
        adapter_late_kernel,
        out_shape=(out, out),
        in_specs=[SMEM] + [VMEM] * 4,
        out_specs=(HBM, HBM),
        scratch_shapes=[pltpu.VMEM(out.shape, F32)] * 2 + [pltpu.SemaphoreType.DMA((2,))],
        compiler_params=params(),
        cost_estimate=cost(64 * groups * rows * width, 8 * groups * rows * width),
        name="adapter_late",
    )(place, early, late, mixed, router)


def swap(value, axis, count, bits):
    return lax.ppermute(value, axis, xor_pairs(count, bits))


def swap_group(value, bits):
    pairs = [(d * 2 + e, (d ^ (bits & 3)) * 2 + (e ^ (bits >> 2))) for d in range(4) for e in range(2)]
    return lax.ppermute(value, ("dp", "expert"), pairs)


def after(value, *others):
    return lax.optimization_barrier((value,) + others)[0]


def direct_device(
    output_gradient,
    saved_router_scores,
    expert_choice_index,
    router_matrix,
    weight_normalized_entries,
    scales,
    stored_hidden_state,
    context,
    adapter_down_factor,
    adapter_up_factor,
):
    dp = lax.axis_index("dp")
    expert = lax.axis_index("expert")
    shard = lax.axis_index("shard")
    is_end = ((shard == 0) | (shard == 3)).astype(jnp.int32)
    group = expert * 4 + dp
    place = jnp.stack([shard, group, expert, is_end]).astype(jnp.int32)
    row_count, ff_share = stored_hidden_state.shape[2:]
    capacity = row_count // 2
    experts = saved_router_scores.shape[1]

    send_rows, slots, info = route(
        place, saved_router_scores, expert_choice_index, output_gradient, capacity, 4
    )
    rows = jnp.stack(
        [send_rows[0]] + [swap(send_rows[k], "shard", 4, k) for k in range(1, 4)]
    )
    weight = dequantize(weight_normalized_entries, scales, 4)
    rows, weight = lax.optimization_barrier((rows, weight))
    other_rows = swap(rows, "expert", 2, 1)

    partial = products(place, rows, weight)
    first, far, last, own = products(place, other_rows, weight, partial)
    near = swap(first, "shard", 4, 1)
    middle = lax.ppermute(last, "shard", [(1, 2), (2, 1)])
    early, picked, mixed = adapter_early(
        after(place, last), output_gradient, context, adapter_down_factor, adapter_up_factor,
        router_matrix, slots, info, 8, 4,
    )
    far, near, early, picked = lax.optimization_barrier((far, near, early, picked))
    forward = add_near(place, far, near)
    across = swap(forward, "shard", 4, 2)
    forward, last, middle = lax.optimization_barrier((forward, last, middle))
    outer = lax.ppermute(last, "shard", [(0, 1), (3, 2)])
    forward, early, picked = lax.optimization_barrier((forward, early, picked))
    other_picked = swap(picked, "expert", 2, 1)
    parts = early.astype(BF16)
    early = early[0] + sum(swap_group(parts[g], g).astype(F32) for g in range(1, 8))
    partial = add_far(place, own, near, middle, across)
    partial, outer, early, other_picked = lax.optimization_barrier(
        (partial, outer, early, other_picked)
    )

    product, prob, prob_other, late = finish(
        place, partial, outer, stored_hidden_state[0, 0], picked, other_picked, experts, 4
    )
    early = jnp.pad(early, ((0, 0), (0, 0), (0, LANES)))
    late = jnp.concatenate([late, early], 1)
    late = late[:2] + swap(late[2:].astype(BF16), "shard", 4, 1).astype(F32)
    hidden_grad = hidden_gradient(place, product, picked, other_picked, experts, 4)
    late, hidden_grad = lax.optimization_barrier((late, hidden_grad))
    prob_got = swap(prob_other, "expert", 2, 1)
    late = late[0] + swap(late[1].astype(BF16), "shard", 4, 2).astype(F32)
    late, early = late[:experts], late[experts:].astype(BF16)
    mine = jnp.concatenate([late.astype(BF16), early], 0)
    got = [swap(mine, "dp", 4, k) for k in range(1, 4)]
    token_grad = token_gradient(prob, prob_got, slots, info, router_matrix, 4)
    got, token_grad = lax.optimization_barrier((got, token_grad))
    late = late + sum(other[:experts].astype(F32) for other in got)
    early = jnp.concatenate([early] + [other[experts:] for other in got], 0)
    got = swap(jnp.concatenate([late.astype(BF16), early], 0), "expert", 2, 1)
    late = late + got[:experts].astype(F32)
    early = jnp.concatenate([early, got[experts:]], 0)
    early = early.reshape(8, -1, early.shape[1])
    grad_down, up_factor_gradient = adapter_late(place, early, late, mixed, router_matrix)
    return (
        hidden_grad.reshape(stored_hidden_state.shape),
        token_grad,
        grad_down,
        up_factor_gradient,
    )


def route_general(saved_router_scores, expert_choice_index, capacity):
    experts = saved_router_scores.shape[1]
    labels = jnp.arange(experts, dtype=jnp.int32)
    choose = expert_choice_index[:, :, None] == labels[None, None, :]
    chosen = jnp.sum(jnp.where(choose, saved_router_scores[:, None, :], 0.0), axis=2)
    first_prob = 1.0 / (1.0 + jnp.exp(chosen[:, 1] - chosen[:, 0]))
    second_prob = 1.0 - first_prob
    in_window = expert_choice_index == 0
    window_flag = jnp.any(in_window, axis=1)
    flag_int = window_flag.astype(jnp.int32)
    slot_index = jnp.cumsum(flag_int) - flag_int
    route_probs = jnp.stack([first_prob, second_prob], axis=1).astype(jnp.bfloat16)
    window_prob = jnp.where(in_window[:, 0], route_probs[:, 0], route_probs[:, 1])
    slot_labels = jnp.arange(capacity, dtype=jnp.int32)
    placement = window_flag[None, :] & (slot_index[None, :] == slot_labels[:, None])
    window_sign = in_window[:, 0].astype(jnp.float32) - in_window[:, 1].astype(jnp.float32)
    sign_table = choose[:, 0, :].astype(jnp.float32) - choose[:, 1, :].astype(jnp.float32)
    factors = (first_prob * second_prob * window_sign)[:, None] * sign_table
    return placement, window_prob, factors


def general_device(
    output_gradient,
    saved_router_scores,
    expert_choice_index,
    router_matrix,
    weight_normalized_entries,
    scales,
    stored_hidden_state,
    context,
    adapter_down_factor,
    adapter_up_factor,
):
    expert_count = lax.axis_size("expert")
    shard_count = lax.axis_size("shard")
    expert = lax.axis_index("expert")
    shard = lax.axis_index("shard")
    tokens, feature_width = output_gradient.shape
    row_count = stored_hidden_state.shape[2]
    capacity = row_count // expert_count
    ff_share = stored_hidden_state.shape[3]
    share_width = feature_width // shard_count
    block_size = weight_normalized_entries.shape[0] // scales.shape[0]
    rank = adapter_up_factor.shape[0]

    placement, window_prob, factors = route_general(saved_router_scores, expert_choice_index, capacity)
    placed = placement.astype(jnp.bfloat16)
    send_rows = jnp.dot(placed, output_gradient, preferred_element_type=jnp.float32).astype(
        jnp.bfloat16
    )
    send_probs = jnp.dot(placed, window_prob, preferred_element_type=jnp.float32).astype(
        jnp.bfloat16
    )
    blocks = lax.all_to_all(
        send_rows.reshape(capacity, shard_count, share_width).transpose(1, 0, 2), "shard", 0, 0
    )
    gathered = lax.all_gather(blocks, "expert", axis=1)
    all_probs = lax.all_gather(send_probs, "expert", axis=0, tiled=True)

    code_blocks = weight_normalized_entries.reshape(scales.shape[0], block_size, ff_share)
    own_weight = (code_blocks * scales[:, None, :]).reshape(
        weight_normalized_entries.shape[0], ff_share
    )
    product = jnp.dot(
        gathered.reshape(shard_count * row_count, share_width),
        own_weight,
        preferred_element_type=jnp.float32,
    ).reshape(shard_count, row_count, ff_share)

    narrow_input = lax.dot_general(
        context, adapter_down_factor, (((1,), (1,)), ((), ())), preferred_element_type=jnp.float32
    ).astype(jnp.bfloat16)
    narrow_gradient = (
        ADAPTER_SCALE
        * lax.dot_general(
            output_gradient,
            adapter_up_factor,
            (((1,), (1,)), ((), ())),
            preferred_element_type=jnp.float32,
        )
    ).astype(jnp.bfloat16)
    early_up = ADAPTER_SCALE * lax.dot_general(
        narrow_input, output_gradient, (((0,), (0,)), ((), ())), preferred_element_type=jnp.float32
    )
    early_down = lax.dot_general(
        narrow_gradient, context, (((0,), (0,)), ((), ())), preferred_element_type=jnp.float32
    )
    early = jnp.concatenate([early_up, early_down], 0)

    total = lax.psum_scatter(product.astype(jnp.bfloat16), "shard", scatter_dimension=0)
    total = total.astype(jnp.float32)
    early = lax.psum(early, ("dp", "expert"))
    early = lax.psum_scatter(early, "shard", scatter_dimension=1, tiled=True)

    hidden_grad = (all_probs.astype(jnp.float32)[:, None] * total).astype(jnp.bfloat16)
    partial_value = jnp.sum(stored_hidden_state[0, 0].astype(jnp.float32) * total, axis=1)
    slot_grad = lax.psum(partial_value, "expert")
    own_grad = lax.dynamic_slice_in_dim(slot_grad, expert * capacity, capacity, 0)
    window_grad = jnp.sum(jnp.where(placement, own_grad[:, None], 0.0), axis=0)
    logit_grad = (factors * window_grad[:, None]).astype(jnp.bfloat16)
    token_grad = jnp.dot(logit_grad, router_matrix, preferred_element_type=jnp.float32).astype(
        jnp.bfloat16
    )
    late_input = lax.dot_general(
        logit_grad, narrow_input, (((0,), (0,)), ((), ())), preferred_element_type=jnp.float32
    )
    late_context = lax.dot_general(
        logit_grad, context, (((0,), (0,)), ((), ())), preferred_element_type=jnp.float32
    )
    late_input = lax.psum(late_input, ("dp", "expert", "shard"))
    late_context = lax.psum(late_context, ("dp", "expert"))
    late_context = lax.psum_scatter(late_context, "shard", scatter_dimension=1, tiled=True)
    own_router = lax.dynamic_slice_in_dim(router_matrix, shard * share_width, share_width, 1)
    factor_router = ADAPTER_SCALE * lax.dot_general(
        adapter_up_factor, router_matrix, (((1,), (1,)), ((), ())), preferred_element_type=jnp.float32
    )
    up_factor_gradient = early[:rank] + ADAPTER_SCALE * lax.dot_general(
        late_input,
        own_router.astype(jnp.float32),
        (((0,), (0,)), ((), ())),
        precision=lax.Precision.HIGHEST,
        preferred_element_type=jnp.float32,
    )
    grad_down = early[rank:] + jnp.dot(
        factor_router,
        late_context,
        precision=lax.Precision.HIGHEST,
        preferred_element_type=jnp.float32,
    )
    return (
        hidden_grad.reshape(stored_hidden_state.shape),
        token_grad,
        grad_down,
        up_factor_gradient,
    )


def solution(mesh):
    axes = dict(mesh.shape)
    direct = (axes["dp"], axes["expert"], axes["shard"]) == (4, 2, 4)
    tokens_spec = P(("dp", "expert", "shard"), None)
    in_specs = (
        tokens_spec,
        tokens_spec,
        tokens_spec,
        P(),
        P("shard", "expert"),
        P("shard", "expert"),
        P("dp", "shard", None, "expert"),
        tokens_spec,
        P(),
        P(),
    )
    out_specs = (
        P("dp", "shard", None, "expert"),
        tokens_spec,
        P(None, "shard"),
        P(None, "shard"),
    )
    return jax.shard_map(
        direct_device if direct else general_device, mesh=mesh, in_specs=in_specs, out_specs=out_specs, check_vma=False
    )
```

```python
import functools

import jax
import jax.numpy as jnp
from jax import lax
from jax.experimental import pallas as pl
from jax.experimental.pallas import tpu as pltpu
from jax.sharding import PartitionSpec as P

ADAPTER_SCALE = 0.25
LANES = 128
F32 = jnp.float32
BF16 = jnp.bfloat16
BLOCKS = (0, 2, 1, 3)
SMEM = pl.BlockSpec(memory_space=pltpu.SMEM)
VMEM = pl.BlockSpec(memory_space=pltpu.VMEM)
HBM = pl.BlockSpec(memory_space=pltpu.HBM)
EXACT = lax.Precision.HIGHEST


def params(mebibytes=16):
    return pltpu.CompilerParams(vmem_limit_bytes=mebibytes * 1024 * 1024)


def cost(flops, bytes_accessed):
    return pl.CostEstimate(flops=flops, bytes_accessed=bytes_accessed, transcendentals=0)


def in_hbm(value):
    return pltpu.with_memory_space_constraint(value, pltpu.HBM)


def whole(shape):
    return pl.BlockSpec(shape, lambda *_: (0,) * len(shape))


def contract(a, b, dim_a, dim_b, precision=None):
    return lax.dot_general(
        a, b, (((dim_a,), (dim_b,)), ((), ())), precision=precision, preferred_element_type=F32
    )


def xor_pairs(count, bits):
    return [(i, i ^ bits) for i in range(count)]


def feature_block(ref, place, k, width):
    start = pl.multiple_of((place[0] ^ k) * width, LANES)
    return ref[:, pl.ds(start, width)]


def route_kernel(
    place, scores_hbm, choice_hbm, grad_hbm, rows_ref, slots_ref, info_ref,
    scores_ref, choice_ref, grad_ref, sems,
):
    load_scores = pltpu.make_async_copy(scores_hbm, scores_ref, sems.at[0])
    load_choice = pltpu.make_async_copy(choice_hbm, choice_ref, sems.at[1])
    load = pltpu.make_async_copy(grad_hbm, grad_ref, sems.at[2])
    load_scores.start()
    load_choice.start()
    load.start()
    load_scores.wait()
    load_choice.wait()
    scores = scores_ref[...]
    experts, tokens = scores.shape
    shards, capacity, width = rows_ref.shape
    first_choice = choice_ref[0:1, :]
    second_choice = choice_ref[1:2, :]
    labels = lax.broadcasted_iota(jnp.int32, (experts, tokens), 0)
    chosen_first = jnp.sum(jnp.where(labels == first_choice, scores, 0.0), axis=0, keepdims=True)
    chosen_second = jnp.sum(jnp.where(labels == second_choice, scores, 0.0), axis=0, keepdims=True)
    first_prob = 1.0 / (1.0 + jnp.exp(chosen_second - chosen_first))
    second_prob = 1.0 - first_prob
    in_first = (first_choice == 0).astype(F32)
    in_second = (second_choice == 0).astype(F32)
    flags = jnp.broadcast_to(in_first + in_second, (capacity, tokens))
    row = lax.broadcasted_iota(jnp.int32, (tokens, tokens), 0)
    column = lax.broadcasted_iota(jnp.int32, (tokens, tokens), 1)
    before = (row < column).astype(F32).astype(BF16)
    slot = jnp.dot(flags.astype(BF16), before, preferred_element_type=F32)
    number = lax.broadcasted_iota(jnp.int32, (capacity, tokens), 0).astype(F32)
    slots = jnp.where((flags > 0.5) & (slot == number), 1.0, 0.0)
    slots_ref[...] = slots
    sign = (labels == first_choice).astype(F32) - (labels == second_choice).astype(F32)
    info_ref[:experts] = first_prob * second_prob * (in_first - in_second) * sign
    window_prob = jnp.where(in_first > 0.5, first_prob, second_prob)
    info_ref[experts:] = jnp.broadcast_to(window_prob, (info_ref.shape[0] - experts, tokens))
    picks = slots.astype(BF16)
    load.wait()
    for k in range(shards):
        block = feature_block(grad_ref, place, k, width)
        rows_ref[k] = jnp.dot(picks, block, preferred_element_type=F32).astype(BF16)


def route(place, scores, choice, grad, capacity, shards):
    tokens, features = grad.shape
    return pl.pallas_call(
        route_kernel,
        out_shape=(
            jax.ShapeDtypeStruct((shards, capacity, features // shards), BF16),
            jax.ShapeDtypeStruct((capacity, tokens), F32),
            jax.ShapeDtypeStruct((2 * scores.shape[1], tokens), F32),
        ),
        in_specs=[SMEM, HBM, HBM, HBM],
        out_specs=(VMEM,) * 3,
        scratch_shapes=[
            pltpu.VMEM(scores.T.shape, F32),
            pltpu.VMEM(choice.T.shape, jnp.int32),
            pltpu.VMEM(grad.shape, BF16),
            pltpu.SemaphoreType.DMA((3,)),
        ],
        compiler_params=params(),
        cost_estimate=cost(2 * tokens * capacity * features, 2 * tokens * features),
        name="route",
    )(place, in_hbm(scores.T), in_hbm(choice.T), in_hbm(grad))


def product_kernel(half, place, rows_ref, weight_ref, *refs):
    outs, lhs = refs[-5:-1], refs[-1]
    shards, capacity, _ = rows_ref.shape
    is_end = place[3]
    order = (1 + 2 * is_end, 2, 3 - 2 * is_end, 0)
    for slot, k in enumerate(order):
        lhs[slot * capacity : (slot + 1) * capacity] = rows_ref[k]
    rows = slice(half * capacity, (half + 1) * capacity)
    tile = 256
    for t in range(weight_ref.shape[1] // tile):
        part = slice(t * tile, (t + 1) * tile)
        result = jnp.dot(lhs[...], weight_ref[:, part], preferred_element_type=F32)
        for slot, ref in enumerate(outs):
            ref[rows, part] = result[slot * capacity : (slot + 1) * capacity].astype(ref.dtype)


def products(place, rows, weight, before=()):
    shards, capacity, width = rows.shape
    hidden = weight.shape[1]
    sent = pltpu.VMEM((2 * capacity, hidden), BF16)
    return pl.pallas_call(
        functools.partial(product_kernel, len(before) // 4),
        out_shape=(sent, sent, sent, pltpu.VMEM((2 * capacity, hidden), F32)),
        in_specs=[SMEM, VMEM, VMEM] + [VMEM] * len(before),
        out_specs=(VMEM,) * 4,
        input_output_aliases={3 + i: i for i in range(len(before))},
        scratch_shapes=[pltpu.VMEM((shards * capacity, width), BF16)],
        compiler_params=params(),
        cost_estimate=cost(2 * shards * capacity * width * hidden, 2 * width * hidden),
        name="products",
    )(place, rows, pltpu.with_memory_space_constraint(weight, pltpu.VMEM), *before)


def forward_kernel(place, far_ref, near_ref, out_ref):
    keep = 1.0 - place[3].astype(F32)
    out_ref[...] = (far_ref[...].astype(F32) + keep * near_ref[...].astype(F32)).astype(BF16)


def add_near(place, far, near):
    return pl.pallas_call(
        forward_kernel,
        out_shape=pltpu.VMEM(far.shape, BF16),
        in_specs=[SMEM, VMEM, VMEM],
        out_specs=VMEM,
        compiler_params=params(),
        cost_estimate=cost(2 * far.size, 6 * far.size),
        name="add_near",
    )(place, far, near)


def partial_kernel(place, own_ref, near_ref, middle_ref, far_ref, out_ref):
    is_end = place[3].astype(F32)
    out_ref[...] = (
        own_ref[...]
        + is_end * near_ref[...].astype(F32)
        + (1.0 - is_end) * middle_ref[...].astype(F32)
        + far_ref[...].astype(F32)
    )


def add_far(place, own, near, middle, far):
    return pl.pallas_call(
        partial_kernel,
        out_shape=pltpu.VMEM(own.shape, F32),
        in_specs=[SMEM] + [VMEM] * 4,
        out_specs=VMEM,
        compiler_params=params(),
        cost_estimate=cost(round(3.0 * 1e9), 14 * own.size),
        name="add_far",
    )(place, own, near, middle, far)


def weight_kernel(codes_hbm, scales_hbm, weight_ref, codes_ref, scales_ref, scale_sem, sems):
    load_scales = pltpu.make_async_copy(scales_hbm, scales_ref, scale_sem)
    load_scales.start()
    tiles = sems.shape[0]
    tile = codes_ref.shape[1] // tiles
    loads = []
    for t in range(tiles):
        part = pl.ds(t * tile, tile)
        loads.append(
            pltpu.make_async_copy(codes_hbm.at[:, part], codes_ref.at[:, part], sems.at[t])
        )
        loads[t].start()
    blocks = scales_ref.shape[0]
    size = codes_ref.shape[0] // blocks
    load_scales.wait()
    for t in range(tiles):
        loads[t].wait()
        part = slice(t * tile, (t + 1) * tile)
        for b in range(blocks):
            rows = slice(b * size, (b + 1) * size)
            weight_ref[rows, part] = codes_ref[rows, part] * scales_ref[b : b + 1, part]


def dequantize(codes, scales, tiles):
    return pl.pallas_call(
        weight_kernel,
        out_shape=pltpu.VMEM(codes.shape, BF16),
        in_specs=[HBM, HBM],
        out_specs=VMEM,
        scratch_shapes=[
            pltpu.VMEM(codes.shape, BF16),
            pltpu.VMEM(scales.shape, BF16),
            pltpu.SemaphoreType.DMA,
            pltpu.SemaphoreType.DMA((tiles,)),
        ],
        compiler_params=params(),
        cost_estimate=cost(codes.size, 4 * codes.size),
        name="dequantize",
    )(in_hbm(codes), in_hbm(scales))


def adapter_kernel(
    place, grad_hbm, context_hbm, down_hbm, up_hbm, router_hbm, slots_ref, info_ref,
    early_ref, picked_ref, mixed_ref,
    grad_ref, context_ref, down_ref, up_ref, router_ref, sems,
):
    pairs = (
        (context_hbm, context_ref),
        (down_hbm, down_ref),
        (grad_hbm, grad_ref),
        (up_hbm, up_ref),
        (router_hbm, router_ref),
    )
    loads = [
        pltpu.make_async_copy(source, target, sems.at[i])
        for i, (source, target) in enumerate(pairs)
    ]
    for load in loads:
        load.start()
    groups, shards, rows, width = early_ref.shape
    capacity = picked_ref.shape[0]
    features = shards * width
    half = groups // 2
    loads[0].wait()
    loads[1].wait()
    low_in = contract(context_ref[...], down_ref[...], 1, 1).astype(BF16)
    for load in loads[2:]:
        load.wait()
    low_grad = (ADAPTER_SCALE * contract(grad_ref[...], up_ref[...], 1, 1)).astype(BF16)
    mixed_ref[...] = ADAPTER_SCALE * contract(up_ref[...], router_ref[...], 1, 1)
    slots = slots_ref[...].astype(BF16)
    for position, k in enumerate(BLOCKS):
        grad = feature_block(grad_ref, place, k, width)
        context = feature_block(context_ref, place, k, width)
        up = ADAPTER_SCALE * contract(low_in, grad, 0, 0)
        down = contract(low_grad, context, 0, 0)
        for g in range(half):
            early_ref[g ^ place[1], position] = up[g * rows : (g + 1) * rows]
            early_ref[(g + half) ^ place[1], position] = down[g * rows : (g + 1) * rows]
        picked_ref[:, k * width : (k + 1) * width] = jnp.dot(
            slots, context, preferred_element_type=F32
        ).astype(BF16)
    low = jnp.dot(slots, low_in, preferred_element_type=F32).astype(BF16)
    picked_ref[:, features:] = jnp.zeros((capacity, 2 * LANES), BF16)
    picked_ref[:, features : features + low.shape[1]] = low
    info = contract(slots_ref[...], info_ref[...], 1, 1, EXACT)
    picked_ref[:, features + LANES : features + LANES + info.shape[1]] = info.astype(BF16)


def adapter_early(place, grad, context, down, up, router, slots, info, groups, shards):
    tokens, features = grad.shape
    rank = up.shape[0]
    rows = 2 * rank // groups
    arrays = (grad, context, down, up, router)
    return pl.pallas_call(
        adapter_kernel,
        out_shape=(
            jax.ShapeDtypeStruct((groups, shards, rows, features // shards), F32),
            jax.ShapeDtypeStruct((slots.shape[0], features + 2 * LANES), BF16),
            jax.ShapeDtypeStruct((rank, router.shape[0]), F32),
        ),
        in_specs=[SMEM] + [HBM] * 5 + [VMEM] * 2,
        out_specs=(VMEM,) * 3,
        scratch_shapes=[pltpu.VMEM(value.shape, BF16) for value in arrays]
        + [pltpu.SemaphoreType.DMA((5,))],
        compiler_params=params(),
        cost_estimate=cost(0, 0),
        name="adapter_early",
    )(place, *[in_hbm(value) for value in arrays], slots, info)


def finish_kernel(
    experts, place, partial_ref, outer_ref, hidden_ref, picked_ref, other_ref,
    product_ref, prob_ref, prob_other_ref, late_ref,
):
    shards, _, late_width = late_ref.shape
    width = late_width - LANES
    features = shards * width
    is_end = place[3].astype(F32)
    hidden = outer_ref.shape[1]
    tile = 512
    capacity = picked_ref.shape[0]
    pickeds = (picked_ref, other_ref)
    infos = [ref[:, features + LANES :].astype(F32) for ref in pickeds]
    totals = [jnp.zeros((capacity, LANES), F32) for _ in pickeds]
    for t in range(hidden // tile):
        part = slice(t * tile, (t + 1) * tile)
        for half in range(2):
            rows = slice(half * capacity, (half + 1) * capacity)
            whole_rows = pl.ds(pl.multiple_of((place[2] ^ half) * capacity, capacity), capacity)
            product = partial_ref[rows, part] + (1.0 - is_end) * outer_ref[rows, part].astype(F32)
            product_ref[rows, part] = product
            weighted = hidden_ref[whole_rows, part].astype(F32) * product
            for j in range(tile // LANES):
                totals[half] = totals[half] + weighted[:, j * LANES : (j + 1) * LANES]
    lane = lax.broadcasted_iota(jnp.int32, (capacity, LANES), 1)
    logits = []
    for info, total, out in zip(infos, totals, (prob_ref, prob_other_ref), strict=True):
        prob = jnp.sum(total, axis=1, keepdims=True)
        out[...] = jnp.broadcast_to(prob, out.shape)
        logits.append(jnp.where(lane < experts, info * prob, 0.0).astype(BF16))

    def late(columns):
        return sum(
            contract(logit, ref[:, columns], 0, 0)[:experts]
            for logit, ref in zip(logits, pickeds, strict=True)
        )

    low = late(slice(features, features + LANES))
    for position, k in enumerate(BLOCKS):
        late_ref[position, :, :width] = late(slice(k * width, (k + 1) * width))
        late_ref[position, :, width:] = low


def hidden_kernel(experts, place, product_ref, picked_ref, other_ref, grad_hbm, grad_ref, sems):
    capacity = picked_ref.shape[0]
    column = picked_ref.shape[1] - LANES + experts
    tiles = sems.shape[0]
    tile = product_ref.shape[1] // tiles
    stores = []
    for t in range(tiles):
        part = pl.ds(t * tile, tile)
        for half, ref in enumerate((picked_ref, other_ref)):
            rows = slice(half * capacity, (half + 1) * capacity)
            whole_rows = pl.ds(pl.multiple_of((place[2] ^ half) * capacity, capacity), capacity)
            window_prob = ref[:, column - experts :].astype(F32)[:, experts : experts + 1]
            grad_ref[whole_rows, part] = (window_prob * product_ref[rows, part]).astype(BF16)
        store = pltpu.make_async_copy(grad_ref.at[:, part], grad_hbm.at[:, part], sems.at[t])
        store.start()
        stores.append(store)
    for store in stores:
        store.wait()


def hidden_gradient(place, product, picked, other, experts, tiles):
    return pl.pallas_call(
        functools.partial(hidden_kernel, experts),
        out_shape=jax.ShapeDtypeStruct(product.shape, BF16),
        in_specs=[SMEM] + [VMEM] * 3,
        out_specs=HBM,
        scratch_shapes=[pltpu.VMEM(product.shape, BF16), pltpu.SemaphoreType.DMA((tiles,))],
        compiler_params=params(),
        cost_estimate=cost(0, 0),
        name="hidden_gradient",
    )(place, product, picked, other)


def finish(place, partial, outer, hidden_state, picked, other, experts, shards):
    rows, hidden = outer.shape
    capacity = picked.shape[0]
    width = (picked.shape[1] - 2 * LANES) // shards
    return pl.pallas_call(
        functools.partial(finish_kernel, experts),
        out_shape=(
            pltpu.VMEM((rows, hidden), F32),
            jax.ShapeDtypeStruct((capacity, LANES), F32),
            jax.ShapeDtypeStruct((capacity, LANES), F32),
            jax.ShapeDtypeStruct((shards, experts, width + LANES), F32),
        ),
        in_specs=[SMEM] + [VMEM] * 5,
        out_specs=(VMEM,) * 4,
        compiler_params=params(),
        cost_estimate=cost(8 * rows * hidden, 10 * rows * hidden),
        name="finish",
    )(place, partial, outer, hidden_state, picked, other)


def token_kernel(prob_ref, prob_got_ref, slots_ref, info_ref, router_ref, token_hbm, token_ref, sems):
    experts = router_ref.shape[0]
    own = prob_ref[:, 0:1] + prob_got_ref[:, 0:1]
    window = jnp.sum(slots_ref[...] * own, axis=0, keepdims=True)
    logits = (info_ref[:experts] * window).astype(BF16)
    tiles = sems.shape[0]
    tile = token_ref.shape[1] // tiles
    stores = []
    for t in range(tiles):
        part = pl.ds(t * tile, tile)
        token_ref[:, part] = contract(logits, router_ref[:, part], 0, 0).astype(BF16)
        store = pltpu.make_async_copy(token_ref.at[:, part], token_hbm.at[:, part], sems.at[t])
        store.start()
        stores.append(store)
    for store in stores:
        store.wait()


def token_gradient(prob, prob_got, slots, info, router, tiles):
    tokens = slots.shape[1]
    features = router.shape[1]
    return pl.pallas_call(
        token_kernel,
        out_shape=jax.ShapeDtypeStruct((tokens, features), BF16),
        in_specs=[VMEM] * 5,
        out_specs=HBM,
        scratch_shapes=[pltpu.VMEM((tokens, features), BF16), pltpu.SemaphoreType.DMA((tiles,))],
        compiler_params=params(),
        cost_estimate=cost(2 * tokens * features * router.shape[0], 2 * tokens * features),
        name="token_gradient",
    )(prob, prob_got, slots, info, router)


def adapter_late_kernel(
    place, early_ref, late_ref, mixed_ref, router_ref, down_hbm, up_hbm, down_ref, up_ref, sems
):
    groups, rows, _ = early_ref.shape
    half = groups // 2
    rank, width = up_ref.shape
    parts = [slice(g * rows, (g + 1) * rows) for g in range(half)]
    down = jnp.dot(
        mixed_ref[...].astype(BF16),
        late_ref[:, :width].astype(BF16),
        preferred_element_type=F32,
    )
    for g, part in enumerate(parts):
        down_ref[part] = early_ref[(g + half) ^ place[1], :, :width].astype(F32) + down[part]
    store_down = pltpu.make_async_copy(down_ref, down_hbm, sems.at[0])
    store_down.start()
    router = feature_block(router_ref, place, 0, width)
    up = ADAPTER_SCALE * contract(late_ref[:, width : width + rank].astype(BF16), router, 0, 0)
    for g, part in enumerate(parts):
        up_ref[part] = early_ref[g ^ place[1], :, :width].astype(F32) + up[part]
    store_up = pltpu.make_async_copy(up_ref, up_hbm, sems.at[1])
    store_up.start()
    store_down.wait()
    store_up.wait()


def adapter_late(place, early, late, mixed, router):
    groups, rows, width = early.shape
    out = jax.ShapeDtypeStruct((groups * rows // 2, width - LANES), F32)
    return pl.pallas_call(
        adapter_late_kernel,
        out_shape=(out, out),
        in_specs=[SMEM] + [VMEM] * 4,
        out_specs=(HBM, HBM),
        scratch_shapes=[pltpu.VMEM(out.shape, F32)] * 2 + [pltpu.SemaphoreType.DMA((2,))],
        compiler_params=params(),
        cost_estimate=cost(64 * groups * rows * width, 8 * groups * rows * width),
        name="adapter_late",
    )(place, early, late, mixed, router)


def swap(value, axis, count, bits):
    return lax.ppermute(value, axis, xor_pairs(count, bits))


def swap_group(value, bits):
    pairs = [(d * 2 + e, (d ^ (bits & 3)) * 2 + (e ^ (bits >> 2))) for d in range(4) for e in range(2)]
    return lax.ppermute(value, ("dp", "expert"), pairs)


def after(value, *others):
    return lax.optimization_barrier((value,) + others)[0]


def direct_device(
    output_gradient,
    saved_router_scores,
    expert_choice_index,
    router_matrix,
    weight_normalized_entries,
    scales,
    stored_hidden_state,
    context,
    adapter_down_factor,
    adapter_up_factor,
):
    dp = lax.axis_index("dp")
    expert = lax.axis_index("expert")
    shard = lax.axis_index("shard")
    is_end = ((shard == 0) | (shard == 3)).astype(jnp.int32)
    group = expert * 4 + dp
    place = jnp.stack([shard, group, expert, is_end]).astype(jnp.int32)
    row_count, ff_share = stored_hidden_state.shape[2:]
    capacity = row_count // 2
    experts = saved_router_scores.shape[1]

    send_rows, slots, info = route(
        place, saved_router_scores, expert_choice_index, output_gradient, capacity, 4
    )
    rows = jnp.stack(
        [send_rows[0]] + [swap(send_rows[k], "shard", 4, k) for k in range(1, 4)]
    )
    weight = dequantize(weight_normalized_entries, scales, 4)
    rows, weight = lax.optimization_barrier((rows, weight))
    other_rows = swap(rows, "expert", 2, 1)

    partial = products(place, rows, weight)
    first, far, last, own = products(place, other_rows, weight, partial)
    near = swap(first, "shard", 4, 1)
    middle = lax.ppermute(last, "shard", [(1, 2), (2, 1)])
    early, picked, mixed = adapter_early(
        after(place, last), output_gradient, context, adapter_down_factor, adapter_up_factor,
        router_matrix, slots, info, 8, 4,
    )
    far, near, early, picked = lax.optimization_barrier((far, near, early, picked))
    forward = add_near(place, far, near)
    across = swap(forward, "shard", 4, 2)
    forward, last, middle = lax.optimization_barrier((forward, last, middle))
    outer = lax.ppermute(last, "shard", [(0, 1), (3, 2)])
    forward, early, picked = lax.optimization_barrier((forward, early, picked))
    other_picked = swap(picked, "expert", 2, 1)
    parts = early.astype(BF16)
    early = early[0] + sum(swap_group(parts[g], g).astype(F32) for g in range(1, 8))
    partial = add_far(place, own, near, middle, across)
    partial, outer, early, other_picked = lax.optimization_barrier(
        (partial, outer, early, other_picked)
    )

    product, prob, prob_other, late = finish(
        place, partial, outer, stored_hidden_state[0, 0], picked, other_picked, experts, 4
    )
    early = jnp.pad(early, ((0, 0), (0, 0), (0, LANES)))
    late = jnp.concatenate([late, early], 1)
    late = late[:2] + swap(late[2:].astype(BF16), "shard", 4, 1).astype(F32)
    hidden_grad = hidden_gradient(place, product, picked, other_picked, experts, 4)
    late, hidden_grad = lax.optimization_barrier((late, hidden_grad))
    prob_got = swap(prob_other, "expert", 2, 1)
    late = late[0] + swap(late[1].astype(BF16), "shard", 4, 2).astype(F32)
    late, early = late[:experts], late[experts:].astype(BF16)
    mine = jnp.concatenate([late.astype(BF16), early], 0)
    got = [swap(mine, "dp", 4, k) for k in range(1, 4)]
    token_grad = token_gradient(prob, prob_got, slots, info, router_matrix, 4)
    got, token_grad = lax.optimization_barrier((got, token_grad))
    late = late + sum(other[:experts].astype(F32) for other in got)
    early = jnp.concatenate([early] + [other[experts:] for other in got], 0)
    got = swap(jnp.concatenate([late.astype(BF16), early], 0), "expert", 2, 1)
    late = late + got[:experts].astype(F32)
    early = jnp.concatenate([early, got[experts:]], 0)
    early = early.reshape(8, -1, early.shape[1])
    grad_down, up_factor_gradient = adapter_late(place, early, late, mixed, router_matrix)
    return (
        hidden_grad.reshape(stored_hidden_state.shape),
        token_grad,
        grad_down,
        up_factor_gradient,
    )


def route_general(saved_router_scores, expert_choice_index, capacity):
    experts = saved_router_scores.shape[1]
    labels = jnp.arange(experts, dtype=jnp.int32)
    choose = expert_choice_index[:, :, None] == labels[None, None, :]
    chosen = jnp.sum(jnp.where(choose, saved_router_scores[:, None, :], 0.0), axis=2)
    first_prob = 1.0 / (1.0 + jnp.exp(chosen[:, 1] - chosen[:, 0]))
    second_prob = 1.0 - first_prob
    in_window = expert_choice_index == 0
    window_flag = jnp.any(in_window, axis=1)
    flag_int = window_flag.astype(jnp.int32)
    slot_index = jnp.cumsum(flag_int) - flag_int
    route_probs = jnp.stack([first_prob, second_prob], axis=1).astype(jnp.bfloat16)
    window_prob = jnp.where(in_window[:, 0], route_probs[:, 0], route_probs[:, 1])
    slot_labels = jnp.arange(capacity, dtype=jnp.int32)
    placement = window_flag[None, :] & (slot_index[None, :] == slot_labels[:, None])
    window_sign = in_window[:, 0].astype(jnp.float32) - in_window[:, 1].astype(jnp.float32)
    sign_table = choose[:, 0, :].astype(jnp.float32) - choose[:, 1, :].astype(jnp.float32)
    factors = (first_prob * second_prob * window_sign)[:, None] * sign_table
    return placement, window_prob, factors


def general_device(
    output_gradient,
    saved_router_scores,
    expert_choice_index,
    router_matrix,
    weight_normalized_entries,
    scales,
    stored_hidden_state,
    context,
    adapter_down_factor,
    adapter_up_factor,
):
    expert_count = lax.axis_size("expert")
    shard_count = lax.axis_size("shard")
    expert = lax.axis_index("expert")
    shard = lax.axis_index("shard")
    tokens, feature_width = output_gradient.shape
    row_count = stored_hidden_state.shape[2]
    capacity = row_count // expert_count
    ff_share = stored_hidden_state.shape[3]
    share_width = feature_width // shard_count
    block_size = weight_normalized_entries.shape[0] // scales.shape[0]
    rank = adapter_up_factor.shape[0]

    placement, window_prob, factors = route_general(saved_router_scores, expert_choice_index, capacity)
    placed = placement.astype(jnp.bfloat16)
    send_rows = jnp.dot(placed, output_gradient, preferred_element_type=jnp.float32).astype(
        jnp.bfloat16
    )
    send_probs = jnp.dot(placed, window_prob, preferred_element_type=jnp.float32).astype(
        jnp.bfloat16
    )
    blocks = lax.all_to_all(
        send_rows.reshape(capacity, shard_count, share_width).transpose(1, 0, 2), "shard", 0, 0
    )
    gathered = lax.all_gather(blocks, "expert", axis=1)
    all_probs = lax.all_gather(send_probs, "expert", axis=0, tiled=True)

    code_blocks = weight_normalized_entries.reshape(scales.shape[0], block_size, ff_share)
    own_weight = (code_blocks * scales[:, None, :]).reshape(
        weight_normalized_entries.shape[0], ff_share
    )
    product = jnp.dot(
        gathered.reshape(shard_count * row_count, share_width),
        own_weight,
        preferred_element_type=jnp.float32,
    ).reshape(shard_count, row_count, ff_share)

    narrow_input = lax.dot_general(
        context, adapter_down_factor, (((1,), (1,)), ((), ())), preferred_element_type=jnp.float32
    ).astype(jnp.bfloat16)
    narrow_gradient = (
        ADAPTER_SCALE
        * lax.dot_general(
            output_gradient,
            adapter_up_factor,
            (((1,), (1,)), ((), ())),
            preferred_element_type=jnp.float32,
        )
    ).astype(jnp.bfloat16)
    early_up = ADAPTER_SCALE * lax.dot_general(
        narrow_input, output_gradient, (((0,), (0,)), ((), ())), preferred_element_type=jnp.float32
    )
    early_down = lax.dot_general(
        narrow_gradient, context, (((0,), (0,)), ((), ())), preferred_element_type=jnp.float32
    )
    early = jnp.concatenate([early_up, early_down], 0)

    total = lax.psum_scatter(product.astype(jnp.bfloat16), "shard", scatter_dimension=0)
    total = total.astype(jnp.float32)
    early = lax.psum(early, ("dp", "expert"))
    early = lax.psum_scatter(early, "shard", scatter_dimension=1, tiled=True)

    hidden_grad = (all_probs.astype(jnp.float32)[:, None] * total).astype(jnp.bfloat16)
    partial_value = jnp.sum(stored_hidden_state[0, 0].astype(jnp.float32) * total, axis=1)
    slot_grad = lax.psum(partial_value, "expert")
    own_grad = lax.dynamic_slice_in_dim(slot_grad, expert * capacity, capacity, 0)
    window_grad = jnp.sum(jnp.where(placement, own_grad[:, None], 0.0), axis=0)
    logit_grad = (factors * window_grad[:, None]).astype(jnp.bfloat16)
    token_grad = jnp.dot(logit_grad, router_matrix, preferred_element_type=jnp.float32).astype(
        jnp.bfloat16
    )
    late_input = lax.dot_general(
        logit_grad, narrow_input, (((0,), (0,)), ((), ())), preferred_element_type=jnp.float32
    )
    late_context = lax.dot_general(
        logit_grad, context, (((0,), (0,)), ((), ())), preferred_element_type=jnp.float32
    )
    late_input = lax.psum(late_input, ("dp", "expert", "shard"))
    late_context = lax.psum(late_context, ("dp", "expert"))
    late_context = lax.psum_scatter(late_context, "shard", scatter_dimension=1, tiled=True)
    own_router = lax.dynamic_slice_in_dim(router_matrix, shard * share_width, share_width, 1)
    factor_router = ADAPTER_SCALE * lax.dot_general(
        adapter_up_factor, router_matrix, (((1,), (1,)), ((), ())), preferred_element_type=jnp.float32
    )
    up_factor_gradient = early[:rank] + ADAPTER_SCALE * lax.dot_general(
        late_input,
        own_router.astype(jnp.float32),
        (((0,), (0,)), ((), ())),
        precision=lax.Precision.HIGHEST,
        preferred_element_type=jnp.float32,
    )
    grad_down = early[rank:] + jnp.dot(
        factor_router,
        late_context,
        precision=lax.Precision.HIGHEST,
        preferred_element_type=jnp.float32,
    )
    return (
        hidden_grad.reshape(stored_hidden_state.shape),
        token_grad,
        grad_down,
        up_factor_gradient,
    )


def solution(mesh):
    axes = dict(mesh.shape)
    direct = (axes["dp"], axes["expert"], axes["shard"]) == (4, 2, 4)
    tokens_spec = P(("dp", "expert", "shard"), None)
    in_specs = (
        tokens_spec,
        tokens_spec,
        tokens_spec,
        P(),
        P("shard", "expert"),
        P("shard", "expert"),
        P("dp", "shard", None, "expert"),
        tokens_spec,
        P(),
        P(),
    )
    out_specs = (
        P("dp", "shard", None, "expert"),
        tokens_spec,
        P(None, "shard"),
        P(None, "shard"),
    )
    return jax.shard_map(
        direct_device if direct else general_device, mesh=mesh, in_specs=in_specs, out_specs=out_specs, check_vma=False
    )
```
